32 devices in a mesh: tile: 16 (over z, x, core), tm: 2 (over y).
Axes of the slice: x: 2, y: 2, z: 4, core: 2. Of those that a mesh axis runs over, the one named last changes fastest.
Arguments:
- features: bfloat16 [192, 8, 16, 16, 128], P('tile', 'tm'), may hold values from -6 to 6
- weight_one: bfloat16 [3, 3, 128, 128], replicated, may hold values from -0.1875 to 0.1875
- bias_one: float32 [128], replicated, may hold values from -3 to 3
- weight_two: bfloat16 [3, 3, 128, 128], replicated, may hold values from -0.1875 to 0.1875
- bias_two: float32 [128], replicated, may hold values from -3 to 3
- cotangent: bfloat16 [192, 8, 16, 16, 128], P('tile', 'tm'), may hold values from -6 to 6
Outputs:
- output: bfloat16 [192, 8, 16, 16, 128], P('tile', 'tm')
- grad_weight_one: float32 [3, 3, 128, 128], replicated
- grad_bias_one: float32 [128], replicated
- grad_weight_two: float32 [3, 3, 128, 128], replicated
- grad_bias_two: float32 [128], replicated
The draws below stay inside these ranges and needn't reach their ends.
All inputs are finite; a program needn't handle non-finite values.
Results may differ from the reference program's by a relative error of at most 0.0085.
Values may be sent and summed in bfloat16 or wider, within the bound.
A program may use at most 256 MiB of HBM per device.

```python
import math
import jax
import jax.numpy as jnp
import numpy as np
from jax import lax

C = 128
S = 4
P_SIZE = 16
TILES = 192
NB = 8
PIXELS = 393216


def block_levels(own_key, shape, split, low, largest):
    factor_of = 1.0
    for dim, shards_of in split:
        draws = jax.random.uniform(jax.random.fold_in(jax.random.fold_in(own_key, 6), dim), (shards_of,), jnp.float32, low / len(split), largest / len(split))
        factor_of = factor_of * jnp.repeat(jnp.exp(draws), shape[dim] // shards_of).reshape((-1,) + (1,) * (len(shape) - 1 - dim))
    return factor_of


def noise(rng, dims, deviation, limit, shards=(), kind=jnp.bfloat16):
    drawn = deviation * jax.random.normal(rng, dims, jnp.float32)
    if shards:
        drawn = drawn * block_levels(rng, dims, shards, -0.22, 0.18)
    return jnp.clip(drawn, -limit, limit).astype(kind)


def setup_inputs(seed: int = 0) -> dict:
    arg_keys = jax.random.split(jax.random.key(seed), 7)
    features = noise(arg_keys[0], (TILES, NB, P_SIZE, P_SIZE, C), 1.0, 6.0, ((0, 16), (1, 2)))
    weight_one = noise(arg_keys[1], (3, 3, C, C), (9 * C) ** -0.5, 0.1875)
    bias_one = noise(arg_keys[2], (C,), 0.5, 3.0, (), jnp.float32)
    weight_two = noise(arg_keys[3], (3, 3, C, C), (9 * C) ** -0.5, 0.1875)
    bias_two = noise(arg_keys[4], (C,), 0.5, 3.0, (), jnp.float32)
    cotangent = noise(arg_keys[5], (TILES, NB, P_SIZE, P_SIZE, C), 1.0, 6.0, ((0, 16), (1, 2)))
    return {"features": features, "weight_one": weight_one, "bias_one": bias_one, "weight_two": weight_two, "bias_two": bias_two, "cotangent": cotangent}


inv_sqrt_two = 0.7071067811865476
inv_sqrt_tau = 0.3989422804014327

def edge_partner(face_id, edge_id):
    group_id = face_id // 4
    within = face_id % 4
    after_id = (within + 1) % 4
    before = (within + 3) % 4
    if group_id == 0:
        options = [(after_id, 2), (4 + within, 0), (before, 0), (4 + after_id, 2)]
    elif group_id == 1:
        options = [(within, 1), (8 + before, 0), (before, 3), (8 + within, 2)]
    else:
        options = [(4 + after_id, 1), (8 + before, 3), (4 + within, 3), (8 + after_id, 1)]
    return options[edge_id]

def entry_pixel(edge_id, along_edge, length):
    if edge_id == 0:
        return (0, along_edge)
    if edge_id == 1:
        return (length - 1, along_edge)
    if edge_id == 2:
        return (along_edge, 0)
    return (along_edge, length - 1)

def step_pixel(face_id, row_at, col_at, row_step, col_step, length):
    row_new = row_at + row_step
    col_new = col_at + col_step
    if 0 <= row_new < length and 0 <= col_new < length:
        return (face_id, row_new, col_new, -1)
    if row_new < 0:
        edge_id = 0
    elif row_new >= length:
        edge_id = 1
    elif col_new < 0:
        edge_id = 2
    else:
        edge_id = 3
    along_edge = col_at if edge_id < 2 else row_at
    partner, entered = edge_partner(face_id, edge_id)
    row_in, col_in = entry_pixel(entered, along_edge, length)
    return (partner, row_in, col_in, entered)

def neighbour_pixel(face_id, row_at, col_at, row_step, col_step, length):
    if row_step == 0 or col_step == 0:
        found = step_pixel(face_id, row_at, col_at, row_step, col_step, length)
        return (found[0], found[1], found[2])
    face_one, row_one, col_one, entered = step_pixel(face_id, row_at, col_at, row_step, 0, length)
    if entered >= 2:
        found = step_pixel(face_one, row_one, col_one, col_step, 0, length)
    else:
        found = step_pixel(face_one, row_one, col_one, 0, col_step, length)
    return (found[0], found[1], found[2])

def tile_slot(face_id, tile_row, tile_col, side_tiles):
    group_id = face_id // 4
    within = face_id % 4
    extra = 1 if group_id == 2 else 0
    column = (side_tiles * (within + extra) + tile_col) % (4 * side_tiles)
    return 3 * side_tiles * column + side_tiles * group_id + tile_row

def padding_tables(side_tiles, pixels):
    slot_count = 12 * side_tiles * side_tiles
    span = pixels + 2
    length = side_tiles * pixels
    index_map = np.zeros((slot_count, span, span), np.int64)
    outer_places = []
    outer_sources = []
    for face_id in range(12):
        for tile_row in range(side_tiles):
            for tile_col in range(side_tiles):
                slot_id = tile_slot(face_id, tile_row, tile_col, side_tiles)
                for row_at in range(-1, pixels + 1):
                    for col_at in range(-1, pixels + 1):
                        inner_row = min(max(row_at, 0), pixels - 1)
                        inner_col = min(max(col_at, 0), pixels - 1)
                        if row_at == inner_row and col_at == inner_col:
                            source = slot_id * pixels * pixels + row_at * pixels + col_at
                        else:
                            partner, row_new, col_new = neighbour_pixel(face_id, tile_row * pixels + inner_row, tile_col * pixels + inner_col, row_at - inner_row, col_at - inner_col, length)
                            source_slot = tile_slot(partner, row_new // pixels, col_new // pixels, side_tiles)
                            source = source_slot * pixels * pixels + row_new % pixels * pixels + col_new % pixels
                            outer_places.append(slot_id * span * span + (row_at + 1) * span + col_at + 1)
                            outer_sources.append(source)
                        index_map[slot_id, row_at + 1, col_at + 1] = source
    return (index_map.reshape(-1), np.array(outer_places, np.int64), np.array(outer_sources, np.int64))

def gelu_exact(value):
    return 0.5 * value * (1.0 + lax.erf(value * inv_sqrt_two))

def gelu_slope(value):
    return 0.5 * (1.0 + lax.erf(value * inv_sqrt_two)) + value * jnp.exp(-0.5 * value * value) * inv_sqrt_tau

def conv_columns(padded, pixels):
    pieces = []
    for row_off in range(3):
        for col_off in range(3):
            pieces.append(padded[..., row_off:row_off + pixels, col_off:col_off + pixels, :])
    joined = jnp.concatenate(pieces, axis=-1)
    return joined.reshape(-1, joined.shape[-1])

def spread_back(columns, lead, pixels, channels):
    parts = columns.reshape(lead + (pixels, pixels, 9, channels))
    total_sum = jnp.zeros(lead + (pixels + 2, pixels + 2, channels), jnp.float32)
    for row_off in range(3):
        for col_off in range(3):
            widths = [(0, 0)] * len(lead) + [(row_off, 2 - row_off), (col_off, 2 - col_off), (0, 0)]
            total_sum = total_sum + jnp.pad(parts[..., row_off * 3 + col_off, :], widths)
    return total_sum

def reference(features, weight_one, bias_one, weight_two, bias_two, cotangent):
    index_np, places_np, sources_np = padding_tables(S, P_SIZE)
    index_map = jnp.asarray(index_np).astype(jnp.int32)
    outer_places = jnp.asarray(places_np).astype(jnp.int32)
    outer_sources = jnp.asarray(sources_np).astype(jnp.int32)
    mat_one = weight_one.reshape(9 * C, C)
    mat_two = weight_two.reshape(9 * C, C)

    def pad_field(field_flat):
        return jnp.take(field_flat, index_map, axis=0).reshape(TILES, P_SIZE + 2, P_SIZE + 2, C)

    def fold_field(grad_pad):
        inner_part = grad_pad[:, 1:-1, 1:-1, :].reshape(-1, C)
        outer = jnp.take(grad_pad.reshape(-1, C), outer_places, axis=0).astype(jnp.bfloat16)
        outer = lax.optimization_barrier(outer)
        return inner_part.at[outer_sources].add(outer.astype(jnp.float32))

    def sample_step(carry, inputs):
        sample, cot_sample = inputs
        columns_one = conv_columns(pad_field(sample.reshape(-1, C)), P_SIZE)
        pre_one = jnp.dot(columns_one, mat_one, preferred_element_type=jnp.float32) + bias_one
        hidden = gelu_exact(pre_one).astype(jnp.bfloat16)
        columns_two = conv_columns(pad_field(hidden), P_SIZE)
        pre_two = jnp.dot(columns_two, mat_two, preferred_element_type=jnp.float32) + bias_two
        output = gelu_exact(pre_two).astype(jnp.bfloat16)
        delta_two = (cot_sample.reshape(-1, C).astype(jnp.float32) * gelu_slope(pre_two)).astype(jnp.bfloat16)
        grad_w_two = lax.dot_general(columns_two, delta_two, (((0,), (0,)), ((), ())), preferred_element_type=jnp.float32)
        grad_b_two = lax.optimization_barrier(jnp.sum(delta_two.astype(jnp.float32), axis=0))
        back_two = lax.dot_general(delta_two, mat_two, (((1,), (1,)), ((), ())), preferred_element_type=jnp.float32)
        grad_hidden = fold_field(spread_back(back_two, (TILES,), P_SIZE, C))
        delta_one = (grad_hidden * gelu_slope(pre_one)).astype(jnp.bfloat16)
        grad_w_one = lax.dot_general(columns_one, delta_one, (((0,), (0,)), ((), ())), preferred_element_type=jnp.float32)
        grad_b_one = lax.optimization_barrier(jnp.sum(delta_one.astype(jnp.float32), axis=0))
        carry = (carry[0] + grad_w_one, carry[1] + grad_b_one, carry[2] + grad_w_two, carry[3] + grad_b_two)
        return (carry, output.reshape(TILES, P_SIZE, P_SIZE, C))
    start = (jnp.zeros((9 * C, C), jnp.float32), jnp.zeros((C,), jnp.float32), jnp.zeros((9 * C, C), jnp.float32), jnp.zeros((C,), jnp.float32))
    carry, stacked = lax.scan(sample_step, start, (jnp.moveaxis(features, 1, 0), jnp.moveaxis(cotangent, 1, 0)))
    grad_scale = 1.0 / math.sqrt(PIXELS)
    output = jnp.moveaxis(stacked, 0, 1)
    return (output, (carry[0] * grad_scale).reshape(3, 3, C, C), carry[1] * grad_scale, (carry[2] * grad_scale).reshape(3, 3, C, C), carry[3] * grad_scale)
```

```python
import functools
import math

import jax
import jax.numpy as jnp
import numpy as np
from jax import lax
from jax.experimental import pallas as pl
from jax.experimental.pallas import tpu as pltpu
from jax.sharding import PartitionSpec as P

S = 4


inv_sqrt_two = 0.7071067811865476
inv_sqrt_tau = 0.3989422804014327
LOG2_E = 1.4426950408889634
MESH = pl.DeviceIdType.MESH


def passed_along(value, axis, steps):
    count = lax.axis_size(axis)
    pairs = [(source, (source + steps) % count) for source in range(count)]
    return lax.ppermute(value, axis, pairs)


def edge_partner(face_id, edge_id):
    group_id = face_id // 4
    within = face_id % 4
    after_id = (within + 1) % 4
    before = (within + 3) % 4
    if group_id == 0:
        options = [(after_id, 2), (4 + within, 0), (before, 0), (4 + after_id, 2)]
    elif group_id == 1:
        options = [(within, 1), (8 + before, 0), (before, 3), (8 + within, 2)]
    else:
        options = [(4 + after_id, 1), (8 + before, 3), (4 + within, 3), (8 + after_id, 1)]
    return options[edge_id]


def entry_pixel(edge_id, along_edge, length):
    if edge_id == 0:
        return (0, along_edge)
    if edge_id == 1:
        return (length - 1, along_edge)
    if edge_id == 2:
        return (along_edge, 0)
    return (along_edge, length - 1)


def step_pixel(face_id, row_at, col_at, row_step, col_step, length):
    row_new = row_at + row_step
    col_new = col_at + col_step
    if 0 <= row_new < length and 0 <= col_new < length:
        return (face_id, row_new, col_new, -1)
    if row_new < 0:
        edge_id = 0
    elif row_new >= length:
        edge_id = 1
    elif col_new < 0:
        edge_id = 2
    else:
        edge_id = 3
    along_edge = col_at if edge_id < 2 else row_at
    partner, entered = edge_partner(face_id, edge_id)
    row_in, col_in = entry_pixel(entered, along_edge, length)
    return (partner, row_in, col_in, entered)


def neighbour_pixel(face_id, row_at, col_at, row_step, col_step, length):
    if row_step == 0 or col_step == 0:
        found = step_pixel(face_id, row_at, col_at, row_step, col_step, length)
        return (found[0], found[1], found[2])
    face_one, row_one, col_one, entered = step_pixel(face_id, row_at, col_at, row_step, 0, length)
    if entered >= 2:
        found = step_pixel(face_one, row_one, col_one, col_step, 0, length)
    else:
        found = step_pixel(face_one, row_one, col_one, 0, col_step, length)
    return (found[0], found[1], found[2])


def tile_slot(face_id, tile_row, tile_col, side_tiles):
    group_id = face_id // 4
    within = face_id % 4
    extra = 1 if group_id == 2 else 0
    column = (side_tiles * (within + extra) + tile_col) % (4 * side_tiles)
    return 3 * side_tiles * column + side_tiles * group_id + tile_row


def cycle_position(row_at, col_at, pixels):
    if row_at == 0:
        return col_at
    if row_at == pixels - 1:
        return pixels + col_at
    if col_at == 0:
        return 2 * pixels + row_at
    return 3 * pixels + row_at


def halo_positions(pixels):
    places = [(-1, column) for column in range(-1, pixels + 1)]
    places = places + [(pixels, column) for column in range(-1, pixels + 1)]
    places = places + [(row_at, -1) for row_at in range(pixels)]
    places = places + [(row_at, pixels) for row_at in range(pixels)]
    return places


def halo_sources(side_tiles, pixels):
    slot_count = 12 * side_tiles * side_tiles
    places = halo_positions(pixels)
    length = side_tiles * pixels
    source_slot = np.zeros((slot_count, len(places)), np.int64)
    source_cycle = np.zeros((slot_count, len(places)), np.int64)
    for face_id in range(12):
        for tile_row in range(side_tiles):
            for tile_col in range(side_tiles):
                slot_id = tile_slot(face_id, tile_row, tile_col, side_tiles)
                for cell_index in range(len(places)):
                    row_at, col_at = places[cell_index]
                    inner_row = min(max(row_at, 0), pixels - 1)
                    inner_col = min(max(col_at, 0), pixels - 1)
                    partner, row_new, col_new = neighbour_pixel(
                        face_id,
                        tile_row * pixels + inner_row,
                        tile_col * pixels + inner_col,
                        row_at - inner_row,
                        col_at - inner_col,
                        length,
                    )
                    source_slot[slot_id, cell_index] = tile_slot(
                        partner, row_new // pixels, col_new // pixels, side_tiles
                    )
                    source_cycle[slot_id, cell_index] = cycle_position(
                        row_new % pixels, col_new % pixels, pixels
                    )
    return (source_slot, source_cycle)


def halo_rows(row_at, col_at, pixels):
    if row_at == -1 or row_at == pixels:
        base = 0 if row_at == -1 else 3 * pixels
        return [
            base + pixels * shift + col_at + 1 - shift
            for shift in range(3)
            if 0 <= col_at + 1 - shift < pixels
        ]
    return [6 * pixels + row_at if col_at == -1 else 7 * pixels + row_at]


def outer_row(row_at, col_at, pixels):
    if col_at == -1:
        return 2 * pixels + row_at + 1
    if col_at == pixels:
        return 4 * pixels + row_at + 1
    return col_at if row_at == -1 else pixels + col_at


def device_tables(device_count, per_device, side_tiles, pixels):
    source_slot, source_cycle = halo_sources(side_tiles, pixels)
    places = halo_positions(pixels)
    rim_len, halo_len, outer_len = 4 * pixels, 8 * pixels, 6 * pixels
    sends = {}
    local = []
    for device in range(device_count):
        local.append([])
        for local_id in range(per_device):
            slot_id = device * per_device + local_id
            for cell in range(len(places)):
                row_at, col_at = places[cell]
                source = int(source_slot[slot_id, cell])
                moved_by = (device - source // per_device) % device_count
                if moved_by > device_count // 2:
                    moved_by -= device_count
                rim = source % per_device * rim_len + int(source_cycle[slot_id, cell])
                halo = [local_id * halo_len + h for h in halo_rows(row_at, col_at, pixels)]
                outer = local_id * outer_len + outer_row(row_at, col_at, pixels)
                record = (rim, halo, outer)
                if moved_by == 0:
                    local[device].append(record)
                else:
                    lists = sends.setdefault(moved_by, [[] for _ in range(device_count)])
                    lists[device].append(record)
    offsets = sorted(sends)
    widths = [-(-max(len(one) for one in sends[offset]) // 16) * 16 for offset in offsets]
    total = sum(widths)
    send = np.full((device_count, total), -1, np.int32)
    receive = np.full((device_count, per_device * halo_len), -1, np.int32)
    back = np.full((device_count, total), -1, np.int32)
    target = np.full((device_count, per_device * outer_len + total), -1, np.int32)
    for device in range(device_count):
        for rim, halo, outer in local[device]:
            receive[device, halo] = rim
            target[device, outer] = rim
        base = 0
        for offset, width in zip(offsets, widths):
            sender = (device - offset) % device_count
            for at, (rim, halo, outer) in enumerate(sends[offset][device]):
                send[sender, base + at] = rim
                receive[device, halo] = per_device * rim_len + base + at
                back[device, base + at] = outer
                target[sender, per_device * outer_len + base + at] = rim
            base += width
    return (offsets, widths, send, receive, back, target)


def one_hot(table_np, tile_index, width):
    row = jnp.asarray(table_np, dtype=jnp.int32)[tile_index]
    return (row[:, None] == lax.broadcasted_iota(jnp.int32, (row.shape[0], width), 1)).astype(
        jnp.bfloat16
    )


def exchanged(rows, offsets, widths, sign):
    pieces, base = [], 0
    for offset, width in zip(offsets, widths):
        pieces.append(passed_along(rows[base : base + width], "tile", sign * offset))
        base += width
    return pieces


def halo_of(rim, layout, tile_index):
    offsets, widths, send, receive = layout[:4]
    outgoing = jnp.dot(one_hot(send, tile_index, rim.shape[0]), rim)
    pool = jnp.concatenate([rim] + exchanged(outgoing, offsets, widths, 1), axis=0)
    return jnp.dot(one_hot(receive, tile_index, pool.shape[0]), pool)


def folded(outer, layout, tile_index, rim_rows):
    offsets, widths, _, _, back, target = layout
    outgoing = jnp.dot(one_hot(back, tile_index, outer.shape[0]), outer)
    pool = jnp.concatenate([outer] + exchanged(outgoing, offsets, widths, -1), axis=0)
    spread = one_hot(target, tile_index, rim_rows)
    return lax.dot_general(
        spread, pool, (((0,), (0,)), ((), ())), preferred_element_type=jnp.float32
    )


def gelu_parts(value):
    half = 0.5 * (1.0 + lax.erf(value * inv_sqrt_two))
    return value * half, half + value * jnp.exp(-0.5 * value * value) * inv_sqrt_tau


def columns_at(tile, halo, work, pixels):
    count = pixels * pixels
    wide = tile.astype(jnp.float32)
    halo_wide = halo[6 * pixels :].astype(jnp.float32)
    work[0, pl.ds(1, count - 1), :] = wide[: count - 1]
    work[0, pl.ds(0, pixels, stride=pixels), :] = halo_wide[:pixels]
    work[1, pl.ds(0, count - 1), :] = wide[1:]
    work[1, pl.ds(pixels - 1, pixels, stride=pixels), :] = halo_wide[pixels:]
    middles = [work[0].astype(jnp.bfloat16), tile, work[1].astype(jnp.bfloat16)]
    joined = jnp.concatenate(
        [
            jnp.concatenate(
                [
                    halo[pixels * b : pixels * (b + 1)],
                    middles[b],
                    halo[pixels * (3 + b) : pixels * (4 + b)],
                ],
                axis=0,
            )
            for b in range(3)
        ],
        axis=1,
    )
    return jnp.concatenate([joined[pixels * a : pixels * a + count] for a in range(3)], axis=1)


def first_kernel(x_ref, halo_ref, w_ref, bias_ref, hidden_ref, slope_ref, rim_ref, work):
    batch, pixels, channels = x_ref.shape[1], x_ref.shape[2], x_ref.shape[4]
    count = pixels * pixels
    for s in range(batch):
        lanes = slice(s * channels, (s + 1) * channels)
        tile = x_ref[0, s].reshape(count, channels)
        cols = columns_at(tile, halo_ref[0, :, lanes], work.at[pl.ds(2 * s, 2)], pixels)
        pre = jnp.dot(cols, w_ref[...], preferred_element_type=jnp.float32) + bias_ref[...]
        hidden, slope = gelu_parts(pre)
        slope_ref[0, s] = slope
        work[2 * batch + s] = hidden
        rounded = hidden.astype(jnp.bfloat16)
        hidden_ref[0, s] = rounded.reshape(pixels, pixels, channels)
        rim_ref[0, 0:pixels, lanes] = rounded[:pixels]
        rim_ref[0, pixels : 2 * pixels, lanes] = rounded[count - pixels :]
        for side in range(2):
            edge = work[2 * batch + s, pl.ds(side * (pixels - 1), pixels, stride=pixels), :]
            rim_ref[0, (2 + side) * pixels : (3 + side) * pixels, lanes] = edge.astype(jnp.bfloat16)


def second_kernel(
    x_ref, halo_ref, cot_ref, w_ref, flip_ref, side_ref, bias_ref,
    out_ref, inner_ref, outer_ref, grad_ref, sum_ref, work, cols_ref, delta_ref, edge_ref,
):
    batch, pixels, channels = x_ref.shape[1], x_ref.shape[2], x_ref.shape[4]
    count = pixels * pixels

    @pl.when(pl.program_id(0) == 0)
    def _():
        grad_ref[...] = jnp.zeros_like(grad_ref)
        sum_ref[...] = jnp.zeros_like(sum_ref)

    zero_row = jnp.zeros((1, channels), jnp.float32)
    zero_col = jnp.zeros((pixels, channels), jnp.float32)
    zeros = jnp.zeros((2 * pixels, 3 * channels), jnp.bfloat16)
    for s in range(batch):
        lanes = slice(s * channels, (s + 1) * channels)
        tile = x_ref[0, s].reshape(count, channels)
        here = work.at[pl.ds(2 * s, 2)]
        cols = columns_at(tile, halo_ref[0, :, lanes], here, pixels)
        cols_ref[s * count : (s + 1) * count, :] = cols
        pre = jnp.dot(cols, w_ref[...], preferred_element_type=jnp.float32) + bias_ref[...]
        value, slope = gelu_parts(pre)
        out_ref[0, s] = value.astype(jnp.bfloat16).reshape(pixels, pixels, channels)
        cot = cot_ref[0, s].reshape(count, channels).astype(jnp.float32)
        delta = (cot * slope).astype(jnp.bfloat16)
        delta_ref[s * count : (s + 1) * count, :] = delta
        wide = delta.astype(jnp.float32)
        sum_ref[...] += jnp.sum(wide, axis=0, keepdims=True)
        edge_ref[s] = jnp.zeros(edge_ref.shape[1:], jnp.float32)
        work[2 * batch + s] = wide
        for side in range(2):
            edge_ref[s, side, pl.ds(2, pixels), :] = work[
                2 * batch + s, pl.ds(side * (pixels - 1), pixels, stride=pixels), :
            ]
        here[0, pl.ds(0, count - 1), :] = wide[1:]
        here[0, pl.ds(pixels - 1, pixels, stride=pixels), :] = zero_col
        here[1, pl.ds(1, count - 1), :] = wide[: count - 1]
        here[1, pl.ds(0, pixels, stride=pixels), :] = zero_col
        joined = jnp.concatenate(
            [here[0].astype(jnp.bfloat16), delta, here[1].astype(jnp.bfloat16)], axis=1
        )
        joined = jnp.concatenate([zeros, joined, zeros], axis=0)
        tall = count + 2 * pixels
        spread = jnp.concatenate(
            [joined[pixels * (2 - a) : pixels * (2 - a) + tall] for a in range(3)], axis=1
        )
        grad = jnp.dot(spread, flip_ref[...], preferred_element_type=jnp.float32)
        inner_ref[0, s] = grad[pixels : pixels + count]
        outer_ref[0, 0:pixels, lanes] = grad[:pixels].astype(jnp.bfloat16)
        outer_ref[0, pixels : 2 * pixels, lanes] = grad[pixels + count :].astype(jnp.bfloat16)
        for side in range(2):
            lhs = jnp.concatenate(
                [edge_ref[s, side, pl.ds(2 - a, 2 * pixels), :] for a in range(3)], axis=1
            ).astype(jnp.bfloat16)
            part = jnp.dot(lhs, side_ref[side], preferred_element_type=jnp.float32)
            outer_ref[0, 2 * pixels * (1 + side) : 2 * pixels * (2 + side), lanes] = part.astype(
                jnp.bfloat16
            )
    grad_ref[...] += lax.dot_general(
        delta_ref[...], cols_ref[...], (((0,), (0,)), ((), ())), preferred_element_type=jnp.float32
    )


def third_kernel(
    x_ref, halo_ref, inner_ref, rim_ref, slope_ref, grad_ref, sum_ref, work, cols_ref, delta_ref
):
    batch, pixels, channels = x_ref.shape[1], x_ref.shape[2], x_ref.shape[4]
    count = pixels * pixels

    @pl.when(pl.program_id(0) == 0)
    def _():
        grad_ref[...] = jnp.zeros_like(grad_ref)
        sum_ref[...] = jnp.zeros_like(sum_ref)

    for s in range(batch):
        lanes = slice(s * channels, (s + 1) * channels)
        tile = x_ref[0, s].reshape(count, channels)
        cols_ref[s * count : (s + 1) * count, :] = columns_at(
            tile, halo_ref[0, :, lanes], work.at[pl.ds(2 * s, 2)], pixels
        )
        at = 2 * batch + s
        work[at] = inner_ref[0, s]
        work[at, pl.ds(0, pixels), :] += rim_ref[0, 0:pixels, lanes]
        work[at, pl.ds(count - pixels, pixels), :] += rim_ref[0, pixels : 2 * pixels, lanes]
        for side in range(2):
            place = pl.ds(side * (pixels - 1), pixels, stride=pixels)
            edge = rim_ref[0, (2 + side) * pixels : (3 + side) * pixels, lanes]
            work[at, place, :] = work[at, place, :] + edge
        delta = (work[at] * slope_ref[0, s]).astype(jnp.bfloat16)
        delta_ref[s * count : (s + 1) * count, :] = delta
        sum_ref[...] += jnp.sum(delta.astype(jnp.float32), axis=0, keepdims=True)
    grad_ref[...] += lax.dot_general(
        delta_ref[...], cols_ref[...], (((0,), (0,)), ((), ())), preferred_element_type=jnp.float32
    )


def per_tile(shape):
    return pl.BlockSpec((1,) + tuple(shape), lambda t: (t,) + (0,) * len(shape))


def whole(shape):
    return pl.BlockSpec(tuple(shape), lambda t: (0,) * len(shape))


params = dict(vmem_limit_bytes=48 * 1024 * 1024)


def body(features, weight_one, bias_one, weight_two, bias_two, cotangent):
    device_count = lax.axis_size("tile")
    samples_count = lax.axis_size("tm")
    tile_index = lax.axis_index("tile")
    per_device, batch, pixels, _, channels = features.shape
    count = pixels * pixels
    lane_count = batch * channels
    layout = device_tables(device_count, per_device, S, pixels)
    bf16, f32 = jnp.bfloat16, jnp.float32
    tile_shape = (batch, pixels, pixels, channels)
    flat_shape = (batch, count, channels)
    halo_shape = (8 * pixels, lane_count)
    rim_shape = (4 * pixels, lane_count)
    outer_shape = (6 * pixels, lane_count)
    mat_one = weight_one.reshape(9 * channels, channels)
    mat_two = weight_two.reshape(9 * channels, channels)
    turned = weight_two.transpose(0, 1, 3, 2)
    flip = turned.reshape(9 * channels, channels)
    sides = jnp.stack([turned[:, 0], turned[:, 2]]).reshape(2, 3 * channels, channels)

    def out(shape, dtype):
        return jax.ShapeDtypeStruct((per_device,) + tuple(shape), dtype)

    work = pltpu.VMEM((3 * batch, count, channels), f32)
    cols = pltpu.VMEM((batch * count, 9 * channels), bf16)
    deltas = pltpu.VMEM((batch * count, channels), bf16)
    grad_shape = (channels, 9 * channels)

    rim_one = jnp.concatenate(
        [features[:, :, 0], features[:, :, -1], features[:, :, :, 0], features[:, :, :, -1]], axis=2
    )
    rim_one = rim_one.transpose(0, 2, 1, 3).reshape(per_device * 4 * pixels, lane_count)
    halo_one = halo_of(rim_one, layout, tile_index).reshape((per_device,) + halo_shape)
    hidden, slope, rim_two = pl.pallas_call(
        first_kernel,
        grid=(per_device,),
        in_specs=[per_tile(tile_shape), per_tile(halo_shape), whole(mat_one.shape), whole((1, channels))],
        out_specs=[per_tile(tile_shape), per_tile(flat_shape), per_tile(rim_shape)],
        out_shape=[out(tile_shape, bf16), out(flat_shape, f32), out(rim_shape, bf16)],
        scratch_shapes=[work],
        compiler_params=pltpu.CompilerParams(**params),
    )(features, halo_one, mat_one, bias_one.reshape(1, channels))
    halo_two = halo_of(rim_two.reshape(-1, lane_count), layout, tile_index)
    output, inner, outer, grad_two, sum_two = pl.pallas_call(
        second_kernel,
        grid=(per_device,),
        in_specs=[
            per_tile(tile_shape), per_tile(halo_shape), per_tile(tile_shape), whole(mat_two.shape),
            whole(flip.shape), whole(sides.shape), whole((1, channels)),
        ],
        out_specs=[
            per_tile(tile_shape), per_tile(flat_shape), per_tile(outer_shape),
            whole(grad_shape), whole((1, channels)),
        ],
        out_shape=[
            out(tile_shape, bf16), out(flat_shape, f32), out(outer_shape, bf16),
            jax.ShapeDtypeStruct(grad_shape, f32), jax.ShapeDtypeStruct((1, channels), f32),
        ],
        scratch_shapes=[work, cols, deltas, pltpu.VMEM((batch, 2, 2 * pixels + 8, channels), f32)],
        compiler_params=pltpu.CompilerParams(**params),
    )(
        hidden, halo_two.reshape((per_device,) + halo_shape), cotangent, mat_two, flip, sides,
        bias_two.reshape(1, channels),
    )
    rim_grad = folded(outer.reshape(-1, lane_count), layout, tile_index, per_device * 4 * pixels)
    grad_one, sum_one = pl.pallas_call(
        third_kernel,
        grid=(per_device,),
        in_specs=[
            per_tile(tile_shape), per_tile(halo_shape), per_tile(flat_shape), per_tile(rim_shape),
            per_tile(flat_shape),
        ],
        out_specs=[whole(grad_shape), whole((1, channels))],
        out_shape=[jax.ShapeDtypeStruct(grad_shape, f32), jax.ShapeDtypeStruct((1, channels), f32)],
        scratch_shapes=[work, cols, deltas],
        compiler_params=pltpu.CompilerParams(**params),
    )(features, halo_one, inner, rim_grad.reshape((per_device,) + rim_shape), slope)

    total_pixels = 12 * S * S * count * batch * samples_count
    grad_scale = 1.0 / math.sqrt(total_pixels)
    devices = device_count * samples_count
    axes = ("tile", "tm")

    def summed(grad, bias):
        rows = jnp.concatenate([grad.reshape(-1, channels), bias], axis=0)
        used = rows.shape[0]
        chunk = -(-used // (8 * devices)) * 8
        rows = jnp.pad(rows, ((0, chunk * devices - used), (0, 0)))
        parts = lax.all_to_all(rows.reshape(devices, chunk, channels), axes, 0, 0)
        mine = (jnp.sum(parts, axis=0) * grad_scale).astype(bf16)
        copies = jnp.broadcast_to(mine[None], (devices, chunk, channels))
        total = lax.all_to_all(copies, axes, 0, 0).reshape(devices * chunk, channels).astype(f32)
        weight = total[: used - 1].reshape(channels, 3, 3, channels).transpose(1, 2, 3, 0)
        return weight, total[used - 1]

    grad_weight_two, grad_bias_two = summed(grad_two, sum_two)
    grad_weight_one, grad_bias_one = summed(grad_one, sum_one)
    return (output, grad_weight_one, grad_bias_one, grad_weight_two, grad_bias_two)


def cdf_parts(value):
    bell = jnp.exp2(value * value * (-0.5 * LOG2_E))
    t = 1.0 / (1.0 + (0.3275911 * inv_sqrt_two) * jnp.abs(value))
    poly = 0.5 * 1.061405429
    for coefficient in (-1.453152027, 1.421413741, -0.284496736, 0.254829592):
        poly = poly * t + 0.5 * coefficient
    tail = poly * t * bell
    return jnp.where(value < 0.0, tail, 1.0 - tail), bell


def put_shifted(ref, sample, base, rows, left, right):
    lanes = rows[0].shape[1]
    half = lax.broadcasted_iota(jnp.int32, (8, lanes), 0)
    first, last = half == 0, half == 7
    zero = jnp.zeros((8, lanes), jnp.float32)
    for t, row in enumerate(rows):
        low, high = row[:8], row[8:]
        group, at = 8 * (t // 8), t % 8
        if left is None:
            from_left, from_right = zero, zero
        else:
            from_left = turned_by(left[group : group + 8], -at)
            from_right = turned_by(right[group : group + 8], 7 - at)
        low_down, high_down = turned_by(low, 1), turned_by(high, 1)
        shifted = jnp.concatenate(
            [jnp.where(first, from_left, low_down), jnp.where(first, low_down, high_down)], axis=0
        )
        ref[sample, base + t, :, 0:lanes] = shifted.astype(jnp.bfloat16)
        low_up, high_up = turned_by(low, 7), turned_by(high, 7)
        shifted = jnp.concatenate(
            [jnp.where(last, high_up, low_up), jnp.where(last, from_right, high_up)], axis=0
        )
        ref[sample, base + t, :, 2 * lanes : 3 * lanes] = shifted.astype(jnp.bfloat16)


def turned_by(value, steps):
    steps = steps % 8
    return value if steps == 0 else pltpu.roll(value, steps, 0)


def edges_of(rows):
    lanes = rows[0].shape[1]
    half = lax.broadcasted_iota(jnp.int32, (8, lanes), 0)
    lefts, rights = [], []
    for group in range(0, len(rows), 8):
        left = rows[group][:8]
        right = turned_by(rows[group][8:], 1)
        for t in range(1, 8):
            left = jnp.where(half == t, turned_by(rows[group + t][:8], t), left)
            right = jnp.where(half == t, turned_by(rows[group + t][8:], t + 1), right)
        lefts.append(left)
        rights.append(right)
    return jnp.concatenate(lefts, axis=0), jnp.concatenate(rights, axis=0)


def split_pairs(value, channels):
    rows = []
    for p in range(value.shape[0] // 16):
        for e in range(2):
            rows.append(value[16 * p : 16 * (p + 1), e * channels : (e + 1) * channels])
    return rows


def pair_window(ref, sample, start, pairs):
    width = ref.shape[3]
    v = ref[sample, pl.ds(start, 2 * pairs + 2)].reshape(pairs + 1, 2, 16, width)
    parts = [v[:pairs, 0], v[:pairs, 1], v[1:, 0], v[1:, 1]]
    return jnp.concatenate([p.reshape(pairs * 16, width) for p in parts], axis=1)


def strip_kernel(
    tm_count,
    x_hbm, cot_hbm, w1_ref, b1_ref, w2_ref, b2_ref,
    out_hbm, gw1_ref, gb1_ref, gw2_ref, gb2_ref,
    field, xs, hs, ds, d1, slope, ghid, w1p, w2p, wback, wside, acc, bias_acc,
    edge_f, fold_f, edge_send, halo_recv, outer_send, corner_send, outer_recv,
    grad_send, grad_recv, plane_recv, plane_send, part_send, part_recv,
    in_sem, cot_sem, out_sem, send_sem, recv_sem, osend_sem, orecv_sem, gsend_sem, grecv_sem,
):
    f32, bf16 = jnp.float32, jnp.bfloat16
    tiles, batch, pixels, _, C = x_hbm.shape
    height = tiles * pixels
    columns = 16
    me = lax.axis_index("tile")
    other = lax.axis_index("tm")
    n, j = me // 4, me % 4
    peers = 4 * tm_count
    plane = j * tm_count + other

    def wrap(c):
        return (c + 2 * columns) % columns

    def dma_in(s):
        return pltpu.make_async_copy(x_hbm.at[:, s], field.at[:, s], in_sem.at[s])

    def dma_cot(s):
        return pltpu.make_async_copy(cot_hbm.at[:, s], field.at[:, s], cot_sem.at[s])

    def dma_out(s):
        return pltpu.make_async_copy(field.at[:, s], out_hbm.at[:, s], out_sem.at[s])

    def remote(src, dst, send, recv, device, side=None):
        pltpu.make_async_remote_copy(
            src_ref=src, dst_ref=dst, send_sem=send, recv_sem=recv,
            device_id=(device, other if side is None else side), device_id_type=MESH,
        ).start()

    def finish(ref, count, sem):
        view = ref.at[pl.ds(0, count)]
        pltpu.make_async_copy(view, view, sem).wait()

    for s in range(batch):
        dma_in(s).start()

    barrier = pltpu.get_barrier_semaphore()
    for offset in range(1, columns):
        pl.semaphore_signal(
            barrier, inc=1, device_id=(wrap(me + offset), other), device_id_type=MESH
        )
    for step in range(1, tm_count):
        for jj in range(4):
            pl.semaphore_signal(
                barrier, inc=1, device_id=(4 * n + jj, (other + step) % tm_count),
                device_id_type=MESH,
            )
    pl.semaphore_wait(barrier, columns - 1 + 4 * (tm_count - 1))

    def send_rim(f, s, field_ref, top, bottom):
        es, er = edge_send.at[f, s, 0], edge_send.at[f, s, 1]
        ss, rs = send_sem.at[f, s], recv_sem.at[f, s]
        land = halo_recv.at[f, s]

        def cut(ref, start, count):
            return ref.at[pl.ds(start, count)]

        @pl.when(j >= 1)
        def _():
            remote(cut(es, 16, height), cut(land, height, height), ss, rs, wrap(me - 1))

        @pl.when(j == 0)
        def _():
            remote(cut(es, 80, height - 64), cut(land, height, height - 64), ss, rs, wrap(me - 1))

        @pl.when(j <= 2)
        def _():
            remote(cut(er, 0, height), cut(land, 0, height), ss, rs, wrap(me + 1))

        @pl.when(j == 3)
        def _():
            remote(cut(er, 0, height - 64), cut(land, 64, height - 64), ss, rs, wrap(me + 1))

        remote(top, cut(land, 16 * j, 16), ss, rs, wrap(4 * n + 4))
        remote(bottom, cut(land, height + 128 + 16 * j, 16), ss, rs, wrap(4 * n - 1))
        upper, lower = 2 * height, 2 * height + 48

        @pl.when(j == 0)
        def _():
            remote(cut(es, 16, 32), cut(land, upper + 16, 32), ss, rs, wrap(me - 4))
            for jj in range(1, 4):
                remote(cut(es, 16 * jj, 48), cut(land, upper, 48), ss, rs, wrap(me - 4 + jj))
            remote(cut(es, 0, 16), cut(land, upper, 16), ss, rs, wrap(me + 8))

        @pl.when(j == 3)
        def _():
            for jj in range(3):
                remote(
                    cut(er, 112 + 16 * jj, 48), cut(land, lower, 48), ss, rs, wrap(me + 1 + jj)
                )
            remote(cut(er, height - 32, 32), cut(land, lower, 32), ss, rs, wrap(me + 4))
            remote(cut(er, height, 16), cut(land, lower + 32, 16), ss, rs, wrap(me + 8))

    def put_edges(f, s, k, rows):
        left, right = edges_of(rows)
        edge_send[f, s, 0, pl.ds(16 + 16 * k, 16), :] = left.astype(bf16)
        edge_send[f, s, 1, pl.ds(16 * k, 16), :] = right.astype(bf16)

    def put_corners(f, s):
        row = edge_send[f, s, 0, 16:32, :].astype(f32)
        edge_send[f, s, 0, 0:16, :] = jnp.broadcast_to(row[0:1], (16, C)).astype(bf16)
        row = edge_send[f, s, 1, height - 16 : height, :].astype(f32)
        edge_send[f, s, 1, height : height + 16, :] = jnp.broadcast_to(row[15:16], (16, C)).astype(
            bf16
        )

    def put_halo_rows(f, s, ref):
        for side in range(2):
            edge_f[0:48, :] = halo_recv[f, s, pl.ds(2 * height + 48 * side, 48), :].astype(f32)
            for b in range(3):
                ref[s, side * (height + 1), :, b * C : (b + 1) * C] = edge_f[
                    15 + b : 31 + b, :
                ].astype(bf16)

    def shift_tile(f, s, k, ref, rows):
        left = halo_recv[f, s, pl.ds(16 * k, 16), :].astype(f32)
        right = halo_recv[f, s, pl.ds(height + 16 * k, 16), :].astype(f32)
        put_shifted(ref, s, 1 + 16 * k, rows, left, right)

    def features_out(s, carry):
        dma_in(s).wait()

        def step(k, carry):
            rows = [field[k, s, t].astype(f32) for t in range(16)]
            put_edges(0, s, k, rows)
            return carry

        lax.fori_loop(0, tiles, step, 0)
        put_corners(0, s)
        send_rim(0, s, field, field.at[0, s, 0], field.at[tiles - 1, s, pixels - 1])
        return carry

    lax.fori_loop(0, batch, features_out, 0)

    one, two = w1_ref[...].reshape(9 * C, C), w2_ref[...].reshape(9 * C, C)
    zeros = jnp.zeros((3 * C, C), bf16)
    for packed, flat in ((w1p, one), (w2p, two)):
        packed[0 : 9 * C, 0:C] = flat
        packed[9 * C : 12 * C, 0:C] = zeros
        packed[0 : 3 * C, C : 2 * C] = zeros
        packed[3 * C : 12 * C, C : 2 * C] = flat
    for e in range(2):
        gap = 3 * (1 - e)
        wback[(9 if e == 0 else 0) * C + 0 : (12 if e == 0 else 3) * C, e * C : (e + 1) * C] = zeros
    for a in range(3):
        for b in range(3):
            block = w2_ref[a, b].astype(f32).T.astype(bf16)
            for e in range(2):
                at = ((2 + e - a) * 3 + 2 - b) * C
                wback[at : at + C, e * C : (e + 1) * C] = block
            if b != 1:
                wside[b // 2, a * C : (a + 1) * C, :] = block

    bias_one = jnp.concatenate([b1_ref[...], b1_ref[...]], axis=1)
    bias_two = jnp.concatenate([b2_ref[...], b2_ref[...]], axis=1)
    bias_acc[...] = jnp.zeros_like(bias_acc)

    def stage_one(s, carry):
        finish(halo_recv.at[0, s], 2 * height + 96, recv_sem.at[0, s])
        put_halo_rows(0, s, xs)

        def build(k, carry):
            for t in range(16):
                xs[s, 1 + 16 * k + t, :, C : 2 * C] = field[k, s, t]
            rows = [field[k, s, t].astype(f32) for t in range(16)]
            shift_tile(0, s, k, xs, rows)
            return carry

        lax.fori_loop(0, tiles, build, 0)

        def conv(c, carry):
            pre = jnp.dot(pair_window(xs, s, 32 * c, 16), w1p[...], preferred_element_type=f32)
            pre = pre + bias_one
            half, bell = cdf_parts(pre)
            hidden = pre * half
            rows = split_pairs(hidden, C)
            slopes = split_pairs(half + pre * (bell * inv_sqrt_tau), C)
            for t in range(32):
                hs[s, 1 + 32 * c + t, :, C : 2 * C] = rows[t].astype(bf16)
                slope[s, 32 * c + t] = slopes[t]
            put_edges(1, s, 2 * c, rows[:16])
            put_edges(1, s, 2 * c + 1, rows[16:])
            return carry

        lax.fori_loop(0, tiles // 2, conv, 0)
        put_corners(1, s)
        top = hs.at[s, 1, :, pl.ds(C, C)]
        bottom = hs.at[s, height, :, pl.ds(C, C)]
        send_rim(1, s, hs, top, bottom)
        @pl.when((j == 0) | (j == 3))
        def _():
            finish(all_rows, 544, send_sem.at[0, s])

        @pl.when((j != 0) & (j != 3))
        def _():
            finish(all_rows, 416, send_sem.at[0, s])

        dma_cot(s).start()
        return carry

    all_rows = grad_recv.at[0]
    lax.fori_loop(0, batch, stage_one, 0)

    for at in (0, 1, height + 2, height + 3, height + 4, height + 5):
        ds[0, at] = jnp.zeros((pixels, 3 * C), bf16)
    for side in range(2):
        edge_f[48 + 240 * side : 48 + 240 * side + 24, :] = jnp.zeros((24, C), f32)
        edge_f[48 + 240 * side + 24 + height : 288 + 240 * side, :] = jnp.zeros(
            (216 - height, C), f32
        )
    acc[...] = jnp.zeros_like(acc)

    def send_outer(s):
        ss, rs = osend_sem.at[s], orecv_sem.at[s]
        ol, orr = outer_send.at[s, 0], outer_send.at[s, 1]
        tb, bb = corner_send.at[s, 0], corner_send.at[s, 1]
        land = outer_recv.at[s]
        g_top, g_bottom, extra = 2 * height, 2 * height + 16, 2 * height + 32

        def cut(ref, start, count):
            return ref.at[pl.ds(start, count)]

        @pl.when(j >= 1)
        def _():
            remote(cut(ol, 16, height), cut(land, height, height), ss, rs, wrap(me - 1))

        @pl.when(j <= 2)
        def _():
            remote(cut(orr, 16, height), cut(land, 0, height), ss, rs, wrap(me + 1))

        @pl.when(j == 0)
        def _():
            remote(cut(ol, 80, height - 64), cut(land, height, height - 64), ss, rs, wrap(me - 1))
            for i in range(4):
                remote(cut(ol, 16 + 16 * i, 16), cut(land, g_top, 16), ss, rs, wrap(me - 4 + i))
            remote(cut(tb, 0, 16), cut(land, extra + 192, 16), ss, rs, wrap(me + 8))

        @pl.when(j == 3)
        def _():
            remote(cut(orr, 16, height - 64), cut(land, 64, height - 64), ss, rs, wrap(me + 1))
            for i in range(4):
                remote(
                    cut(orr, 144 + 16 * i, 16), cut(land, g_bottom, 16), ss, rs, wrap(me + 1 + i)
                )
            remote(cut(bb, 32, 16), cut(land, extra + 192, 16), ss, rs, wrap(me + 8))

        remote(tb, cut(land, extra + 48 * j, 48), ss, rs, wrap(4 * n + 4))
        remote(bb, cut(land, extra + 48 * j, 48), ss, rs, wrap(4 * n - 1))

    def stage_two(s, carry):
        finish(halo_recv.at[1, s], 2 * height + 96, recv_sem.at[1, s])
        put_halo_rows(1, s, hs)

        def build(k, carry):
            rows = [hs[s, 1 + 16 * k + t, :, C : 2 * C].astype(f32) for t in range(16)]
            shift_tile(1, s, k, hs, rows)
            return carry

        lax.fori_loop(0, tiles, build, 0)
        dma_cot(s).wait()

        def conv(c, carry):
            pre = jnp.dot(pair_window(hs, s, 32 * c, 16), w2p[...], preferred_element_type=f32)
            pre = pre + bias_two
            half, bell = cdf_parts(pre)
            outs = split_pairs(pre * half, C)
            slopes = split_pairs(half + pre * (bell * inv_sqrt_tau), C)
            total = jnp.zeros((pixels, C), f32)
            for q in range(2):
                deltas = []
                for t in range(16):
                    cot = field[2 * c + q, s, t].astype(f32)
                    delta = cot * slopes[16 * q + t]
                    field[2 * c + q, s, t] = outs[16 * q + t].astype(bf16)
                    ds[0, 2 + 32 * c + 16 * q + t, :, C : 2 * C] = delta.astype(bf16)
                    total = total + delta
                    deltas.append(delta)
                put_shifted(ds, 0, 2 + 32 * c + 16 * q, deltas, None, None)
                left, right = edges_of(deltas)
                edge_f[pl.ds(72 + 32 * c + 16 * q, 16), :] = left
                edge_f[pl.ds(312 + 32 * c + 16 * q, 16), :] = right
            bias_acc[1] += total
            return carry

        lax.fori_loop(0, tiles // 2, conv, 0)
        dma_out(s).start()

        fold_f[0:96, :] = jnp.zeros((96, C), f32)
        for side in range(2):
            base = 48 + 240 * side
            lhs = jnp.concatenate(
                [edge_f[base + 9 - a : base + 233 - a, :] for a in range(3)], axis=1
            ).astype(bf16)
            cells = jnp.dot(lhs, wside[side], preferred_element_type=f32)
            outer_send[s, side] = cells.astype(bf16)
            fold_f[15 + 17 * side : 16 + 17 * side, :] = cells[15:16]
            fold_f[63 + 17 * side : 64 + 17 * side, :] = cells[16 + height : 17 + height]

        def back(c, carry):
            grad = jnp.dot(pair_window(ds, 0, 28 * c, 14), wback[...], preferred_element_type=f32)
            rows = split_pairs(grad, C)
            for t in range(28):
                ghid[s, 28 * c + t] = rows[t]
            return carry

        lax.fori_loop(0, 7, back, 0)
        fold_f[16:32, :] = ghid[s, 0]
        fold_f[64:80, :] = ghid[s, height + 1]
        corner_send[s, 0] = fold_f[0:48, :].astype(bf16)
        corner_send[s, 1] = fold_f[48:96, :].astype(bf16)
        send_outer(s)

        weight_sum(hs, s, ds, 2)
        return carry

    def weight_sum(ref, s, delta_ref, first):
        pairs = height // 2
        if first == 2:
            v = delta_ref[0, pl.ds(2, height), :, C : 2 * C]
        else:
            v = delta_ref[...]
        v = v.reshape(pairs, 2, 16, C)
        lhs = jnp.concatenate([v[:, e].reshape(pairs * 16, C) for e in range(2)], axis=1)
        for w in range(4):
            x = ref[s, pl.ds(0, height + 2)].reshape(pairs + 1, 2, 16, 3 * C)
            rhs = (x[:pairs, w] if w < 2 else x[1:, w - 2]).reshape(pairs * 16, 3 * C)
            acc[:, w * 3 * C : (w + 1) * 3 * C] += lax.dot_general(
                lhs, rhs, (((0,), (0,)), ((), ())), preferred_element_type=f32
            )

    lax.fori_loop(0, batch, stage_two, 0)

    share = 9 * C // peers
    block = share + 16

    def sum_start(g):
        for i in range(9):
            at = i * C
            value = (acc[0:C, at : at + C] + acc[C : 2 * C, at + 3 * C : at + 4 * C]).T.astype(bf16)
            for u in range(C // 16):
                row = at + 16 * u
                grad_send[g, row // share, row % share : row % share + 16, :] = value[
                    16 * u : 16 * u + 16
                ]
        bias = jnp.broadcast_to(
            jnp.sum(bias_acc[g], axis=0, keepdims=True), (16, C)
        ).astype(bf16)
        for d in range(peers):
            grad_send[g, d, share:block, :] = bias
        for step in range(1, peers):
            to = (plane + step) % peers
            remote(
                grad_send.at[g, to], grad_recv.at[g, pl.ds(plane * block, block)],
                gsend_sem.at[g, 0], grecv_sem.at[g, 0], 4 * n + to // tm_count, to % tm_count,
            )
        grad_recv[g, pl.ds(plane * block, block), :] = grad_send[g, plane]

    def sum_plane(g):
        finish(grad_recv.at[g], (peers - 1) * block, grecv_sem.at[g, 0])
        total = grad_recv[g, 0:block, :].astype(f32)
        for d in range(1, peers):
            total = total + grad_recv[g, d * block : (d + 1) * block, :].astype(f32)
        plane_send[g] = total.astype(bf16)
        for step in range(1, 4):
            remote(
                plane_send.at[g], plane_recv.at[g, pl.ds(n * block, block)],
                gsend_sem.at[g, 1], grecv_sem.at[g, 1], wrap(me + 4 * step),
            )
        plane_recv[g, pl.ds(n * block, block), :] = total.astype(bf16)

    def sum_copies(g, bias_out):
        finish(plane_recv.at[g], 3 * block, grecv_sem.at[g, 1])
        total = plane_recv[g, 0:block, :].astype(f32)
        for d in range(1, 4):
            total = total + plane_recv[g, d * block : (d + 1) * block, :].astype(f32)
        pixel_count = 16 * height * pixels * batch * tm_count
        total = total * (1.0 / math.sqrt(pixel_count))
        bias_out[...] = total[share : share + 1]
        mine = total[0:share].astype(bf16)
        part_send[g] = mine
        for step in range(1, peers):
            to = (plane + step) % peers
            remote(
                part_send.at[g], part_recv.at[g, pl.ds(plane * share, share)],
                gsend_sem.at[g, 2], grecv_sem.at[g, 2], 4 * n + to // tm_count, to % tm_count,
            )
        part_recv[g, pl.ds(plane * share, share), :] = mine

    def sum_end(g, weight_out):
        finish(part_recv.at[g], (peers - 1) * share, grecv_sem.at[g, 2])
        weight_out[...] = part_recv[g].astype(f32)
        finish(grad_recv.at[g], (peers - 1) * block, gsend_sem.at[g, 0])
        finish(plane_recv.at[g], 3 * block, gsend_sem.at[g, 1])
        finish(part_recv.at[g], (peers - 1) * share, gsend_sem.at[g, 2])

    sum_start(1)
    acc[...] = jnp.zeros_like(acc)

    def stage_three(s, carry):
        @pl.when((j == 0) | (j == 3))
        def _():
            finish(all_rows, 560, orecv_sem.at[s])

        @pl.when((j != 0) & (j != 3))
        def _():
            finish(all_rows, 416, orecv_sem.at[s])

        extra = 2 * height + 32
        left_at, right_at = 16, 240

        @pl.when(j != 0)
        def _():
            fold_f[left_at : left_at + height, :] = outer_recv[s, 0:height, :].astype(f32)

        @pl.when(j == 0)
        def _():
            fold_f[left_at - 16 : left_at + 64, :] = jnp.zeros((80, C), f32)
            fold_f[left_at + 64 : left_at + height, :] = outer_recv[s, 64:height, :].astype(f32)
            for jj in range(4):
                at = left_at - 16 + 16 * jj
                fold_f[at : at + 48, :] += outer_recv[
                    s, extra + 48 * jj : extra + 48 * jj + 48, :
                ].astype(f32)
            corner = outer_recv[s, extra + 192 : extra + 208, :].astype(f32)
            fold_f[left_at : left_at + 1, :] += corner[15:16]

        @pl.when(j != 3)
        def _():
            fold_f[right_at : right_at + height, :] = outer_recv[s, height : 2 * height, :].astype(
                f32
            )

        @pl.when(j == 3)
        def _():
            fold_f[right_at : right_at + height - 64, :] = outer_recv[
                s, height : 2 * height - 64, :
            ].astype(f32)
            fold_f[right_at + height - 64 : right_at + height + 16, :] = jnp.zeros((80, C), f32)
            for jj in range(4):
                at = right_at + 112 + 16 * jj
                fold_f[at : at + 48, :] += outer_recv[
                    s, extra + 48 * jj : extra + 48 * jj + 48, :
                ].astype(f32)
            corner = outer_recv[s, extra + 192 : extra + 208, :].astype(f32)
            last = right_at + height - 1
            fold_f[last : last + 1, :] += corner[0:1]

        ghid[s, 1] += outer_recv[s, 2 * height : 2 * height + 16, :].astype(f32)
        ghid[s, height] += outer_recv[s, 2 * height + 16 : 2 * height + 32, :].astype(f32)

        def scale(k, carry):
            total = jnp.zeros((pixels, C), f32)
            half = lax.broadcasted_iota(jnp.int32, (8, C), 0)
            for t in range(16):
                if t % 8 == 0:
                    left = fold_f[pl.ds(left_at + 16 * k + t, 8), :]
                    right = fold_f[pl.ds(right_at + 16 * k + t, 8), :]
                at = t % 8
                value = ghid[s, 1 + 16 * k + t]
                low = value[:8] + jnp.where(half == 0, turned_by(left, -at), 0.0)
                high = value[8:] + jnp.where(half == 7, turned_by(right, 7 - at), 0.0)
                delta = jnp.concatenate([low, high], axis=0) * slope[s, 16 * k + t]
                d1[16 * k + t] = delta.astype(bf16)
                total = total + delta
            bias_acc[0] += total
            return carry

        lax.fori_loop(0, tiles, scale, 0)
        weight_sum(xs, s, d1, 0)

        @pl.when(s == 0)
        def _():
            sum_plane(1)

        @pl.when(s == min(1, batch - 1))
        def _():
            sum_copies(1, gb2_ref)

        return carry

    lax.fori_loop(0, batch, stage_three, 0)
    sum_start(0)
    sum_end(1, gw2_ref)

    for s in range(batch):
        dma_out(s).wait()

        @pl.when((j == 0) | (j == 3))
        def _():
            finish(all_rows, 544, send_sem.at[1, s])
            finish(all_rows, 496, osend_sem.at[s])

        @pl.when((j != 0) & (j != 3))
        def _():
            finish(all_rows, 416, send_sem.at[1, s])
            finish(all_rows, 480, osend_sem.at[s])

    sum_plane(0)
    sum_copies(0, gb1_ref)
    sum_end(0, gw1_ref)


def strip_body(features, weight_one, bias_one, weight_two, bias_two, cotangent):
    tm_count = lax.axis_size("tm")
    tiles, batch, pixels, _, C = features.shape
    height = tiles * pixels
    bf16, f32 = jnp.bfloat16, jnp.float32
    peers = 4 * tm_count
    share = 9 * C // peers
    block = share + 16
    vmem = pl.BlockSpec(memory_space=pltpu.VMEM)
    hbm = pl.BlockSpec(memory_space=pl.ANY)
    dma = pltpu.SemaphoreType.DMA
    flops = 10 * tiles * batch * pixels * pixels * 9 * C * C
    output, gw1, gb1, gw2, gb2 = pl.pallas_call(
        functools.partial(strip_kernel, tm_count),
        in_specs=[hbm, hbm, vmem, vmem, vmem, vmem],
        out_specs=[hbm, vmem, vmem, vmem, vmem],
        out_shape=[
            jax.ShapeDtypeStruct(features.shape, bf16),
            jax.ShapeDtypeStruct((9 * C, C), f32), jax.ShapeDtypeStruct((1, C), f32),
            jax.ShapeDtypeStruct((9 * C, C), f32), jax.ShapeDtypeStruct((1, C), f32),
        ],
        scratch_shapes=[
            pltpu.VMEM(features.shape, bf16),
            pltpu.VMEM((batch, height + 2, pixels, 3 * C), bf16),
            pltpu.VMEM((batch, height + 2, pixels, 3 * C), bf16),
            pltpu.VMEM((1, height + 6, pixels, 3 * C), bf16),
            pltpu.VMEM((height, pixels, C), bf16),
            pltpu.VMEM((batch, height, pixels, C), f32),
            pltpu.VMEM((batch, height + 4, pixels, C), f32),
            pltpu.VMEM((12 * C, 2 * C), bf16),
            pltpu.VMEM((12 * C, 2 * C), bf16),
            pltpu.VMEM((12 * C, 2 * C), bf16),
            pltpu.VMEM((2, 3 * C, C), bf16),
            pltpu.VMEM((2 * C, 12 * C), f32),
            pltpu.VMEM((2, pixels, C), f32),
            pltpu.VMEM((528, C), f32),
            pltpu.VMEM((464, C), f32),
            pltpu.VMEM((2, batch, 2, height + 16, C), bf16),
            pltpu.VMEM((2, batch, 2 * height + 96, C), bf16),
            pltpu.VMEM((batch, 2, height + 32, C), bf16),
            pltpu.VMEM((batch, 2, 48, C), bf16),
            pltpu.VMEM((batch, 2 * height + 240, C), bf16),
            pltpu.VMEM((2, peers, block, C), bf16),
            pltpu.VMEM((2, peers * block, C), bf16),
            pltpu.VMEM((2, 4 * block, C), bf16),
            pltpu.VMEM((2, block, C), bf16),
            pltpu.VMEM((2, share, C), bf16),
            pltpu.VMEM((2, 9 * C, C), bf16),
            dma((batch,)), dma((batch,)), dma((batch,)),
            dma((2, batch)), dma((2, batch)), dma((batch,)), dma((batch,)), dma((2, 3)), dma((2, 3)),
        ],
        compiler_params=pltpu.CompilerParams(
            collective_id=0, has_side_effects=True, vmem_limit_bytes=60 * 1024 * 1024
        ),
        cost_estimate=pl.CostEstimate(
            flops=flops, bytes_accessed=6 * features.size, transcendentals=4 * features.size
        ),
    )(
        features, cotangent, weight_one, bias_one.reshape(1, C), weight_two,
        bias_two.reshape(1, C),
    )
    shape = weight_one.shape
    return (output, gw1.reshape(shape), gb1.reshape(C), gw2.reshape(shape), gb2.reshape(C))


def whole_columns(mesh, tiles):
    columns, samples = mesh.shape["tile"], mesh.shape["tm"]
    return columns == 4 * S and tiles == 3 * S * columns and samples in (1, 2)


def solution(mesh):
    def call(*arrays):
        if whole_columns(mesh, arrays[0].shape[0]):
            chosen = strip_body
        else:
            chosen = body
        return jax.shard_map(
            chosen,
            mesh=mesh,
            in_specs=(
                P("tile", "tm", None, None, None),
                P(),
                P(),
                P(),
                P(),
                P("tile", "tm", None, None, None),
            ),
            out_specs=(P("tile", "tm", None, None, None), P(), P(), P(), P()),
            check_vma=False,
        )(*arrays)

    return call
```

```python
import functools
import math

import jax
import jax.numpy as jnp
import numpy as np
from jax import lax
from jax.experimental import pallas as pl
from jax.experimental.pallas import tpu as pltpu
from jax.sharding import PartitionSpec as P

S = 4


inv_sqrt_two = 0.7071067811865476
inv_sqrt_tau = 0.3989422804014327
LOG2_E = 1.4426950408889634
MESH = pl.DeviceIdType.MESH


def passed_along(value, axis, steps):
    count = lax.axis_size(axis)
    pairs = [(source, (source + steps) % count) for source in range(count)]
    return lax.ppermute(value, axis, pairs)


def edge_partner(face_id, edge_id):
    group_id = face_id // 4
    within = face_id % 4
    after_id = (within + 1) % 4
    before = (within + 3) % 4
    if group_id == 0:
        options = [(after_id, 2), (4 + within, 0), (before, 0), (4 + after_id, 2)]
    elif group_id == 1:
        options = [(within, 1), (8 + before, 0), (before, 3), (8 + within, 2)]
    else:
        options = [(4 + after_id, 1), (8 + before, 3), (4 + within, 3), (8 + after_id, 1)]
    return options[edge_id]


def entry_pixel(edge_id, along_edge, length):
    if edge_id == 0:
        return (0, along_edge)
    if edge_id == 1:
        return (length - 1, along_edge)
    if edge_id == 2:
        return (along_edge, 0)
    return (along_edge, length - 1)


def step_pixel(face_id, row_at, col_at, row_step, col_step, length):
    row_new = row_at + row_step
    col_new = col_at + col_step
    if 0 <= row_new < length and 0 <= col_new < length:
        return (face_id, row_new, col_new, -1)
    if row_new < 0:
        edge_id = 0
    elif row_new >= length:
        edge_id = 1
    elif col_new < 0:
        edge_id = 2
    else:
        edge_id = 3
    along_edge = col_at if edge_id < 2 else row_at
    partner, entered = edge_partner(face_id, edge_id)
    row_in, col_in = entry_pixel(entered, along_edge, length)
    return (partner, row_in, col_in, entered)


def neighbour_pixel(face_id, row_at, col_at, row_step, col_step, length):
    if row_step == 0 or col_step == 0:
        found = step_pixel(face_id, row_at, col_at, row_step, col_step, length)
        return (found[0], found[1], found[2])
    face_one, row_one, col_one, entered = step_pixel(face_id, row_at, col_at, row_step, 0, length)
    if entered >= 2:
        found = step_pixel(face_one, row_one, col_one, col_step, 0, length)
    else:
        found = step_pixel(face_one, row_one, col_one, 0, col_step, length)
    return (found[0], found[1], found[2])


def tile_slot(face_id, tile_row, tile_col, side_tiles):
    group_id = face_id // 4
    within = face_id % 4
    extra = 1 if group_id == 2 else 0
    column = (side_tiles * (within + extra) + tile_col) % (4 * side_tiles)
    return 3 * side_tiles * column + side_tiles * group_id + tile_row


def cycle_position(row_at, col_at, pixels):
    if row_at == 0:
        return col_at
    if row_at == pixels - 1:
        return pixels + col_at
    if col_at == 0:
        return 2 * pixels + row_at
    return 3 * pixels + row_at


def halo_positions(pixels):
    places = [(-1, column) for column in range(-1, pixels + 1)]
    places = places + [(pixels, column) for column in range(-1, pixels + 1)]
    places = places + [(row_at, -1) for row_at in range(pixels)]
    places = places + [(row_at, pixels) for row_at in range(pixels)]
    return places


def halo_sources(side_tiles, pixels):
    slot_count = 12 * side_tiles * side_tiles
    places = halo_positions(pixels)
    length = side_tiles * pixels
    source_slot = np.zeros((slot_count, len(places)), np.int64)
    source_cycle = np.zeros((slot_count, len(places)), np.int64)
    for face_id in range(12):
        for tile_row in range(side_tiles):
            for tile_col in range(side_tiles):
                slot_id = tile_slot(face_id, tile_row, tile_col, side_tiles)
                for cell_index in range(len(places)):
                    row_at, col_at = places[cell_index]
                    inner_row = min(max(row_at, 0), pixels - 1)
                    inner_col = min(max(col_at, 0), pixels - 1)
                    partner, row_new, col_new = neighbour_pixel(
                        face_id,
                        tile_row * pixels + inner_row,
                        tile_col * pixels + inner_col,
                        row_at - inner_row,
                        col_at - inner_col,
                        length,
                    )
                    source_slot[slot_id, cell_index] = tile_slot(
                        partner, row_new // pixels, col_new // pixels, side_tiles
                    )
                    source_cycle[slot_id, cell_index] = cycle_position(
                        row_new % pixels, col_new % pixels, pixels
                    )
    return (source_slot, source_cycle)


def halo_rows(row_at, col_at, pixels):
    if row_at == -1 or row_at == pixels:
        base = 0 if row_at == -1 else 3 * pixels
        return [
            base + pixels * shift + col_at + 1 - shift
            for shift in range(3)
            if 0 <= col_at + 1 - shift < pixels
        ]
    return [6 * pixels + row_at if col_at == -1 else 7 * pixels + row_at]


def outer_row(row_at, col_at, pixels):
    if col_at == -1:
        return 2 * pixels + row_at + 1
    if col_at == pixels:
        return 4 * pixels + row_at + 1
    return col_at if row_at == -1 else pixels + col_at


def device_tables(device_count, per_device, side_tiles, pixels):
    source_slot, source_cycle = halo_sources(side_tiles, pixels)
    places = halo_positions(pixels)
    rim_len, halo_len, outer_len = 4 * pixels, 8 * pixels, 6 * pixels
    sends = {}
    local = []
    for device in range(device_count):
        local.append([])
        for local_id in range(per_device):
            slot_id = device * per_device + local_id
            for cell in range(len(places)):
                row_at, col_at = places[cell]
                source = int(source_slot[slot_id, cell])
                moved_by = (device - source // per_device) % device_count
                if moved_by > device_count // 2:
                    moved_by -= device_count
                rim = source % per_device * rim_len + int(source_cycle[slot_id, cell])
                halo = [local_id * halo_len + h for h in halo_rows(row_at, col_at, pixels)]
                outer = local_id * outer_len + outer_row(row_at, col_at, pixels)
                record = (rim, halo, outer)
                if moved_by == 0:
                    local[device].append(record)
                else:
                    lists = sends.setdefault(moved_by, [[] for _ in range(device_count)])
                    lists[device].append(record)
    offsets = sorted(sends)
    widths = [-(-max(len(one) for one in sends[offset]) // 16) * 16 for offset in offsets]
    total = sum(widths)
    send = np.full((device_count, total), -1, np.int32)
    receive = np.full((device_count, per_device * halo_len), -1, np.int32)
    back = np.full((device_count, total), -1, np.int32)
    target = np.full((device_count, per_device * outer_len + total), -1, np.int32)
    for device in range(device_count):
        for rim, halo, outer in local[device]:
            receive[device, halo] = rim
            target[device, outer] = rim
        base = 0
        for offset, width in zip(offsets, widths):
            sender = (device - offset) % device_count
            for at, (rim, halo, outer) in enumerate(sends[offset][device]):
                send[sender, base + at] = rim
                receive[device, halo] = per_device * rim_len + base + at
                back[device, base + at] = outer
                target[sender, per_device * outer_len + base + at] = rim
            base += width
    return (offsets, widths, send, receive, back, target)


def one_hot(table_np, tile_index, width):
    row = jnp.asarray(table_np, dtype=jnp.int32)[tile_index]
    return (row[:, None] == lax.broadcasted_iota(jnp.int32, (row.shape[0], width), 1)).astype(
        jnp.bfloat16
    )


def exchanged(rows, offsets, widths, sign):
    pieces, base = [], 0
    for offset, width in zip(offsets, widths):
        pieces.append(passed_along(rows[base : base + width], "tile", sign * offset))
        base += width
    return pieces


def halo_of(rim, layout, tile_index):
    offsets, widths, send, receive = layout[:4]
    outgoing = jnp.dot(one_hot(send, tile_index, rim.shape[0]), rim)
    pool = jnp.concatenate([rim] + exchanged(outgoing, offsets, widths, 1), axis=0)
    return jnp.dot(one_hot(receive, tile_index, pool.shape[0]), pool)


def folded(outer, layout, tile_index, rim_rows):
    offsets, widths, _, _, back, target = layout
    outgoing = jnp.dot(one_hot(back, tile_index, outer.shape[0]), outer)
    pool = jnp.concatenate([outer] + exchanged(outgoing, offsets, widths, -1), axis=0)
    spread = one_hot(target, tile_index, rim_rows)
    return lax.dot_general(
        spread, pool, (((0,), (0,)), ((), ())), preferred_element_type=jnp.float32
    )


def gelu_parts(value):
    half = 0.5 * (1.0 + lax.erf(value * inv_sqrt_two))
    return value * half, half + value * jnp.exp(-0.5 * value * value) * inv_sqrt_tau


def columns_at(tile, halo, work, pixels):
    count = pixels * pixels
    wide = tile.astype(jnp.float32)
    halo_wide = halo[6 * pixels :].astype(jnp.float32)
    work[0, pl.ds(1, count - 1), :] = wide[: count - 1]
    work[0, pl.ds(0, pixels, stride=pixels), :] = halo_wide[:pixels]
    work[1, pl.ds(0, count - 1), :] = wide[1:]
    work[1, pl.ds(pixels - 1, pixels, stride=pixels), :] = halo_wide[pixels:]
    middles = [work[0].astype(jnp.bfloat16), tile, work[1].astype(jnp.bfloat16)]
    joined = jnp.concatenate(
        [
            jnp.concatenate(
                [
                    halo[pixels * b : pixels * (b + 1)],
                    middles[b],
                    halo[pixels * (3 + b) : pixels * (4 + b)],
                ],
                axis=0,
            )
            for b in range(3)
        ],
        axis=1,
    )
    return jnp.concatenate([joined[pixels * a : pixels * a + count] for a in range(3)], axis=1)


def first_kernel(x_ref, halo_ref, w_ref, bias_ref, hidden_ref, slope_ref, rim_ref, work):
    batch, pixels, channels = x_ref.shape[1], x_ref.shape[2], x_ref.shape[4]
    count = pixels * pixels
    for s in range(batch):
        lanes = slice(s * channels, (s + 1) * channels)
        tile = x_ref[0, s].reshape(count, channels)
        cols = columns_at(tile, halo_ref[0, :, lanes], work.at[pl.ds(2 * s, 2)], pixels)
        pre = jnp.dot(cols, w_ref[...], preferred_element_type=jnp.float32) + bias_ref[...]
        hidden, slope = gelu_parts(pre)
        slope_ref[0, s] = slope
        work[2 * batch + s] = hidden
        rounded = hidden.astype(jnp.bfloat16)
        hidden_ref[0, s] = rounded.reshape(pixels, pixels, channels)
        rim_ref[0, 0:pixels, lanes] = rounded[:pixels]
        rim_ref[0, pixels : 2 * pixels, lanes] = rounded[count - pixels :]
        for side in range(2):
            edge = work[2 * batch + s, pl.ds(side * (pixels - 1), pixels, stride=pixels), :]
            rim_ref[0, (2 + side) * pixels : (3 + side) * pixels, lanes] = edge.astype(jnp.bfloat16)


def second_kernel(
    x_ref, halo_ref, cot_ref, w_ref, flip_ref, side_ref, bias_ref,
    out_ref, inner_ref, outer_ref, grad_ref, sum_ref, work, cols_ref, delta_ref, edge_ref,
):
    batch, pixels, channels = x_ref.shape[1], x_ref.shape[2], x_ref.shape[4]
    count = pixels * pixels

    @pl.when(pl.program_id(0) == 0)
    def _():
        grad_ref[...] = jnp.zeros_like(grad_ref)
        sum_ref[...] = jnp.zeros_like(sum_ref)

    zero_row = jnp.zeros((1, channels), jnp.float32)
    zero_col = jnp.zeros((pixels, channels), jnp.float32)
    zeros = jnp.zeros((2 * pixels, 3 * channels), jnp.bfloat16)
    for s in range(batch):
        lanes = slice(s * channels, (s + 1) * channels)
        tile = x_ref[0, s].reshape(count, channels)
        here = work.at[pl.ds(2 * s, 2)]
        cols = columns_at(tile, halo_ref[0, :, lanes], here, pixels)
        cols_ref[s * count : (s + 1) * count, :] = cols
        pre = jnp.dot(cols, w_ref[...], preferred_element_type=jnp.float32) + bias_ref[...]
        value, slope = gelu_parts(pre)
        out_ref[0, s] = value.astype(jnp.bfloat16).reshape(pixels, pixels, channels)
        cot = cot_ref[0, s].reshape(count, channels).astype(jnp.float32)
        delta = (cot * slope).astype(jnp.bfloat16)
        delta_ref[s * count : (s + 1) * count, :] = delta
        wide = delta.astype(jnp.float32)
        sum_ref[...] += jnp.sum(wide, axis=0, keepdims=True)
        edge_ref[s] = jnp.zeros(edge_ref.shape[1:], jnp.float32)
        work[2 * batch + s] = wide
        for side in range(2):
            edge_ref[s, side, pl.ds(2, pixels), :] = work[
                2 * batch + s, pl.ds(side * (pixels - 1), pixels, stride=pixels), :
            ]
        here[0, pl.ds(0, count - 1), :] = wide[1:]
        here[0, pl.ds(pixels - 1, pixels, stride=pixels), :] = zero_col
        here[1, pl.ds(1, count - 1), :] = wide[: count - 1]
        here[1, pl.ds(0, pixels, stride=pixels), :] = zero_col
        joined = jnp.concatenate(
            [here[0].astype(jnp.bfloat16), delta, here[1].astype(jnp.bfloat16)], axis=1
        )
        joined = jnp.concatenate([zeros, joined, zeros], axis=0)
        tall = count + 2 * pixels
        spread = jnp.concatenate(
            [joined[pixels * (2 - a) : pixels * (2 - a) + tall] for a in range(3)], axis=1
        )
        grad = jnp.dot(spread, flip_ref[...], preferred_element_type=jnp.float32)
        inner_ref[0, s] = grad[pixels : pixels + count]
        outer_ref[0, 0:pixels, lanes] = grad[:pixels].astype(jnp.bfloat16)
        outer_ref[0, pixels : 2 * pixels, lanes] = grad[pixels + count :].astype(jnp.bfloat16)
        for side in range(2):
            lhs = jnp.concatenate(
                [edge_ref[s, side, pl.ds(2 - a, 2 * pixels), :] for a in range(3)], axis=1
            ).astype(jnp.bfloat16)
            part = jnp.dot(lhs, side_ref[side], preferred_element_type=jnp.float32)
            outer_ref[0, 2 * pixels * (1 + side) : 2 * pixels * (2 + side), lanes] = part.astype(
                jnp.bfloat16
            )
    grad_ref[...] += lax.dot_general(
        delta_ref[...], cols_ref[...], (((0,), (0,)), ((), ())), preferred_element_type=jnp.float32
    )


def third_kernel(
    x_ref, halo_ref, inner_ref, rim_ref, slope_ref, grad_ref, sum_ref, work, cols_ref, delta_ref
):
    batch, pixels, channels = x_ref.shape[1], x_ref.shape[2], x_ref.shape[4]
    count = pixels * pixels

    @pl.when(pl.program_id(0) == 0)
    def _():
        grad_ref[...] = jnp.zeros_like(grad_ref)
        sum_ref[...] = jnp.zeros_like(sum_ref)

    for s in range(batch):
        lanes = slice(s * channels, (s + 1) * channels)
        tile = x_ref[0, s].reshape(count, channels)
        cols_ref[s * count : (s + 1) * count, :] = columns_at(
            tile, halo_ref[0, :, lanes], work.at[pl.ds(2 * s, 2)], pixels
        )
        at = 2 * batch + s
        work[at] = inner_ref[0, s]
        work[at, pl.ds(0, pixels), :] += rim_ref[0, 0:pixels, lanes]
        work[at, pl.ds(count - pixels, pixels), :] += rim_ref[0, pixels : 2 * pixels, lanes]
        for side in range(2):
            place = pl.ds(side * (pixels - 1), pixels, stride=pixels)
            edge = rim_ref[0, (2 + side) * pixels : (3 + side) * pixels, lanes]
            work[at, place, :] = work[at, place, :] + edge
        delta = (work[at] * slope_ref[0, s]).astype(jnp.bfloat16)
        delta_ref[s * count : (s + 1) * count, :] = delta
        sum_ref[...] += jnp.sum(delta.astype(jnp.float32), axis=0, keepdims=True)
    grad_ref[...] += lax.dot_general(
        delta_ref[...], cols_ref[...], (((0,), (0,)), ((), ())), preferred_element_type=jnp.float32
    )


def per_tile(shape):
    return pl.BlockSpec((1,) + tuple(shape), lambda t: (t,) + (0,) * len(shape))


def whole(shape):
    return pl.BlockSpec(tuple(shape), lambda t: (0,) * len(shape))


params = dict(vmem_limit_bytes=48 * 1024 * 1024)


def body(features, weight_one, bias_one, weight_two, bias_two, cotangent):
    device_count = lax.axis_size("tile")
    samples_count = lax.axis_size("tm")
    tile_index = lax.axis_index("tile")
    per_device, batch, pixels, _, channels = features.shape
    count = pixels * pixels
    lane_count = batch * channels
    layout = device_tables(device_count, per_device, S, pixels)
    bf16, f32 = jnp.bfloat16, jnp.float32
    tile_shape = (batch, pixels, pixels, channels)
    flat_shape = (batch, count, channels)
    halo_shape = (8 * pixels, lane_count)
    rim_shape = (4 * pixels, lane_count)
    outer_shape = (6 * pixels, lane_count)
    mat_one = weight_one.reshape(9 * channels, channels)
    mat_two = weight_two.reshape(9 * channels, channels)
    turned = weight_two.transpose(0, 1, 3, 2)
    flip = turned.reshape(9 * channels, channels)
    sides = jnp.stack([turned[:, 0], turned[:, 2]]).reshape(2, 3 * channels, channels)

    def out(shape, dtype):
        return jax.ShapeDtypeStruct((per_device,) + tuple(shape), dtype)

    work = pltpu.VMEM((3 * batch, count, channels), f32)
    cols = pltpu.VMEM((batch * count, 9 * channels), bf16)
    deltas = pltpu.VMEM((batch * count, channels), bf16)
    grad_shape = (channels, 9 * channels)

    rim_one = jnp.concatenate(
        [features[:, :, 0], features[:, :, -1], features[:, :, :, 0], features[:, :, :, -1]], axis=2
    )
    rim_one = rim_one.transpose(0, 2, 1, 3).reshape(per_device * 4 * pixels, lane_count)
    halo_one = halo_of(rim_one, layout, tile_index).reshape((per_device,) + halo_shape)
    hidden, slope, rim_two = pl.pallas_call(
        first_kernel,
        grid=(per_device,),
        in_specs=[per_tile(tile_shape), per_tile(halo_shape), whole(mat_one.shape), whole((1, channels))],
        out_specs=[per_tile(tile_shape), per_tile(flat_shape), per_tile(rim_shape)],
        out_shape=[out(tile_shape, bf16), out(flat_shape, f32), out(rim_shape, bf16)],
        scratch_shapes=[work],
        compiler_params=pltpu.CompilerParams(**params),
    )(features, halo_one, mat_one, bias_one.reshape(1, channels))
    halo_two = halo_of(rim_two.reshape(-1, lane_count), layout, tile_index)
    output, inner, outer, grad_two, sum_two = pl.pallas_call(
        second_kernel,
        grid=(per_device,),
        in_specs=[
            per_tile(tile_shape), per_tile(halo_shape), per_tile(tile_shape), whole(mat_two.shape),
            whole(flip.shape), whole(sides.shape), whole((1, channels)),
        ],
        out_specs=[
            per_tile(tile_shape), per_tile(flat_shape), per_tile(outer_shape),
            whole(grad_shape), whole((1, channels)),
        ],
        out_shape=[
            out(tile_shape, bf16), out(flat_shape, f32), out(outer_shape, bf16),
            jax.ShapeDtypeStruct(grad_shape, f32), jax.ShapeDtypeStruct((1, channels), f32),
        ],
        scratch_shapes=[work, cols, deltas, pltpu.VMEM((batch, 2, 2 * pixels + 8, channels), f32)],
        compiler_params=pltpu.CompilerParams(**params),
    )(
        hidden, halo_two.reshape((per_device,) + halo_shape), cotangent, mat_two, flip, sides,
        bias_two.reshape(1, channels),
    )
    rim_grad = folded(outer.reshape(-1, lane_count), layout, tile_index, per_device * 4 * pixels)
    grad_one, sum_one = pl.pallas_call(
        third_kernel,
        grid=(per_device,),
        in_specs=[
            per_tile(tile_shape), per_tile(halo_shape), per_tile(flat_shape), per_tile(rim_shape),
            per_tile(flat_shape),
        ],
        out_specs=[whole(grad_shape), whole((1, channels))],
        out_shape=[jax.ShapeDtypeStruct(grad_shape, f32), jax.ShapeDtypeStruct((1, channels), f32)],
        scratch_shapes=[work, cols, deltas],
        compiler_params=pltpu.CompilerParams(**params),
    )(features, halo_one, inner, rim_grad.reshape((per_device,) + rim_shape), slope)

    total_pixels = 12 * S * S * count * batch * samples_count
    grad_scale = 1.0 / math.sqrt(total_pixels)
    devices = device_count * samples_count
    axes = ("tile", "tm")

    def summed(grad, bias):
        rows = jnp.concatenate([grad.reshape(-1, channels), bias], axis=0)
        used = rows.shape[0]
        chunk = -(-used // (8 * devices)) * 8
        rows = jnp.pad(rows, ((0, chunk * devices - used), (0, 0)))
        parts = lax.all_to_all(rows.reshape(devices, chunk, channels), axes, 0, 0)
        mine = (jnp.sum(parts, axis=0) * grad_scale).astype(bf16)
        copies = jnp.broadcast_to(mine[None], (devices, chunk, channels))
        total = lax.all_to_all(copies, axes, 0, 0).reshape(devices * chunk, channels).astype(f32)
        weight = total[: used - 1].reshape(channels, 3, 3, channels).transpose(1, 2, 3, 0)
        return weight, total[used - 1]

    grad_weight_two, grad_bias_two = summed(grad_two, sum_two)
    grad_weight_one, grad_bias_one = summed(grad_one, sum_one)
    return (output, grad_weight_one, grad_bias_one, grad_weight_two, grad_bias_two)


def cdf_parts(value):
    bell = jnp.exp2(value * value * (-0.5 * LOG2_E))
    t = 1.0 / (1.0 + (0.3275911 * inv_sqrt_two) * jnp.abs(value))
    poly = 0.5 * 1.061405429
    for coefficient in (-1.453152027, 1.421413741, -0.284496736, 0.254829592):
        poly = poly * t + 0.5 * coefficient
    tail = poly * t * bell
    return jnp.where(value < 0.0, tail, 1.0 - tail), bell


def put_shifted(ref, sample, at, row, first, last, from_left, from_right):
    low, high = row[:8], row[8:]
    low_down, high_down = turned_by(low, 1), turned_by(high, 1)
    shifted = jnp.concatenate(
        [jnp.where(first, from_left, low_down), jnp.where(first, low_down, high_down)], axis=0
    )
    ref[sample, at, 0] = shifted.astype(jnp.bfloat16)
    low_up, high_up = turned_by(low, 7), turned_by(high, 7)
    shifted = jnp.concatenate(
        [jnp.where(last, high_up, low_up), jnp.where(last, from_right, high_up)], axis=0
    )
    ref[sample, at, 2] = shifted.astype(jnp.bfloat16)


def turned_by(value, steps):
    steps = steps % 8
    return value if steps == 0 else pltpu.roll(value, steps, 0)


class Edges:
    def __init__(self, half):
        self.half, self.lefts, self.rights = half, [], []

    def add(self, t, row):
        if t % 8 == 0:
            self.lefts.append(row[:8])
            self.rights.append(turned_by(row[8:], 1))
        else:
            here = self.half == t % 8
            self.lefts[-1] = jnp.where(here, turned_by(row[:8], t), self.lefts[-1])
            self.rights[-1] = jnp.where(here, turned_by(row[8:], t + 1), self.rights[-1])

    def columns(self):
        return jnp.concatenate(self.lefts, axis=0), jnp.concatenate(self.rights, axis=0)


def pair_window(ref, sample, start, pairs):
    lanes = ref.shape[4]
    v = ref[sample, pl.ds(start, 2 * pairs + 2)].reshape(pairs + 1, 2, 3, 16, lanes)
    parts = [v[:pairs, 0], v[:pairs, 1], v[1:, 0], v[1:, 1]]
    return jnp.concatenate(
        [p[:, b].reshape(pairs * 16, lanes) for p in parts for b in range(3)], axis=1
    )


def strip_kernel(
    tm_count,
    x_hbm, cot_hbm, w1_ref, b1_ref, w2_ref, b2_ref,
    out_hbm, gw1_ref, gb1_ref, gw2_ref, gb2_ref,
    field, xs, hs, ds, d1, turned, slope, ghid, pre_f, w1p, w2p, wback, wside, acc, bias_acc,
    edge_f, fold_f, edge_send, halo_recv, outer_send, corner_send, outer_recv,
    grad_send, grad_recv, plane_recv, plane_send, part_send, part_recv,
    in_sem, cot_sem, out_sem, send_sem, recv_sem, osend_sem, orecv_sem, gsend_sem, grecv_sem,
):
    f32, bf16 = jnp.float32, jnp.bfloat16
    tiles, batch, pixels, _, C = x_hbm.shape
    height = tiles * pixels
    columns = 16
    me = lax.axis_index("tile")
    other = lax.axis_index("tm")
    n, j = me // 4, me % 4
    peers = 4 * tm_count
    plane = j * tm_count + other

    def wrap(c):
        return (c + 2 * columns) % columns

    def dma_in(s):
        return pltpu.make_async_copy(x_hbm.at[:, s], field.at[:, s], in_sem.at[s])

    def dma_cot(s):
        return pltpu.make_async_copy(cot_hbm.at[:, s], field.at[:, s], cot_sem.at[s])

    def dma_out(s):
        return pltpu.make_async_copy(field.at[:, s], out_hbm.at[:, s], out_sem.at[s])

    def remote(src, dst, send, recv, device, side=None):
        pltpu.make_async_remote_copy(
            src_ref=src, dst_ref=dst, send_sem=send, recv_sem=recv,
            device_id=(device, other if side is None else side), device_id_type=MESH,
        ).start()

    def finish(ref, count, sem):
        view = ref.at[pl.ds(0, count)]
        pltpu.make_async_copy(view, view, sem).wait()

    for s in range(batch):
        dma_in(s).start()

    barrier = pltpu.get_barrier_semaphore()
    for offset in range(1, columns):
        pl.semaphore_signal(
            barrier, inc=1, device_id=(wrap(me + offset), other), device_id_type=MESH
        )
    for step in range(1, tm_count):
        for jj in range(4):
            pl.semaphore_signal(
                barrier, inc=1, device_id=(4 * n + jj, (other + step) % tm_count),
                device_id_type=MESH,
            )
    pl.semaphore_wait(barrier, columns - 1 + 4 * (tm_count - 1))

    def send_rim(f, s, field_ref, top, bottom):
        es, er = edge_send.at[f, s, 0], edge_send.at[f, s, 1]
        ss, rs = send_sem.at[f, s], recv_sem.at[f, s]
        land = halo_recv.at[f, s]

        def cut(ref, start, count):
            return ref.at[pl.ds(start, count)]

        @pl.when(j >= 1)
        def _():
            remote(cut(es, 16, height), cut(land, height, height), ss, rs, wrap(me - 1))

        @pl.when(j == 0)
        def _():
            remote(cut(es, 80, height - 64), cut(land, height, height - 64), ss, rs, wrap(me - 1))

        @pl.when(j <= 2)
        def _():
            remote(cut(er, 0, height), cut(land, 0, height), ss, rs, wrap(me + 1))

        @pl.when(j == 3)
        def _():
            remote(cut(er, 0, height - 64), cut(land, 64, height - 64), ss, rs, wrap(me + 1))

        remote(top, cut(land, 16 * j, 16), ss, rs, wrap(4 * n + 4))
        remote(bottom, cut(land, height + 128 + 16 * j, 16), ss, rs, wrap(4 * n - 1))
        upper, lower = 2 * height, 2 * height + 48

        @pl.when(j == 0)
        def _():
            remote(cut(es, 16, 32), cut(land, upper + 16, 32), ss, rs, wrap(me - 4))
            for jj in range(1, 4):
                remote(cut(es, 16 * jj, 48), cut(land, upper, 48), ss, rs, wrap(me - 4 + jj))
            remote(cut(es, 0, 16), cut(land, upper, 16), ss, rs, wrap(me + 8))

        @pl.when(j == 3)
        def _():
            for jj in range(3):
                remote(
                    cut(er, 112 + 16 * jj, 48), cut(land, lower, 48), ss, rs, wrap(me + 1 + jj)
                )
            remote(cut(er, height - 32, 32), cut(land, lower, 32), ss, rs, wrap(me + 4))
            remote(cut(er, height, 16), cut(land, lower + 32, 16), ss, rs, wrap(me + 8))

    half_iota = lax.broadcasted_iota(jnp.int32, (8, C), 0)
    first_pixel, last_pixel = half_iota == 0, half_iota == 7

    def put_edges(f, s, k, edges):
        left, right = edges.columns()
        edge_send[f, s, 0, pl.ds(16 + 16 * k, 16), :] = left.astype(bf16)
        edge_send[f, s, 1, pl.ds(16 * k, 16), :] = right.astype(bf16)

    def put_corners(f, s):
        row = edge_send[f, s, 0, 16:32, :].astype(f32)
        edge_send[f, s, 0, 0:16, :] = jnp.broadcast_to(row[0:1], (16, C)).astype(bf16)
        row = edge_send[f, s, 1, height - 16 : height, :].astype(f32)
        edge_send[f, s, 1, height : height + 16, :] = jnp.broadcast_to(row[15:16], (16, C)).astype(
            bf16
        )

    def put_halo_rows(f, s, ref):
        for side in range(2):
            edge_f[0:48, :] = halo_recv[f, s, pl.ds(2 * height + 48 * side, 48), :].astype(f32)
            for b in range(3):
                ref[s, side * (height + 1), b] = edge_f[
                    15 + b : 31 + b, :
                ].astype(bf16)

    def shift_tile(f, s, k, ref, row_of):
        left = halo_recv[f, s, pl.ds(16 * k, 16), :].astype(f32)
        right = halo_recv[f, s, pl.ds(height + 16 * k, 16), :].astype(f32)
        for t in range(16):
            group = 8 * (t // 8)
            put_shifted(
                ref, s, 1 + 16 * k + t, row_of(t), first_pixel, last_pixel,
                turned_by(left[group : group + 8], -t), turned_by(right[group : group + 8], 7 - t),
            )

    def features_out(s, carry):
        dma_in(s).wait()

        def step(k, carry):
            edges = Edges(half_iota)
            for t in range(16):
                edges.add(t, field[k, s, t].astype(f32))
            put_edges(0, s, k, edges)
            return carry

        lax.fori_loop(0, tiles, step, 0)
        put_corners(0, s)
        send_rim(0, s, field, field.at[0, s, 0], field.at[tiles - 1, s, pixels - 1])
        return carry

    lax.fori_loop(0, batch, features_out, 0)

    one, two = w1_ref[...].reshape(9 * C, C), w2_ref[...].reshape(9 * C, C)
    zeros = jnp.zeros((3 * C, C), bf16)
    for packed, flat in ((w1p, one), (w2p, two)):
        packed[0 : 9 * C, 0:C] = flat
        packed[9 * C : 12 * C, 0:C] = zeros
        packed[0 : 3 * C, C : 2 * C] = zeros
        packed[3 * C : 12 * C, C : 2 * C] = flat
    for e in range(2):
        gap = 3 * (1 - e)
        wback[(9 if e == 0 else 0) * C + 0 : (12 if e == 0 else 3) * C, e * C : (e + 1) * C] = zeros
    for a in range(3):
        for b in range(3):
            block = w2_ref[a, b].astype(f32).T.astype(bf16)
            for e in range(2):
                at = ((2 + e - a) * 3 + 2 - b) * C
                wback[at : at + C, e * C : (e + 1) * C] = block
            if b != 1:
                wside[b // 2, a * C : (a + 1) * C, :] = block

    bias_one = jnp.concatenate([b1_ref[...], b1_ref[...]], axis=1)
    bias_two = jnp.concatenate([b2_ref[...], b2_ref[...]], axis=1)
    bias_acc[...] = jnp.zeros_like(bias_acc)

    def stage_one(s, carry):
        finish(halo_recv.at[0, s], 2 * height + 96, recv_sem.at[0, s])
        put_halo_rows(0, s, xs)

        def build(k, carry):
            for t in range(16):
                xs[s, 1 + 16 * k + t, 1] = field[k, s, t]
            shift_tile(0, s, k, xs, lambda t: field[k, s, t].astype(f32))
            return carry

        lax.fori_loop(0, tiles, build, 0)

        def dot(c):
            pre_f[rows_of * c : rows_of * (c + 1), :] = jnp.dot(
                pair_window(xs, s, 2 * per_chunk * c, per_chunk), w1p[...],
                preferred_element_type=f32,
            )

        def after(k):
            edges = Edges(half_iota)
            for q in range(8):
                at = 128 * k + 16 * q
                pre = pre_f[at : at + 16, :] + bias_one
                half, bell = cdf_parts(pre)
                hidden = pre * half
                slopes = half + pre * (bell * inv_sqrt_tau)
                for e in range(2):
                    t = 2 * q + e
                    row = hidden[:, e * C : (e + 1) * C]
                    hs[s, 1 + 16 * k + t, 1] = row.astype(bf16)
                    slope[s, 16 * k + t] = slopes[:, e * C : (e + 1) * C]
                    edges.add(t, row)
            put_edges(1, s, k, edges)

        in_turn(dot, after)
        put_corners(1, s)
        top = hs.at[s, 1, 1]
        bottom = hs.at[s, height, 1]
        send_rim(1, s, hs, top, bottom)
        @pl.when((j == 0) | (j == 3))
        def _():
            finish(all_rows, 544, send_sem.at[0, s])

        @pl.when((j != 0) & (j != 3))
        def _():
            finish(all_rows, 416, send_sem.at[0, s])

        dma_cot(s).start()
        return carry

    all_rows = outer_recv.at[0]
    chunks = 3
    per_chunk = height // 2 // chunks
    rows_of = 16 * per_chunk

    def in_turn(dot, after):
        for c in range(chunks + 1):
            if c < chunks:
                dot(c)
            if c > 0:
                for k in range(tiles // chunks * (c - 1), tiles // chunks * c):
                    after(k)

    lax.fori_loop(0, batch, stage_one, 0)

    for at in (0, 1, height + 2, height + 3):
        ds[0, at] = jnp.zeros((3, pixels, C), bf16)
    for side in range(2):
        edge_f[48 + 240 * side : 48 + 240 * side + 24, :] = jnp.zeros((24, C), f32)
        edge_f[48 + 240 * side + 24 + height : 288 + 240 * side, :] = jnp.zeros(
            (216 - height, C), f32
        )

    def send_outer(s):
        ss, rs = osend_sem.at[s], orecv_sem.at[s]
        ol, orr = outer_send.at[s, 0], outer_send.at[s, 1]
        tb, bb = corner_send.at[s, 0], corner_send.at[s, 1]
        land = outer_recv.at[s]
        g_top, g_bottom, extra = 2 * height, 2 * height + 16, 2 * height + 32

        def cut(ref, start, count):
            return ref.at[pl.ds(start, count)]

        @pl.when(j >= 1)
        def _():
            remote(cut(ol, 16, height), cut(land, height, height), ss, rs, wrap(me - 1))

        @pl.when(j <= 2)
        def _():
            remote(cut(orr, 16, height), cut(land, 0, height), ss, rs, wrap(me + 1))

        @pl.when(j == 0)
        def _():
            remote(cut(ol, 80, height - 64), cut(land, height, height - 64), ss, rs, wrap(me - 1))
            for i in range(4):
                remote(cut(ol, 16 + 16 * i, 16), cut(land, g_top, 16), ss, rs, wrap(me - 4 + i))
            remote(cut(tb, 0, 16), cut(land, extra + 192, 16), ss, rs, wrap(me + 8))

        @pl.when(j == 3)
        def _():
            remote(cut(orr, 16, height - 64), cut(land, 64, height - 64), ss, rs, wrap(me + 1))
            for i in range(4):
                remote(
                    cut(orr, 144 + 16 * i, 16), cut(land, g_bottom, 16), ss, rs, wrap(me + 1 + i)
                )
            remote(cut(bb, 32, 16), cut(land, extra + 192, 16), ss, rs, wrap(me + 8))

        remote(tb, cut(land, extra + 48 * j, 48), ss, rs, wrap(4 * n + 4))
        remote(bb, cut(land, extra + 48 * j, 48), ss, rs, wrap(4 * n - 1))

    def stage_two(s, carry):
        finish(halo_recv.at[1, s], 2 * height + 96, recv_sem.at[1, s])
        put_halo_rows(1, s, hs)

        def build(k, carry):
            shift_tile(1, s, k, hs, lambda t: hs[s, 1 + 16 * k + t, 1].astype(f32))
            return carry

        lax.fori_loop(0, tiles, build, 0)
        dma_cot(s).wait()

        def dot(c):
            pre_f[rows_of * c : rows_of * (c + 1), :] = jnp.dot(
                pair_window(hs, s, 2 * per_chunk * c, per_chunk), w2p[...],
                preferred_element_type=f32,
            )

        zero = jnp.zeros((8, C), f32)

        def after(k):
            edges = Edges(half_iota)
            total = jnp.zeros((pixels, C), f32)
            for q in range(8):
                at = 128 * k + 16 * q
                pre = pre_f[at : at + 16, :] + bias_two
                half, bell = cdf_parts(pre)
                outs = pre * half
                slopes = half + pre * (bell * inv_sqrt_tau)
                for e in range(2):
                    t = 2 * q + e
                    delta = field[k, s, t].astype(f32) * slopes[:, e * C : (e + 1) * C]
                    field[k, s, t] = outs[:, e * C : (e + 1) * C].astype(bf16)
                    row = 2 + 16 * k + t
                    ds[0, row, 1] = delta.astype(bf16)
                    total = total + delta
                    put_shifted(ds, 0, row, delta, first_pixel, last_pixel, zero, zero)
                    edges.add(t, delta)
            left, right = edges.columns()
            edge_f[72 + 16 * k : 88 + 16 * k, :] = left
            edge_f[312 + 16 * k : 328 + 16 * k, :] = right
            bias_acc[1] += total

        in_turn(dot, after)
        dma_out(s).start()

        fold_f[0:96, :] = jnp.zeros((96, C), f32)
        for side in range(2):
            base = 48 + 240 * side
            lhs = jnp.concatenate(
                [edge_f[base + 9 - a : base + 233 - a, :] for a in range(3)], axis=1
            ).astype(bf16)
            cells = jnp.dot(lhs, wside[side], preferred_element_type=f32)
            outer_send[s, side] = cells.astype(bf16)
            fold_f[15 + 17 * side : 16 + 17 * side, :] = cells[15:16]
            fold_f[63 + 17 * side : 64 + 17 * side, :] = cells[16 + height : 17 + height]

        ghid[s] = jnp.dot(
            pair_window(ds, 0, 0, height // 2 + 1), wback[...], preferred_element_type=f32
        )
        fold_f[16:32, :] = ghid[s, 0:16, 0:C]
        fold_f[64:80, :] = ghid[s, 8 * height : 8 * height + 16, C : 2 * C]
        corner_send[s, 0] = fold_f[0:48, :].astype(bf16)
        corner_send[s, 1] = fold_f[48:96, :].astype(bf16)
        send_outer(s)

        turn_pairs(s, ds[0, 2 : 2 + height, 1])
        return carry

    def turn_pairs(s, value):
        v = value.reshape(height // 2, 2, pixels, C)
        turned[s] = jnp.concatenate(
            [v[:, e].reshape(8 * height, C) for e in range(2)], axis=1
        ).T

    def weight_sum(ref, window, samples):
        pairs = height // 2
        lanes = slice(window[0] * 3 * C, (window[-1] + 1) * 3 * C)
        if samples[0] == 0:
            acc[:, lanes] = jnp.zeros((2 * C, 3 * C * len(window)), f32)

        def step(s, carry):
            v = ref[s].reshape(pairs + 1, 2, 3, pixels, C)
            parts = []
            for w in window:
                x = v[:pairs, w] if w < 2 else v[1:, w - 2]
                parts += [x[:, b].reshape(pairs * pixels, C) for b in range(3)]
            acc[:, lanes] += jnp.dot(
                turned[s], jnp.concatenate(parts, axis=1), preferred_element_type=f32
            )
            return carry

        lax.fori_loop(samples[0], samples[1], step, 0)

    lax.fori_loop(0, batch, stage_two, 0)

    share = 3 * C // peers
    blocks = (share + 16, share, share)

    def sum_start(g, p):
        block = blocks[p]
        for b in range(3):
            at = (3 * p + b) * C
            value = (acc[0:C, at : at + C] + acc[C : 2 * C, at + 3 * C : at + 4 * C]).T.astype(bf16)
            for u in range(C // 16):
                row = b * C + 16 * u
                grad_send[g, p, row // share, row % share : row % share + 16, :] = value[
                    16 * u : 16 * u + 16
                ]
        if p == 0:
            bias = jnp.broadcast_to(
                jnp.sum(bias_acc[g], axis=0, keepdims=True), (16, C)
            ).astype(bf16)
            for d in range(peers):
                grad_send[g, p, d, share:block, :] = bias
        for step in range(1, peers):
            to = (plane + step) % peers
            remote(
                grad_send.at[g, p, to, pl.ds(0, block)],
                grad_recv.at[g, p, pl.ds(plane * block, block)],
                gsend_sem.at[g, p, 0], grecv_sem.at[g, p, 0],
                4 * n + to // tm_count, to % tm_count,
            )
        grad_recv[g, p, pl.ds(plane * block, block), :] = grad_send[g, p, plane, 0:block, :]

    def sum_plane(g, p):
        block = blocks[p]
        finish(grad_recv.at[g, p], (peers - 1) * block, grecv_sem.at[g, p, 0])
        total = grad_recv[g, p, 0:block, :].astype(f32)
        for d in range(1, peers):
            total = total + grad_recv[g, p, d * block : (d + 1) * block, :].astype(f32)
        plane_send[g, p, 0:block, :] = total.astype(bf16)
        for step in range(1, 4):
            remote(
                plane_send.at[g, p, pl.ds(0, block)],
                plane_recv.at[g, p, pl.ds(n * block, block)],
                gsend_sem.at[g, p, 1], grecv_sem.at[g, p, 1], wrap(me + 4 * step),
            )
        plane_recv[g, p, pl.ds(n * block, block), :] = total.astype(bf16)

    def sum_copies(g, p):
        block = blocks[p]
        finish(plane_recv.at[g, p], 3 * block, grecv_sem.at[g, p, 1])
        total = plane_recv[g, p, 0:block, :].astype(f32)
        for d in range(1, 4):
            total = total + plane_recv[g, p, d * block : (d + 1) * block, :].astype(f32)
        pixel_count = 16 * height * pixels * batch * tm_count
        total = total * (1.0 / math.sqrt(pixel_count))
        if p == 0:
            (gb1_ref, gb2_ref)[g][...] = total[share : share + 1]
        mine = total[0:share].astype(bf16)
        part_send[g, p] = mine
        for step in range(1, peers):
            to = (plane + step) % peers
            remote(
                part_send.at[g, p], part_recv.at[g, p, pl.ds(plane * share, share)],
                gsend_sem.at[g, p, 2], grecv_sem.at[g, p, 2],
                4 * n + to // tm_count, to % tm_count,
            )
        part_recv[g, p, pl.ds(plane * share, share), :] = mine

    def sum_end(g, p):
        finish(part_recv.at[g, p], (peers - 1) * share, grecv_sem.at[g, p, 2])
        (gw1_ref, gw2_ref)[g][3 * C * p : 3 * C * (p + 1), :] = part_recv[g, p].astype(f32)

    weight_sum(hs, (0, 1), (0, batch))
    sum_start(1, 0)
    weight_sum(hs, (2,), (0, batch))
    sum_start(1, 1)
    weight_sum(hs, (3,), (0, batch))
    sum_start(1, 2)

    def stage_three(s, carry):
        @pl.when((j == 0) | (j == 3))
        def _():
            finish(all_rows, 560, orecv_sem.at[s])

        @pl.when((j != 0) & (j != 3))
        def _():
            finish(all_rows, 416, orecv_sem.at[s])

        extra = 2 * height + 32
        left_at, right_at = 16, 240

        @pl.when(j != 0)
        def _():
            fold_f[left_at : left_at + height, :] = outer_recv[s, 0:height, :].astype(f32)

        @pl.when(j == 0)
        def _():
            fold_f[left_at - 16 : left_at + 64, :] = jnp.zeros((80, C), f32)
            fold_f[left_at + 64 : left_at + height, :] = outer_recv[s, 64:height, :].astype(f32)
            for jj in range(4):
                at = left_at - 16 + 16 * jj
                fold_f[at : at + 48, :] += outer_recv[
                    s, extra + 48 * jj : extra + 48 * jj + 48, :
                ].astype(f32)
            corner = outer_recv[s, extra + 192 : extra + 208, :].astype(f32)
            fold_f[left_at : left_at + 1, :] += corner[15:16]

        @pl.when(j != 3)
        def _():
            fold_f[right_at : right_at + height, :] = outer_recv[s, height : 2 * height, :].astype(
                f32
            )

        @pl.when(j == 3)
        def _():
            fold_f[right_at : right_at + height - 64, :] = outer_recv[
                s, height : 2 * height - 64, :
            ].astype(f32)
            fold_f[right_at + height - 64 : right_at + height + 16, :] = jnp.zeros((80, C), f32)
            for jj in range(4):
                at = right_at + 112 + 16 * jj
                fold_f[at : at + 48, :] += outer_recv[
                    s, extra + 48 * jj : extra + 48 * jj + 48, :
                ].astype(f32)
            corner = outer_recv[s, extra + 192 : extra + 208, :].astype(f32)
            last = right_at + height - 1
            fold_f[last : last + 1, :] += corner[0:1]

        ghid[s, 0:16, C : 2 * C] += outer_recv[s, 2 * height : 2 * height + 16, :].astype(f32)
        ghid[s, 8 * height : 8 * height + 16, 0:C] += outer_recv[s, 2 * height + 16 : 2 * height + 32, :].astype(f32)

        def scale(k, carry):
            total = jnp.zeros((pixels, C), f32)
            half = lax.broadcasted_iota(jnp.int32, (8, C), 0)
            for t in range(16):
                if t % 8 == 0:
                    left = fold_f[pl.ds(left_at + 16 * k + t, 8), :]
                    right = fold_f[pl.ds(right_at + 16 * k + t, 8), :]
                at = t % 8
                pair, e = (1 + t) // 2, (1 + t) % 2
                value = ghid[s, pl.ds(128 * k + 16 * pair, 16), e * C : (e + 1) * C]
                low = value[:8] + jnp.where(half == 0, turned_by(left, -at), 0.0)
                high = value[8:] + jnp.where(half == 7, turned_by(right, 7 - at), 0.0)
                delta = jnp.concatenate([low, high], axis=0) * slope[s, 16 * k + t]
                d1[16 * k + t] = delta.astype(bf16)
                total = total + delta
            bias_acc[0] += total
            return carry

        lax.fori_loop(0, tiles, scale, 0)
        turn_pairs(s, d1[...])
        return carry

    middle = batch // 2
    lax.fori_loop(0, middle, stage_three, 0)
    sum_plane(1, 0)
    lax.fori_loop(middle, batch, stage_three, 0)
    sum_plane(1, 1)
    weight_sum(xs, (0, 1), (0, middle))
    sum_plane(1, 2)
    sum_copies(1, 0)
    weight_sum(xs, (0, 1), (middle, batch))
    sum_start(0, 0)
    sum_copies(1, 1)
    weight_sum(xs, (2,), (0, batch))
    sum_start(0, 1)
    sum_copies(1, 2)
    weight_sum(xs, (3,), (0, middle))
    sum_plane(0, 0)
    weight_sum(xs, (3,), (middle, batch))
    sum_start(0, 2)

    for s in range(batch):
        dma_out(s).wait()

        @pl.when((j == 0) | (j == 3))
        def _():
            finish(all_rows, 544, send_sem.at[1, s])
            finish(all_rows, 496, osend_sem.at[s])

        @pl.when((j != 0) & (j != 3))
        def _():
            finish(all_rows, 416, send_sem.at[1, s])
            finish(all_rows, 480, osend_sem.at[s])

    for p in range(3):
        sum_end(1, p)
    sum_plane(0, 1)
    sum_copies(0, 0)
    sum_plane(0, 2)
    sum_copies(0, 1)
    sum_end(0, 0)
    sum_copies(0, 2)
    sum_end(0, 1)
    sum_end(0, 2)
    for g in range(2):
        for p in range(3):
            finish(grad_recv.at[g, p], (peers - 1) * blocks[p], gsend_sem.at[g, p, 0])
            finish(plane_recv.at[g, p], 3 * blocks[p], gsend_sem.at[g, p, 1])
            finish(part_recv.at[g, p], (peers - 1) * share, gsend_sem.at[g, p, 2])


def hand_over(*refs):
    sources, targets, held, sems = refs[:5], refs[5:10], refs[10:15], refs[15]
    parts = 4
    views = []
    tiles = sources[0].shape[0] // parts
    for i in range(parts):
        views.append(tuple(r[0].at[pl.ds(i * tiles, tiles)] for r in (sources, held, targets)))
    for i in range(1, 5):
        views.append((sources[i], held[i], targets[i]))
    arriving = [
        pltpu.make_async_copy(source, middle, sems.at[0, i])
        for i, (source, middle, _) in enumerate(views)
    ]
    leaving = [
        pltpu.make_async_copy(middle, target, sems.at[1, i])
        for i, (_, middle, target) in enumerate(views)
    ]
    for copy in arriving:
        copy.start()
    for first, second in zip(arriving, leaving):
        first.wait()
        second.start()
    for copy in leaving:
        copy.wait()


def strip_body(features, weight_one, bias_one, weight_two, bias_two, cotangent):
    tm_count = lax.axis_size("tm")
    tiles, batch, pixels, _, C = features.shape
    height = tiles * pixels
    bf16, f32 = jnp.bfloat16, jnp.float32
    peers = 4 * tm_count
    share = 3 * C // peers
    block = share + 16
    vmem = pl.BlockSpec(memory_space=pltpu.VMEM)
    hbm = pl.BlockSpec(memory_space=pl.ANY)
    dma = pltpu.SemaphoreType.DMA
    flops = 10 * tiles * batch * pixels * pixels * 9 * C * C
    output, gw1, gb1, gw2, gb2 = pl.pallas_call(
        functools.partial(strip_kernel, tm_count),
        in_specs=[hbm, hbm, vmem, vmem, vmem, vmem],
        out_specs=[hbm, vmem, vmem, vmem, vmem],
        out_shape=[
            jax.ShapeDtypeStruct(features.shape, bf16),
            jax.ShapeDtypeStruct((9 * C, C), f32), jax.ShapeDtypeStruct((1, C), f32),
            jax.ShapeDtypeStruct((9 * C, C), f32), jax.ShapeDtypeStruct((1, C), f32),
        ],
        scratch_shapes=[
            pltpu.VMEM(features.shape, bf16),
            pltpu.VMEM((batch, height + 2, 3, pixels, C), bf16),
            pltpu.VMEM((batch, height + 2, 3, pixels, C), bf16),
            pltpu.VMEM((1, height + 4, 3, pixels, C), bf16),
            pltpu.VMEM((height, pixels, C), bf16),
            pltpu.VMEM((batch, 2 * C, 8 * height), bf16),
            pltpu.VMEM((batch, height, pixels, C), f32),
            pltpu.VMEM((batch, 8 * height + 16, 2 * C), f32),
            pltpu.VMEM((8 * height, 2 * C), f32),
            pltpu.VMEM((12 * C, 2 * C), bf16),
            pltpu.VMEM((12 * C, 2 * C), bf16),
            pltpu.VMEM((12 * C, 2 * C), bf16),
            pltpu.VMEM((2, 3 * C, C), bf16),
            pltpu.VMEM((2 * C, 12 * C), f32),
            pltpu.VMEM((2, pixels, C), f32),
            pltpu.VMEM((528, C), f32),
            pltpu.VMEM((464, C), f32),
            pltpu.VMEM((2, batch, 2, height + 16, C), bf16),
            pltpu.VMEM((2, batch, 2 * height + 96, C), bf16),
            pltpu.VMEM((batch, 2, height + 32, C), bf16),
            pltpu.VMEM((batch, 2, 48, C), bf16),
            pltpu.VMEM((batch, 2 * height + 240, C), bf16),
            pltpu.VMEM((2, 3, peers, block, C), bf16),
            pltpu.VMEM((2, 3, peers * block, C), bf16),
            pltpu.VMEM((2, 3, 4 * block, C), bf16),
            pltpu.VMEM((2, 3, block, C), bf16),
            pltpu.VMEM((2, 3, share, C), bf16),
            pltpu.VMEM((2, 3, 3 * C, C), bf16),
            dma((batch,)), dma((batch,)), dma((batch,)),
            dma((2, batch)), dma((2, batch)), dma((batch,)), dma((batch,)), dma((2, 3, 3)), dma((2, 3, 3)),
        ],
        compiler_params=pltpu.CompilerParams(
            collective_id=0, has_side_effects=True, vmem_limit_bytes=60 * 1024 * 1024
        ),
        cost_estimate=pl.CostEstimate(
            flops=flops, bytes_accessed=6 * features.size, transcendentals=4 * features.size
        ),
    )(
        features, cotangent, weight_one, bias_one.reshape(1, C), weight_two,
        bias_two.reshape(1, C),
    )
    results = [output, gw1, gb1, gw2, gb2]
    output, gw1, gb1, gw2, gb2 = pl.pallas_call(
        hand_over,
        in_specs=[hbm] * 5,
        out_specs=[hbm] * 5,
        out_shape=[jax.ShapeDtypeStruct(r.shape, r.dtype) for r in results],
        scratch_shapes=[pltpu.VMEM(r.shape, r.dtype) for r in results] + [dma((2, 8))],
        compiler_params=pltpu.CompilerParams(vmem_limit_bytes=60 * 1024 * 1024),
    )(*results)
    shape = weight_one.shape
    return (output, gw1.reshape(shape), gb1.reshape(C), gw2.reshape(shape), gb2.reshape(C))


def whole_columns(mesh, tiles):
    columns, samples = mesh.shape["tile"], mesh.shape["tm"]
    return columns == 4 * S and tiles == 3 * S * columns and samples in (1, 2)


def solution(mesh):
    def call(*arrays):
        if whole_columns(mesh, arrays[0].shape[0]):
            chosen = strip_body
        else:
            chosen = body
        return jax.shard_map(
            chosen,
            mesh=mesh,
            in_specs=(
                P("tile", "tm", None, None, None),
                P(),
                P(),
                P(),
                P(),
                P("tile", "tm", None, None, None),
            ),
            out_specs=(P("tile", "tm", None, None, None), P(), P(), P(), P()),
            check_vma=False,
        )(*arrays)

    return call
```

```python
import functools
import math

import jax
import jax.numpy as jnp
import numpy as np
from jax import lax
from jax.experimental import pallas as pl
from jax.experimental.pallas import tpu as pltpu
from jax.sharding import PartitionSpec as P

S = 4


inv_sqrt_two = 0.7071067811865476
inv_sqrt_tau = 0.3989422804014327
LOG2_E = 1.4426950408889634
MESH = pl.DeviceIdType.MESH


def passed_along(value, axis, steps):
    count = lax.axis_size(axis)
    pairs = [(source, (source + steps) % count) for source in range(count)]
    return lax.ppermute(value, axis, pairs)


def edge_partner(face_id, edge_id):
    group_id = face_id // 4
    within = face_id % 4
    after_id = (within + 1) % 4
    before = (within + 3) % 4
    if group_id == 0:
        options = [(after_id, 2), (4 + within, 0), (before, 0), (4 + after_id, 2)]
    elif group_id == 1:
        options = [(within, 1), (8 + before, 0), (before, 3), (8 + within, 2)]
    else:
        options = [(4 + after_id, 1), (8 + before, 3), (4 + within, 3), (8 + after_id, 1)]
    return options[edge_id]


def entry_pixel(edge_id, along_edge, length):
    if edge_id == 0:
        return (0, along_edge)
    if edge_id == 1:
        return (length - 1, along_edge)
    if edge_id == 2:
        return (along_edge, 0)
    return (along_edge, length - 1)


def step_pixel(face_id, row_at, col_at, row_step, col_step, length):
    row_new = row_at + row_step
    col_new = col_at + col_step
    if 0 <= row_new < length and 0 <= col_new < length:
        return (face_id, row_new, col_new, -1)
    if row_new < 0:
        edge_id = 0
    elif row_new >= length:
        edge_id = 1
    elif col_new < 0:
        edge_id = 2
    else:
        edge_id = 3
    along_edge = col_at if edge_id < 2 else row_at
    partner, entered = edge_partner(face_id, edge_id)
    row_in, col_in = entry_pixel(entered, along_edge, length)
    return (partner, row_in, col_in, entered)


def neighbour_pixel(face_id, row_at, col_at, row_step, col_step, length):
    if row_step == 0 or col_step == 0:
        found = step_pixel(face_id, row_at, col_at, row_step, col_step, length)
        return (found[0], found[1], found[2])
    face_one, row_one, col_one, entered = step_pixel(face_id, row_at, col_at, row_step, 0, length)
    if entered >= 2:
        found = step_pixel(face_one, row_one, col_one, col_step, 0, length)
    else:
        found = step_pixel(face_one, row_one, col_one, 0, col_step, length)
    return (found[0], found[1], found[2])


def tile_slot(face_id, tile_row, tile_col, side_tiles):
    group_id = face_id // 4
    within = face_id % 4
    extra = 1 if group_id == 2 else 0
    column = (side_tiles * (within + extra) + tile_col) % (4 * side_tiles)
    return 3 * side_tiles * column + side_tiles * group_id + tile_row


def cycle_position(row_at, col_at, pixels):
    if row_at == 0:
        return col_at
    if row_at == pixels - 1:
        return pixels + col_at
    if col_at == 0:
        return 2 * pixels + row_at
    return 3 * pixels + row_at


def halo_positions(pixels):
    places = [(-1, column) for column in range(-1, pixels + 1)]
    places = places + [(pixels, column) for column in range(-1, pixels + 1)]
    places = places + [(row_at, -1) for row_at in range(pixels)]
    places = places + [(row_at, pixels) for row_at in range(pixels)]
    return places


def halo_sources(side_tiles, pixels):
    slot_count = 12 * side_tiles * side_tiles
    places = halo_positions(pixels)
    length = side_tiles * pixels
    source_slot = np.zeros((slot_count, len(places)), np.int64)
    source_cycle = np.zeros((slot_count, len(places)), np.int64)
    for face_id in range(12):
        for tile_row in range(side_tiles):
            for tile_col in range(side_tiles):
                slot_id = tile_slot(face_id, tile_row, tile_col, side_tiles)
                for cell_index in range(len(places)):
                    row_at, col_at = places[cell_index]
                    inner_row = min(max(row_at, 0), pixels - 1)
                    inner_col = min(max(col_at, 0), pixels - 1)
                    partner, row_new, col_new = neighbour_pixel(
                        face_id,
                        tile_row * pixels + inner_row,
                        tile_col * pixels + inner_col,
                        row_at - inner_row,
                        col_at - inner_col,
                        length,
                    )
                    source_slot[slot_id, cell_index] = tile_slot(
                        partner, row_new // pixels, col_new // pixels, side_tiles
                    )
                    source_cycle[slot_id, cell_index] = cycle_position(
                        row_new % pixels, col_new % pixels, pixels
                    )
    return (source_slot, source_cycle)


def halo_rows(row_at, col_at, pixels):
    if row_at == -1 or row_at == pixels:
        base = 0 if row_at == -1 else 3 * pixels
        return [
            base + pixels * shift + col_at + 1 - shift
            for shift in range(3)
            if 0 <= col_at + 1 - shift < pixels
        ]
    return [6 * pixels + row_at if col_at == -1 else 7 * pixels + row_at]


def outer_row(row_at, col_at, pixels):
    if col_at == -1:
        return 2 * pixels + row_at + 1
    if col_at == pixels:
        return 4 * pixels + row_at + 1
    return col_at if row_at == -1 else pixels + col_at


def device_tables(device_count, per_device, side_tiles, pixels):
    source_slot, source_cycle = halo_sources(side_tiles, pixels)
    places = halo_positions(pixels)
    rim_len, halo_len, outer_len = 4 * pixels, 8 * pixels, 6 * pixels
    sends = {}
    local = []
    for device in range(device_count):
        local.append([])
        for local_id in range(per_device):
            slot_id = device * per_device + local_id
            for cell in range(len(places)):
                row_at, col_at = places[cell]
                source = int(source_slot[slot_id, cell])
                moved_by = (device - source // per_device) % device_count
                if moved_by > device_count // 2:
                    moved_by -= device_count
                rim = source % per_device * rim_len + int(source_cycle[slot_id, cell])
                halo = [local_id * halo_len + h for h in halo_rows(row_at, col_at, pixels)]
                outer = local_id * outer_len + outer_row(row_at, col_at, pixels)
                record = (rim, halo, outer)
                if moved_by == 0:
                    local[device].append(record)
                else:
                    lists = sends.setdefault(moved_by, [[] for _ in range(device_count)])
                    lists[device].append(record)
    offsets = sorted(sends)
    widths = [-(-max(len(one) for one in sends[offset]) // 16) * 16 for offset in offsets]
    total = sum(widths)
    send = np.full((device_count, total), -1, np.int32)
    receive = np.full((device_count, per_device * halo_len), -1, np.int32)
    back = np.full((device_count, total), -1, np.int32)
    target = np.full((device_count, per_device * outer_len + total), -1, np.int32)
    for device in range(device_count):
        for rim, halo, outer in local[device]:
            receive[device, halo] = rim
            target[device, outer] = rim
        base = 0
        for offset, width in zip(offsets, widths):
            sender = (device - offset) % device_count
            for at, (rim, halo, outer) in enumerate(sends[offset][device]):
                send[sender, base + at] = rim
                receive[device, halo] = per_device * rim_len + base + at
                back[device, base + at] = outer
                target[sender, per_device * outer_len + base + at] = rim
            base += width
    return (offsets, widths, send, receive, back, target)


def one_hot(table_np, tile_index, width):
    row = jnp.asarray(table_np, dtype=jnp.int32)[tile_index]
    return (row[:, None] == lax.broadcasted_iota(jnp.int32, (row.shape[0], width), 1)).astype(
        jnp.bfloat16
    )


def exchanged(rows, offsets, widths, sign):
    pieces, base = [], 0
    for offset, width in zip(offsets, widths):
        pieces.append(passed_along(rows[base : base + width], "tile", sign * offset))
        base += width
    return pieces


def halo_of(rim, layout, tile_index):
    offsets, widths, send, receive = layout[:4]
    outgoing = jnp.dot(one_hot(send, tile_index, rim.shape[0]), rim)
    pool = jnp.concatenate([rim] + exchanged(outgoing, offsets, widths, 1), axis=0)
    return jnp.dot(one_hot(receive, tile_index, pool.shape[0]), pool)


def folded(outer, layout, tile_index, rim_rows):
    offsets, widths, _, _, back, target = layout
    outgoing = jnp.dot(one_hot(back, tile_index, outer.shape[0]), outer)
    pool = jnp.concatenate([outer] + exchanged(outgoing, offsets, widths, -1), axis=0)
    spread = one_hot(target, tile_index, rim_rows)
    return lax.dot_general(
        spread, pool, (((0,), (0,)), ((), ())), preferred_element_type=jnp.float32
    )


def gelu_parts(value):
    half = 0.5 * (1.0 + lax.erf(value * inv_sqrt_two))
    return value * half, half + value * jnp.exp(-0.5 * value * value) * inv_sqrt_tau


def columns_at(tile, halo, work, pixels):
    count = pixels * pixels
    wide = tile.astype(jnp.float32)
    halo_wide = halo[6 * pixels :].astype(jnp.float32)
    work[0, pl.ds(1, count - 1), :] = wide[: count - 1]
    work[0, pl.ds(0, pixels, stride=pixels), :] = halo_wide[:pixels]
    work[1, pl.ds(0, count - 1), :] = wide[1:]
    work[1, pl.ds(pixels - 1, pixels, stride=pixels), :] = halo_wide[pixels:]
    middles = [work[0].astype(jnp.bfloat16), tile, work[1].astype(jnp.bfloat16)]
    joined = jnp.concatenate(
        [
            jnp.concatenate(
                [
                    halo[pixels * b : pixels * (b + 1)],
                    middles[b],
                    halo[pixels * (3 + b) : pixels * (4 + b)],
                ],
                axis=0,
            )
            for b in range(3)
        ],
        axis=1,
    )
    return jnp.concatenate([joined[pixels * a : pixels * a + count] for a in range(3)], axis=1)


def first_kernel(x_ref, halo_ref, w_ref, bias_ref, hidden_ref, slope_ref, rim_ref, work):
    batch, pixels, channels = x_ref.shape[1], x_ref.shape[2], x_ref.shape[4]
    count = pixels * pixels
    for s in range(batch):
        lanes = slice(s * channels, (s + 1) * channels)
        tile = x_ref[0, s].reshape(count, channels)
        cols = columns_at(tile, halo_ref[0, :, lanes], work.at[pl.ds(2 * s, 2)], pixels)
        pre = jnp.dot(cols, w_ref[...], preferred_element_type=jnp.float32) + bias_ref[...]
        hidden, slope = gelu_parts(pre)
        slope_ref[0, s] = slope
        work[2 * batch + s] = hidden
        rounded = hidden.astype(jnp.bfloat16)
        hidden_ref[0, s] = rounded.reshape(pixels, pixels, channels)
        rim_ref[0, 0:pixels, lanes] = rounded[:pixels]
        rim_ref[0, pixels : 2 * pixels, lanes] = rounded[count - pixels :]
        for side in range(2):
            edge = work[2 * batch + s, pl.ds(side * (pixels - 1), pixels, stride=pixels), :]
            rim_ref[0, (2 + side) * pixels : (3 + side) * pixels, lanes] = edge.astype(jnp.bfloat16)


def second_kernel(
    x_ref, halo_ref, cot_ref, w_ref, flip_ref, side_ref, bias_ref,
    out_ref, inner_ref, outer_ref, grad_ref, sum_ref, work, cols_ref, delta_ref, edge_ref,
):
    batch, pixels, channels = x_ref.shape[1], x_ref.shape[2], x_ref.shape[4]
    count = pixels * pixels

    @pl.when(pl.program_id(0) == 0)
    def _():
        grad_ref[...] = jnp.zeros_like(grad_ref)
        sum_ref[...] = jnp.zeros_like(sum_ref)

    zero_row = jnp.zeros((1, channels), jnp.float32)
    zero_col = jnp.zeros((pixels, channels), jnp.float32)
    zeros = jnp.zeros((2 * pixels, 3 * channels), jnp.bfloat16)
    for s in range(batch):
        lanes = slice(s * channels, (s + 1) * channels)
        tile = x_ref[0, s].reshape(count, channels)
        here = work.at[pl.ds(2 * s, 2)]
        cols = columns_at(tile, halo_ref[0, :, lanes], here, pixels)
        cols_ref[s * count : (s + 1) * count, :] = cols
        pre = jnp.dot(cols, w_ref[...], preferred_element_type=jnp.float32) + bias_ref[...]
        value, slope = gelu_parts(pre)
        out_ref[0, s] = value.astype(jnp.bfloat16).reshape(pixels, pixels, channels)
        cot = cot_ref[0, s].reshape(count, channels).astype(jnp.float32)
        delta = (cot * slope).astype(jnp.bfloat16)
        delta_ref[s * count : (s + 1) * count, :] = delta
        wide = delta.astype(jnp.float32)
        sum_ref[...] += jnp.sum(wide, axis=0, keepdims=True)
        edge_ref[s] = jnp.zeros(edge_ref.shape[1:], jnp.float32)
        work[2 * batch + s] = wide
        for side in range(2):
            edge_ref[s, side, pl.ds(2, pixels), :] = work[
                2 * batch + s, pl.ds(side * (pixels - 1), pixels, stride=pixels), :
            ]
        here[0, pl.ds(0, count - 1), :] = wide[1:]
        here[0, pl.ds(pixels - 1, pixels, stride=pixels), :] = zero_col
        here[1, pl.ds(1, count - 1), :] = wide[: count - 1]
        here[1, pl.ds(0, pixels, stride=pixels), :] = zero_col
        joined = jnp.concatenate(
            [here[0].astype(jnp.bfloat16), delta, here[1].astype(jnp.bfloat16)], axis=1
        )
        joined = jnp.concatenate([zeros, joined, zeros], axis=0)
        tall = count + 2 * pixels
        spread = jnp.concatenate(
            [joined[pixels * (2 - a) : pixels * (2 - a) + tall] for a in range(3)], axis=1
        )
        grad = jnp.dot(spread, flip_ref[...], preferred_element_type=jnp.float32)
        inner_ref[0, s] = grad[pixels : pixels + count]
        outer_ref[0, 0:pixels, lanes] = grad[:pixels].astype(jnp.bfloat16)
        outer_ref[0, pixels : 2 * pixels, lanes] = grad[pixels + count :].astype(jnp.bfloat16)
        for side in range(2):
            lhs = jnp.concatenate(
                [edge_ref[s, side, pl.ds(2 - a, 2 * pixels), :] for a in range(3)], axis=1
            ).astype(jnp.bfloat16)
            part = jnp.dot(lhs, side_ref[side], preferred_element_type=jnp.float32)
            outer_ref[0, 2 * pixels * (1 + side) : 2 * pixels * (2 + side), lanes] = part.astype(
                jnp.bfloat16
            )
    grad_ref[...] += lax.dot_general(
        delta_ref[...], cols_ref[...], (((0,), (0,)), ((), ())), preferred_element_type=jnp.float32
    )


def third_kernel(
    x_ref, halo_ref, inner_ref, rim_ref, slope_ref, grad_ref, sum_ref, work, cols_ref, delta_ref
):
    batch, pixels, channels = x_ref.shape[1], x_ref.shape[2], x_ref.shape[4]
    count = pixels * pixels

    @pl.when(pl.program_id(0) == 0)
    def _():
        grad_ref[...] = jnp.zeros_like(grad_ref)
        sum_ref[...] = jnp.zeros_like(sum_ref)

    for s in range(batch):
        lanes = slice(s * channels, (s + 1) * channels)
        tile = x_ref[0, s].reshape(count, channels)
        cols_ref[s * count : (s + 1) * count, :] = columns_at(
            tile, halo_ref[0, :, lanes], work.at[pl.ds(2 * s, 2)], pixels
        )
        at = 2 * batch + s
        work[at] = inner_ref[0, s]
        work[at, pl.ds(0, pixels), :] += rim_ref[0, 0:pixels, lanes]
        work[at, pl.ds(count - pixels, pixels), :] += rim_ref[0, pixels : 2 * pixels, lanes]
        for side in range(2):
            place = pl.ds(side * (pixels - 1), pixels, stride=pixels)
            edge = rim_ref[0, (2 + side) * pixels : (3 + side) * pixels, lanes]
            work[at, place, :] = work[at, place, :] + edge
        delta = (work[at] * slope_ref[0, s]).astype(jnp.bfloat16)
        delta_ref[s * count : (s + 1) * count, :] = delta
        sum_ref[...] += jnp.sum(delta.astype(jnp.float32), axis=0, keepdims=True)
    grad_ref[...] += lax.dot_general(
        delta_ref[...], cols_ref[...], (((0,), (0,)), ((), ())), preferred_element_type=jnp.float32
    )


def per_tile(shape):
    return pl.BlockSpec((1,) + tuple(shape), lambda t: (t,) + (0,) * len(shape))


def whole(shape):
    return pl.BlockSpec(tuple(shape), lambda t: (0,) * len(shape))


params = dict(vmem_limit_bytes=48 * 1024 * 1024)


def body(features, weight_one, bias_one, weight_two, bias_two, cotangent):
    device_count = lax.axis_size("tile")
    samples_count = lax.axis_size("tm")
    tile_index = lax.axis_index("tile")
    per_device, batch, pixels, _, channels = features.shape
    count = pixels * pixels
    lane_count = batch * channels
    layout = device_tables(device_count, per_device, S, pixels)
    bf16, f32 = jnp.bfloat16, jnp.float32
    tile_shape = (batch, pixels, pixels, channels)
    flat_shape = (batch, count, channels)
    halo_shape = (8 * pixels, lane_count)
    rim_shape = (4 * pixels, lane_count)
    outer_shape = (6 * pixels, lane_count)
    mat_one = weight_one.reshape(9 * channels, channels)
    mat_two = weight_two.reshape(9 * channels, channels)
    turned = weight_two.transpose(0, 1, 3, 2)
    flip = turned.reshape(9 * channels, channels)
    sides = jnp.stack([turned[:, 0], turned[:, 2]]).reshape(2, 3 * channels, channels)

    def out(shape, dtype):
        return jax.ShapeDtypeStruct((per_device,) + tuple(shape), dtype)

    work = pltpu.VMEM((3 * batch, count, channels), f32)
    cols = pltpu.VMEM((batch * count, 9 * channels), bf16)
    deltas = pltpu.VMEM((batch * count, channels), bf16)
    grad_shape = (channels, 9 * channels)

    rim_one = jnp.concatenate(
        [features[:, :, 0], features[:, :, -1], features[:, :, :, 0], features[:, :, :, -1]], axis=2
    )
    rim_one = rim_one.transpose(0, 2, 1, 3).reshape(per_device * 4 * pixels, lane_count)
    halo_one = halo_of(rim_one, layout, tile_index).reshape((per_device,) + halo_shape)
    hidden, slope, rim_two = pl.pallas_call(
        first_kernel,
        grid=(per_device,),
        in_specs=[per_tile(tile_shape), per_tile(halo_shape), whole(mat_one.shape), whole((1, channels))],
        out_specs=[per_tile(tile_shape), per_tile(flat_shape), per_tile(rim_shape)],
        out_shape=[out(tile_shape, bf16), out(flat_shape, f32), out(rim_shape, bf16)],
        scratch_shapes=[work],
        compiler_params=pltpu.CompilerParams(**params),
    )(features, halo_one, mat_one, bias_one.reshape(1, channels))
    halo_two = halo_of(rim_two.reshape(-1, lane_count), layout, tile_index)
    output, inner, outer, grad_two, sum_two = pl.pallas_call(
        second_kernel,
        grid=(per_device,),
        in_specs=[
            per_tile(tile_shape), per_tile(halo_shape), per_tile(tile_shape), whole(mat_two.shape),
            whole(flip.shape), whole(sides.shape), whole((1, channels)),
        ],
        out_specs=[
            per_tile(tile_shape), per_tile(flat_shape), per_tile(outer_shape),
            whole(grad_shape), whole((1, channels)),
        ],
        out_shape=[
            out(tile_shape, bf16), out(flat_shape, f32), out(outer_shape, bf16),
            jax.ShapeDtypeStruct(grad_shape, f32), jax.ShapeDtypeStruct((1, channels), f32),
        ],
        scratch_shapes=[work, cols, deltas, pltpu.VMEM((batch, 2, 2 * pixels + 8, channels), f32)],
        compiler_params=pltpu.CompilerParams(**params),
    )(
        hidden, halo_two.reshape((per_device,) + halo_shape), cotangent, mat_two, flip, sides,
        bias_two.reshape(1, channels),
    )
    rim_grad = folded(outer.reshape(-1, lane_count), layout, tile_index, per_device * 4 * pixels)
    grad_one, sum_one = pl.pallas_call(
        third_kernel,
        grid=(per_device,),
        in_specs=[
            per_tile(tile_shape), per_tile(halo_shape), per_tile(flat_shape), per_tile(rim_shape),
            per_tile(flat_shape),
        ],
        out_specs=[whole(grad_shape), whole((1, channels))],
        out_shape=[jax.ShapeDtypeStruct(grad_shape, f32), jax.ShapeDtypeStruct((1, channels), f32)],
        scratch_shapes=[work, cols, deltas],
        compiler_params=pltpu.CompilerParams(**params),
    )(features, halo_one, inner, rim_grad.reshape((per_device,) + rim_shape), slope)

    total_pixels = 12 * S * S * count * batch * samples_count
    grad_scale = 1.0 / math.sqrt(total_pixels)
    devices = device_count * samples_count
    axes = ("tile", "tm")

    def summed(grad, bias):
        rows = jnp.concatenate([grad.reshape(-1, channels), bias], axis=0)
        used = rows.shape[0]
        chunk = -(-used // (8 * devices)) * 8
        rows = jnp.pad(rows, ((0, chunk * devices - used), (0, 0)))
        parts = lax.all_to_all(rows.reshape(devices, chunk, channels), axes, 0, 0)
        mine = (jnp.sum(parts, axis=0) * grad_scale).astype(bf16)
        copies = jnp.broadcast_to(mine[None], (devices, chunk, channels))
        total = lax.all_to_all(copies, axes, 0, 0).reshape(devices * chunk, channels).astype(f32)
        weight = total[: used - 1].reshape(channels, 3, 3, channels).transpose(1, 2, 3, 0)
        return weight, total[used - 1]

    grad_weight_two, grad_bias_two = summed(grad_two, sum_two)
    grad_weight_one, grad_bias_one = summed(grad_one, sum_one)
    return (output, grad_weight_one, grad_bias_one, grad_weight_two, grad_bias_two)


def cdf_parts(value):
    bell = jnp.exp2(value * value * (-0.5 * LOG2_E))
    t = 1.0 / (1.0 + (0.3275911 * inv_sqrt_two) * jnp.abs(value))
    poly = 0.5 * 1.061405429
    for coefficient in (-1.453152027, 1.421413741, -0.284496736, 0.254829592):
        poly = poly * t + 0.5 * coefficient
    tail = poly * t * bell
    return jnp.where(value < 0.0, tail, 1.0 - tail), bell


def put_shifted(ref, sample, at, row, first, last, from_left, from_right):
    low, high = row[:8], row[8:]
    low_down, high_down = turned_by(low, 1), turned_by(high, 1)
    shifted = jnp.concatenate(
        [jnp.where(first, from_left, low_down), jnp.where(first, low_down, high_down)], axis=0
    )
    ref[sample, at, 0] = shifted.astype(jnp.bfloat16)
    low_up, high_up = turned_by(low, 7), turned_by(high, 7)
    shifted = jnp.concatenate(
        [jnp.where(last, high_up, low_up), jnp.where(last, from_right, high_up)], axis=0
    )
    ref[sample, at, 2] = shifted.astype(jnp.bfloat16)


def turned_by(value, steps):
    steps = steps % 8
    return value if steps == 0 else pltpu.roll(value, steps, 0)


class Edges:
    def __init__(self, half):
        self.half, self.lefts, self.rights = half, [], []

    def add(self, t, row):
        if t % 8 == 0:
            self.lefts.append(row[:8])
            self.rights.append(turned_by(row[8:], 1))
        else:
            here = self.half == t % 8
            self.lefts[-1] = jnp.where(here, turned_by(row[:8], t), self.lefts[-1])
            self.rights[-1] = jnp.where(here, turned_by(row[8:], t + 1), self.rights[-1])

    def columns(self):
        return jnp.concatenate(self.lefts, axis=0), jnp.concatenate(self.rights, axis=0)


def pair_window(ref, sample, start, pairs):
    lanes = ref.shape[4]
    v = ref[sample, pl.ds(start, 2 * pairs + 2)].reshape(pairs + 1, 2, 3, 16, lanes)
    parts = [v[:pairs, 0], v[:pairs, 1], v[1:, 0], v[1:, 1]]
    return jnp.concatenate(
        [p[:, b].reshape(pairs * 16, lanes) for p in parts for b in range(3)], axis=1
    )


def strip_kernel(
    tm_count,
    x_hbm, cot_hbm, w1_ref, b1_ref, w2_ref, b2_ref,
    out_hbm, gw1_ref, gb1_ref, gw2_ref, gb2_ref,
    field, xs, hs, ds, d1, turned, slope, ghid, pre_f, w1p, w2p, wback, wside, acc, bias_acc,
    edge_f, fold_f, edge_send, halo_recv, outer_send, corner_send, outer_recv,
    grad_send, grad_recv, plane_recv, plane_send, part_send, part_recv,
    in_sem, cot_sem, out_sem, send_sem, recv_sem, osend_sem, orecv_sem, gsend_sem, grecv_sem,
):
    f32, bf16 = jnp.float32, jnp.bfloat16
    tiles, batch, pixels, _, C = x_hbm.shape
    height = tiles * pixels
    columns = 16
    me = lax.axis_index("tile")
    other = lax.axis_index("tm")
    n, j = me // 4, me % 4
    peers = 4 * tm_count
    plane = j * tm_count + other

    def wrap(c):
        return (c + 2 * columns) % columns

    def dma_in(s):
        return pltpu.make_async_copy(x_hbm.at[:, s], field.at[:, s], in_sem.at[s])

    def dma_cot(s):
        return pltpu.make_async_copy(cot_hbm.at[:, s], field.at[:, s], cot_sem.at[s])

    def dma_out(s):
        return pltpu.make_async_copy(field.at[:, s], out_hbm.at[:, s], out_sem.at[s])

    def remote(src, dst, send, recv, device, side=None):
        pltpu.make_async_remote_copy(
            src_ref=src, dst_ref=dst, send_sem=send, recv_sem=recv,
            device_id=(device, other if side is None else side), device_id_type=MESH,
        ).start()

    def finish(ref, count, sem):
        view = ref.at[pl.ds(0, count)]
        pltpu.make_async_copy(view, view, sem).wait()

    for s in range(batch):
        dma_in(s).start()

    barrier = pltpu.get_barrier_semaphore()
    for offset in range(1, columns):
        pl.semaphore_signal(
            barrier, inc=1, device_id=(wrap(me + offset), other), device_id_type=MESH
        )
    for step in range(1, tm_count):
        for jj in range(4):
            pl.semaphore_signal(
                barrier, inc=1, device_id=(4 * n + jj, (other + step) % tm_count),
                device_id_type=MESH,
            )
    pl.semaphore_wait(barrier, columns - 1 + 4 * (tm_count - 1))

    def send_rim(f, s, field_ref, top, bottom):
        es, er = edge_send.at[f, s, 0], edge_send.at[f, s, 1]
        ss, rs = send_sem.at[f, s], recv_sem.at[f, s]
        land = halo_recv.at[f, s]

        def cut(ref, start, count):
            return ref.at[pl.ds(start, count)]

        @pl.when(j >= 1)
        def _():
            remote(cut(es, 16, height), cut(land, height, height), ss, rs, wrap(me - 1))

        @pl.when(j == 0)
        def _():
            remote(cut(es, 80, height - 64), cut(land, height, height - 64), ss, rs, wrap(me - 1))

        @pl.when(j <= 2)
        def _():
            remote(cut(er, 0, height), cut(land, 0, height), ss, rs, wrap(me + 1))

        @pl.when(j == 3)
        def _():
            remote(cut(er, 0, height - 64), cut(land, 64, height - 64), ss, rs, wrap(me + 1))

        remote(top, cut(land, 16 * j, 16), ss, rs, wrap(4 * n + 4))
        remote(bottom, cut(land, height + 128 + 16 * j, 16), ss, rs, wrap(4 * n - 1))
        upper, lower = 2 * height, 2 * height + 48

        @pl.when(j == 0)
        def _():
            remote(cut(es, 16, 32), cut(land, upper + 16, 32), ss, rs, wrap(me - 4))
            for jj in range(1, 4):
                remote(cut(es, 16 * jj, 48), cut(land, upper, 48), ss, rs, wrap(me - 4 + jj))
            remote(cut(es, 0, 16), cut(land, upper, 16), ss, rs, wrap(me + 8))

        @pl.when(j == 3)
        def _():
            for jj in range(3):
                remote(
                    cut(er, 112 + 16 * jj, 48), cut(land, lower, 48), ss, rs, wrap(me + 1 + jj)
                )
            remote(cut(er, height - 32, 32), cut(land, lower, 32), ss, rs, wrap(me + 4))
            remote(cut(er, height, 16), cut(land, lower + 32, 16), ss, rs, wrap(me + 8))

    half_iota = lax.broadcasted_iota(jnp.int32, (8, C), 0)
    first_pixel, last_pixel = half_iota == 0, half_iota == 7

    def put_edges(f, s, k, edges):
        left, right = edges.columns()
        edge_send[f, s, 0, pl.ds(16 + 16 * k, 16), :] = left.astype(bf16)
        edge_send[f, s, 1, pl.ds(16 * k, 16), :] = right.astype(bf16)

    def put_corners(f, s):
        row = edge_send[f, s, 0, 16:32, :].astype(f32)
        edge_send[f, s, 0, 0:16, :] = jnp.broadcast_to(row[0:1], (16, C)).astype(bf16)
        row = edge_send[f, s, 1, height - 16 : height, :].astype(f32)
        edge_send[f, s, 1, height : height + 16, :] = jnp.broadcast_to(row[15:16], (16, C)).astype(
            bf16
        )

    def put_halo_rows(f, s, ref):
        for side in range(2):
            edge_f[0:48, :] = halo_recv[f, s, pl.ds(2 * height + 48 * side, 48), :].astype(f32)
            for b in range(3):
                ref[s, side * (height + 1), b] = edge_f[
                    15 + b : 31 + b, :
                ].astype(bf16)

    def shift_tile(f, s, k, ref, row_of):
        left = halo_recv[f, s, pl.ds(16 * k, 16), :].astype(f32)
        right = halo_recv[f, s, pl.ds(height + 16 * k, 16), :].astype(f32)
        for t in range(16):
            group = 8 * (t // 8)
            put_shifted(
                ref, s, 1 + 16 * k + t, row_of(t), first_pixel, last_pixel,
                turned_by(left[group : group + 8], -t), turned_by(right[group : group + 8], 7 - t),
            )

    def features_out(s, carry):
        dma_in(s).wait()

        def step(k, carry):
            edges = Edges(half_iota)
            for t in range(16):
                edges.add(t, field[k, s, t].astype(f32))
            put_edges(0, s, k, edges)
            return carry

        lax.fori_loop(0, tiles, step, 0)
        put_corners(0, s)
        send_rim(0, s, field, field.at[0, s, 0], field.at[tiles - 1, s, pixels - 1])
        return carry

    lax.fori_loop(0, batch, features_out, 0)

    one, two = w1_ref[...].reshape(9 * C, C), w2_ref[...].reshape(9 * C, C)
    zeros = jnp.zeros((3 * C, C), bf16)
    for packed, flat in ((w1p, one), (w2p, two)):
        packed[0 : 9 * C, 0:C] = flat
        packed[9 * C : 12 * C, 0:C] = zeros
        packed[0 : 3 * C, C : 2 * C] = zeros
        packed[3 * C : 12 * C, C : 2 * C] = flat
    for e in range(2):
        gap = 3 * (1 - e)
        wback[(9 if e == 0 else 0) * C + 0 : (12 if e == 0 else 3) * C, e * C : (e + 1) * C] = zeros
    for a in range(3):
        for b in range(3):
            block = w2_ref[a, b].astype(f32).T.astype(bf16)
            for e in range(2):
                at = ((2 + e - a) * 3 + 2 - b) * C
                wback[at : at + C, e * C : (e + 1) * C] = block
            if b != 1:
                wside[b // 2, a * C : (a + 1) * C, :] = block

    bias_one = jnp.concatenate([b1_ref[...], b1_ref[...]], axis=1)
    bias_two = jnp.concatenate([b2_ref[...], b2_ref[...]], axis=1)
    bias_acc[...] = jnp.zeros_like(bias_acc)

    def build_one(s, k):
        for t in range(16):
            xs[s, 1 + 16 * k + t, 1] = field[k, s, t]
        shift_tile(0, s, k, xs, lambda t: field[k, s, t].astype(f32))

    def build_two(s, k):
        shift_tile(1, s, k, hs, lambda t: hs[s, 1 + 16 * k + t, 1].astype(f32))

    def first_copies(f, ref, build):
        finish(halo_recv.at[f, 0], 2 * height + 96, recv_sem.at[f, 0])
        put_halo_rows(f, 0, ref)

        def step(k, carry):
            build(0, k)
            return carry

        lax.fori_loop(0, tiles, step, 0)

    def stage_one(s, carry):
        @pl.when(s + 1 < batch)
        def _():
            finish(halo_recv.at[0, s + 1], 2 * height + 96, recv_sem.at[0, s + 1])

        following = s + 1 - (s + 1) // batch

        def dot(c):
            pre_f[rows_of * c : rows_of * (c + 1), :] = jnp.dot(
                pair_window(xs, s, 2 * per_chunk * c, per_chunk), w1p[...],
                preferred_element_type=f32,
            )

        def after(k):
            edges = Edges(half_iota)
            for q in range(8):
                at = 128 * k + 16 * q
                pre = pre_f[at : at + 16, :] + bias_one
                half, bell = cdf_parts(pre)
                hidden = pre * half
                slopes = half + pre * (bell * inv_sqrt_tau)
                for e in range(2):
                    t = 2 * q + e
                    row = hidden[:, e * C : (e + 1) * C]
                    hs[s, 1 + 16 * k + t, 1] = row.astype(bf16)
                    slope[s, 16 * k + t] = slopes[:, e * C : (e + 1) * C]
                    edges.add(t, row)
            put_edges(1, s, k, edges)

        dot(0)
        put_halo_rows(0, following, xs)
        for k in range(tiles // 2):
            build_one(following, k)
        dot(1)
        for k in range(tiles // 2, tiles):
            build_one(following, k)
            if k % 2:
                after((k - tiles // 2) // 2)
        after(3)
        dot(2)
        for k in range(4, tiles):
            after(k)
        put_corners(1, s)
        top = hs.at[s, 1, 1]
        bottom = hs.at[s, height, 1]
        send_rim(1, s, hs, top, bottom)
        @pl.when((j == 0) | (j == 3))
        def _():
            finish(all_rows, 544, send_sem.at[0, s])

        @pl.when((j != 0) & (j != 3))
        def _():
            finish(all_rows, 416, send_sem.at[0, s])

        dma_cot(s).start()
        return carry

    all_rows = outer_recv.at[0]
    chunks = 3
    per_chunk = pairs_of = height // 2 // chunks
    rows_of = 16 * per_chunk

    first_copies(0, xs, build_one)
    lax.fori_loop(0, batch, stage_one, 0)

    for at in (0, 1, height + 2, height + 3):
        ds[0, at] = jnp.zeros((3, pixels, C), bf16)
    for side in range(2):
        edge_f[48 + 240 * side : 48 + 240 * side + 24, :] = jnp.zeros((24, C), f32)
        edge_f[48 + 240 * side + 24 + height : 288 + 240 * side, :] = jnp.zeros(
            (216 - height, C), f32
        )

    def send_outer(s):
        ss, rs = osend_sem.at[s], orecv_sem.at[s]
        ol, orr = outer_send.at[s, 0], outer_send.at[s, 1]
        tb, bb = corner_send.at[s, 0], corner_send.at[s, 1]
        land = outer_recv.at[s]
        g_top, g_bottom, extra = 2 * height, 2 * height + 16, 2 * height + 32

        def cut(ref, start, count):
            return ref.at[pl.ds(start, count)]

        @pl.when(j >= 1)
        def _():
            remote(cut(ol, 16, height), cut(land, height, height), ss, rs, wrap(me - 1))

        @pl.when(j <= 2)
        def _():
            remote(cut(orr, 16, height), cut(land, 0, height), ss, rs, wrap(me + 1))

        @pl.when(j == 0)
        def _():
            remote(cut(ol, 80, height - 64), cut(land, height, height - 64), ss, rs, wrap(me - 1))
            for i in range(4):
                remote(cut(ol, 16 + 16 * i, 16), cut(land, g_top, 16), ss, rs, wrap(me - 4 + i))
            remote(cut(tb, 0, 16), cut(land, extra + 192, 16), ss, rs, wrap(me + 8))

        @pl.when(j == 3)
        def _():
            remote(cut(orr, 16, height - 64), cut(land, 64, height - 64), ss, rs, wrap(me + 1))
            for i in range(4):
                remote(
                    cut(orr, 144 + 16 * i, 16), cut(land, g_bottom, 16), ss, rs, wrap(me + 1 + i)
                )
            remote(cut(bb, 32, 16), cut(land, extra + 192, 16), ss, rs, wrap(me + 8))

        remote(tb, cut(land, extra + 48 * j, 48), ss, rs, wrap(4 * n + 4))
        remote(bb, cut(land, extra + 48 * j, 48), ss, rs, wrap(4 * n - 1))

    def stage_two(s, carry):
        @pl.when(s + 1 < batch)
        def _():
            finish(halo_recv.at[1, s + 1], 2 * height + 96, recv_sem.at[1, s + 1])

        following = s + 1 - (s + 1) // batch
        earlier = s - (s + batch - 1) // batch
        dma_cot(s).wait()

        def dot(c):
            pre_f[rows_of * c : rows_of * (c + 1), :] = jnp.dot(
                pair_window(hs, s, 2 * per_chunk * c, per_chunk), w2p[...],
                preferred_element_type=f32,
            )

        zero = jnp.zeros((8, C), f32)

        def after(k):
            edges = Edges(half_iota)
            total = jnp.zeros((pixels, C), f32)
            for q in range(8):
                at = 128 * k + 16 * q
                pre = pre_f[at : at + 16, :] + bias_two
                half, bell = cdf_parts(pre)
                outs = pre * half
                slopes = half + pre * (bell * inv_sqrt_tau)
                for e in range(2):
                    t = 2 * q + e
                    delta = field[k, s, t].astype(f32) * slopes[:, e * C : (e + 1) * C]
                    field[k, s, t] = outs[:, e * C : (e + 1) * C].astype(bf16)
                    row = 2 + 16 * k + t
                    ds[0, row, 1] = delta.astype(bf16)
                    total = total + delta
                    put_shifted(ds, 0, row, delta, first_pixel, last_pixel, zero, zero)
                    edges.add(t, delta)
            left, right = edges.columns()
            edge_f[72 + 16 * k : 88 + 16 * k, :] = left
            edge_f[312 + 16 * k : 328 + 16 * k, :] = right
            bias_acc[1] += total

        def back(c):
            first, last = (pairs_of * c, pairs_of * (c + 1) + c // (chunks - 1))
            ghid[s, 16 * first : 16 * last] = jnp.dot(
                pair_window(ds, 0, 2 * first, last - first), wback[...],
                preferred_element_type=f32,
            )

        dot(0)
        dot(1)
        for k in range(tiles):
            after(k)
            if k == 3:
                dot(2)
            if k in (1, 5, 9):
                window_sum(hs, earlier, s, ((1, 5, 9).index(k),))
            if k in (6, 10):
                back((k - 6) // 4)
        window_sum(hs, earlier, s, (3,))
        put_halo_rows(1, following, hs)
        for k in range(tiles // 2):
            build_two(following, k)
        back(2)
        for k in range(tiles // 2, tiles):
            build_two(following, k)
        dma_out(s).start()

        fold_f[0:96, :] = jnp.zeros((96, C), f32)
        for side in range(2):
            base = 48 + 240 * side
            lhs = jnp.concatenate(
                [edge_f[base + 9 - a : base + 233 - a, :] for a in range(3)], axis=1
            ).astype(bf16)
            cells = jnp.dot(lhs, wside[side], preferred_element_type=f32)
            outer_send[s, side] = cells.astype(bf16)
            fold_f[15 + 17 * side : 16 + 17 * side, :] = cells[15:16]
            fold_f[63 + 17 * side : 64 + 17 * side, :] = cells[16 + height : 17 + height]

        fold_f[16:32, :] = ghid[s, 0:16, 0:C]
        fold_f[64:80, :] = ghid[s, 8 * height : 8 * height + 16, C : 2 * C]
        corner_send[s, 0] = fold_f[0:48, :].astype(bf16)
        corner_send[s, 1] = fold_f[48:96, :].astype(bf16)
        send_outer(s)

        turn_pairs(s, ds[0, 2 : 2 + height, 1])
        return carry

    def turn_pairs(s, value):
        v = value.reshape(height // 2, 2, pixels, C)
        turned[s + 1] = jnp.concatenate(
            [v[:, e].reshape(8 * height, C) for e in range(2)], axis=1
        ).T

    def window_sum(ref, s, slot, window):
        pairs = height // 2
        lanes = slice(window[0] * 3 * C, (window[-1] + 1) * 3 * C)
        v = ref[s].reshape(pairs + 1, 2, 3, pixels, C)
        parts = []
        for w in window:
            x = v[:pairs, w] if w < 2 else v[1:, w - 2]
            parts += [x[:, b].reshape(pairs * pixels, C) for b in range(3)]
        acc[:, lanes] += jnp.dot(
            turned[slot], jnp.concatenate(parts, axis=1), preferred_element_type=f32
        )

    def weight_sum(ref, window, samples):
        lanes = slice(window[0] * 3 * C, (window[-1] + 1) * 3 * C)
        if samples[0] == 0:
            acc[:, lanes] = jnp.zeros((2 * C, 3 * C * len(window)), f32)

        def step(s, carry):
            window_sum(ref, s, s + 1, window)
            return carry

        lax.fori_loop(samples[0], samples[1], step, 0)

    acc[...] = jnp.zeros_like(acc)
    turned[0] = jnp.zeros(turned.shape[1:], bf16)
    first_copies(1, hs, build_two)
    lax.fori_loop(0, batch, stage_two, 0)

    share = 3 * C // peers
    blocks = (share + 16, share, share)

    def sum_start(g, p):
        block = blocks[p]
        for b in range(3):
            at = (3 * p + b) * C
            value = (acc[0:C, at : at + C] + acc[C : 2 * C, at + 3 * C : at + 4 * C]).T.astype(bf16)
            for u in range(C // 16):
                row = b * C + 16 * u
                grad_send[g, p, row // share, row % share : row % share + 16, :] = value[
                    16 * u : 16 * u + 16
                ]
        if p == 0:
            bias = jnp.broadcast_to(
                jnp.sum(bias_acc[g], axis=0, keepdims=True), (16, C)
            ).astype(bf16)
            for d in range(peers):
                grad_send[g, p, d, share:block, :] = bias
        for step in range(1, peers):
            to = (plane + step) % peers
            remote(
                grad_send.at[g, p, to, pl.ds(0, block)],
                grad_recv.at[g, p, pl.ds(plane * block, block)],
                gsend_sem.at[g, p, 0], grecv_sem.at[g, p, 0],
                4 * n + to // tm_count, to % tm_count,
            )
        grad_recv[g, p, pl.ds(plane * block, block), :] = grad_send[g, p, plane, 0:block, :]

    def sum_plane(g, p):
        block = blocks[p]
        finish(grad_recv.at[g, p], (peers - 1) * block, grecv_sem.at[g, p, 0])
        total = grad_recv[g, p, 0:block, :].astype(f32)
        for d in range(1, peers):
            total = total + grad_recv[g, p, d * block : (d + 1) * block, :].astype(f32)
        plane_send[g, p, 0:block, :] = total.astype(bf16)
        for step in range(1, 4):
            remote(
                plane_send.at[g, p, pl.ds(0, block)],
                plane_recv.at[g, p, pl.ds(n * block, block)],
                gsend_sem.at[g, p, 1], grecv_sem.at[g, p, 1], wrap(me + 4 * step),
            )
        plane_recv[g, p, pl.ds(n * block, block), :] = total.astype(bf16)

    def sum_copies(g, p):
        block = blocks[p]
        finish(plane_recv.at[g, p], 3 * block, grecv_sem.at[g, p, 1])
        total = plane_recv[g, p, 0:block, :].astype(f32)
        for d in range(1, 4):
            total = total + plane_recv[g, p, d * block : (d + 1) * block, :].astype(f32)
        pixel_count = 16 * height * pixels * batch * tm_count
        total = total * (1.0 / math.sqrt(pixel_count))
        if p == 0:
            (gb1_ref, gb2_ref)[g][...] = total[share : share + 1]
        mine = total[0:share].astype(bf16)
        part_send[g, p] = mine
        for step in range(1, peers):
            to = (plane + step) % peers
            remote(
                part_send.at[g, p], part_recv.at[g, p, pl.ds(plane * share, share)],
                gsend_sem.at[g, p, 2], grecv_sem.at[g, p, 2],
                4 * n + to // tm_count, to % tm_count,
            )
        part_recv[g, p, pl.ds(plane * share, share), :] = mine

    def sum_end(g, p):
        finish(part_recv.at[g, p], (peers - 1) * share, grecv_sem.at[g, p, 2])
        (gw1_ref, gw2_ref)[g][3 * C * p : 3 * C * (p + 1), :] = part_recv[g, p].astype(f32)

    weight_sum(hs, (0, 1), (batch - 1, batch))
    sum_start(1, 0)
    weight_sum(hs, (2,), (batch - 1, batch))
    sum_start(1, 1)
    weight_sum(hs, (3,), (batch - 1, batch))
    sum_start(1, 2)

    def stage_three(s, carry):
        @pl.when((j == 0) | (j == 3))
        def _():
            finish(all_rows, 560, orecv_sem.at[s])

        @pl.when((j != 0) & (j != 3))
        def _():
            finish(all_rows, 416, orecv_sem.at[s])

        extra = 2 * height + 32
        left_at, right_at = 16, 240

        @pl.when(j != 0)
        def _():
            fold_f[left_at : left_at + height, :] = outer_recv[s, 0:height, :].astype(f32)

        @pl.when(j == 0)
        def _():
            fold_f[left_at - 16 : left_at + 64, :] = jnp.zeros((80, C), f32)
            fold_f[left_at + 64 : left_at + height, :] = outer_recv[s, 64:height, :].astype(f32)
            for jj in range(4):
                at = left_at - 16 + 16 * jj
                fold_f[at : at + 48, :] += outer_recv[
                    s, extra + 48 * jj : extra + 48 * jj + 48, :
                ].astype(f32)
            corner = outer_recv[s, extra + 192 : extra + 208, :].astype(f32)
            fold_f[left_at : left_at + 1, :] += corner[15:16]

        @pl.when(j != 3)
        def _():
            fold_f[right_at : right_at + height, :] = outer_recv[s, height : 2 * height, :].astype(
                f32
            )

        @pl.when(j == 3)
        def _():
            fold_f[right_at : right_at + height - 64, :] = outer_recv[
                s, height : 2 * height - 64, :
            ].astype(f32)
            fold_f[right_at + height - 64 : right_at + height + 16, :] = jnp.zeros((80, C), f32)
            for jj in range(4):
                at = right_at + 112 + 16 * jj
                fold_f[at : at + 48, :] += outer_recv[
                    s, extra + 48 * jj : extra + 48 * jj + 48, :
                ].astype(f32)
            corner = outer_recv[s, extra + 192 : extra + 208, :].astype(f32)
            last = right_at + height - 1
            fold_f[last : last + 1, :] += corner[0:1]

        ghid[s, 0:16, C : 2 * C] += outer_recv[s, 2 * height : 2 * height + 16, :].astype(f32)
        ghid[s, 8 * height : 8 * height + 16, 0:C] += outer_recv[s, 2 * height + 16 : 2 * height + 32, :].astype(f32)

        def scale(k, carry):
            total = jnp.zeros((pixels, C), f32)
            half = lax.broadcasted_iota(jnp.int32, (8, C), 0)
            for t in range(16):
                if t % 8 == 0:
                    left = fold_f[pl.ds(left_at + 16 * k + t, 8), :]
                    right = fold_f[pl.ds(right_at + 16 * k + t, 8), :]
                at = t % 8
                pair, e = (1 + t) // 2, (1 + t) % 2
                value = ghid[s, pl.ds(128 * k + 16 * pair, 16), e * C : (e + 1) * C]
                low = value[:8] + jnp.where(half == 0, turned_by(left, -at), 0.0)
                high = value[8:] + jnp.where(half == 7, turned_by(right, 7 - at), 0.0)
                delta = jnp.concatenate([low, high], axis=0) * slope[s, 16 * k + t]
                d1[16 * k + t] = delta.astype(bf16)
                total = total + delta
            bias_acc[0] += total
            return carry

        lax.fori_loop(0, tiles, scale, 0)
        turn_pairs(s, d1[...])
        return carry

    middle = batch // 2
    most = batch - 1
    lax.fori_loop(0, most, stage_three, 0)
    sum_plane(1, 0)
    weight_sum(xs, (0, 1), (0, most))
    sum_plane(1, 1)
    lax.fori_loop(most, batch, stage_three, 0)
    sum_plane(1, 2)
    sum_copies(1, 0)
    weight_sum(xs, (0, 1), (most, batch))
    sum_start(0, 0)
    sum_copies(1, 1)
    weight_sum(xs, (2,), (0, batch))
    sum_start(0, 1)
    sum_copies(1, 2)
    weight_sum(xs, (3,), (0, middle))
    sum_plane(0, 0)
    weight_sum(xs, (3,), (middle, batch))
    sum_start(0, 2)

    for s in range(batch):
        dma_out(s).wait()

        @pl.when((j == 0) | (j == 3))
        def _():
            finish(all_rows, 544, send_sem.at[1, s])
            finish(all_rows, 496, osend_sem.at[s])

        @pl.when((j != 0) & (j != 3))
        def _():
            finish(all_rows, 416, send_sem.at[1, s])
            finish(all_rows, 480, osend_sem.at[s])

    for p in range(3):
        sum_end(1, p)
    sum_plane(0, 1)
    sum_copies(0, 0)
    sum_plane(0, 2)
    sum_copies(0, 1)
    sum_end(0, 0)
    sum_copies(0, 2)
    sum_end(0, 1)
    sum_end(0, 2)
    for g in range(2):
        for p in range(3):
            finish(grad_recv.at[g, p], (peers - 1) * blocks[p], gsend_sem.at[g, p, 0])
            finish(plane_recv.at[g, p], 3 * blocks[p], gsend_sem.at[g, p, 1])
            finish(part_recv.at[g, p], (peers - 1) * share, gsend_sem.at[g, p, 2])


def hand_over(*refs):
    sources, targets, held, sems = refs[:5], refs[5:10], refs[10:15], refs[15]
    parts = 4
    views = []
    tiles = sources[0].shape[0] // parts
    for i in range(parts):
        views.append(tuple(r[0].at[pl.ds(i * tiles, tiles)] for r in (sources, held, targets)))
    for i in range(1, 5):
        views.append((sources[i], held[i], targets[i]))
    arriving = [
        pltpu.make_async_copy(source, middle, sems.at[0, i])
        for i, (source, middle, _) in enumerate(views)
    ]
    leaving = [
        pltpu.make_async_copy(middle, target, sems.at[1, i])
        for i, (_, middle, target) in enumerate(views)
    ]
    for copy in arriving:
        copy.start()
    for first, second in zip(arriving, leaving):
        first.wait()
        second.start()
    for copy in leaving:
        copy.wait()


def strip_body(features, weight_one, bias_one, weight_two, bias_two, cotangent):
    tm_count = lax.axis_size("tm")
    tiles, batch, pixels, _, C = features.shape
    height = tiles * pixels
    bf16, f32 = jnp.bfloat16, jnp.float32
    peers = 4 * tm_count
    share = 3 * C // peers
    block = share + 16
    vmem = pl.BlockSpec(memory_space=pltpu.VMEM)
    hbm = pl.BlockSpec(memory_space=pl.ANY)
    dma = pltpu.SemaphoreType.DMA
    flops = 10 * tiles * batch * pixels * pixels * 9 * C * C
    output, gw1, gb1, gw2, gb2 = pl.pallas_call(
        functools.partial(strip_kernel, tm_count),
        in_specs=[hbm, hbm, vmem, vmem, vmem, vmem],
        out_specs=[hbm, vmem, vmem, vmem, vmem],
        out_shape=[
            jax.ShapeDtypeStruct(features.shape, bf16),
            jax.ShapeDtypeStruct((9 * C, C), f32), jax.ShapeDtypeStruct((1, C), f32),
            jax.ShapeDtypeStruct((9 * C, C), f32), jax.ShapeDtypeStruct((1, C), f32),
        ],
        scratch_shapes=[
            pltpu.VMEM(features.shape, bf16),
            pltpu.VMEM((batch, height + 2, 3, pixels, C), bf16),
            pltpu.VMEM((batch, height + 2, 3, pixels, C), bf16),
            pltpu.VMEM((1, height + 4, 3, pixels, C), bf16),
            pltpu.VMEM((height, pixels, C), bf16),
            pltpu.VMEM((batch + 1, 2 * C, 8 * height), bf16),
            pltpu.VMEM((batch, height, pixels, C), f32),
            pltpu.VMEM((batch, 8 * height + 16, 2 * C), f32),
            pltpu.VMEM((8 * height, 2 * C), f32),
            pltpu.VMEM((12 * C, 2 * C), bf16),
            pltpu.VMEM((12 * C, 2 * C), bf16),
            pltpu.VMEM((12 * C, 2 * C), bf16),
            pltpu.VMEM((2, 3 * C, C), bf16),
            pltpu.VMEM((2 * C, 12 * C), f32),
            pltpu.VMEM((2, pixels, C), f32),
            pltpu.VMEM((528, C), f32),
            pltpu.VMEM((464, C), f32),
            pltpu.VMEM((2, batch, 2, height + 16, C), bf16),
            pltpu.VMEM((2, batch, 2 * height + 96, C), bf16),
            pltpu.VMEM((batch, 2, height + 32, C), bf16),
            pltpu.VMEM((batch, 2, 48, C), bf16),
            pltpu.VMEM((batch, 2 * height + 240, C), bf16),
            pltpu.VMEM((2, 3, peers, block, C), bf16),
            pltpu.VMEM((2, 3, peers * block, C), bf16),
            pltpu.VMEM((2, 3, 4 * block, C), bf16),
            pltpu.VMEM((2, 3, block, C), bf16),
            pltpu.VMEM((2, 3, share, C), bf16),
            pltpu.VMEM((2, 3, 3 * C, C), bf16),
            dma((batch,)), dma((batch,)), dma((batch,)),
            dma((2, batch)), dma((2, batch)), dma((batch,)), dma((batch,)), dma((2, 3, 3)), dma((2, 3, 3)),
        ],
        compiler_params=pltpu.CompilerParams(
            collective_id=0, has_side_effects=True, vmem_limit_bytes=60 * 1024 * 1024
        ),
        cost_estimate=pl.CostEstimate(
            flops=flops, bytes_accessed=6 * features.size, transcendentals=4 * features.size
        ),
    )(
        features, cotangent, weight_one, bias_one.reshape(1, C), weight_two,
        bias_two.reshape(1, C),
    )
    results = [output, gw1, gb1, gw2, gb2]
    output, gw1, gb1, gw2, gb2 = pl.pallas_call(
        hand_over,
        in_specs=[hbm] * 5,
        out_specs=[hbm] * 5,
        out_shape=[jax.ShapeDtypeStruct(r.shape, r.dtype) for r in results],
        scratch_shapes=[pltpu.VMEM(r.shape, r.dtype) for r in results] + [dma((2, 8))],
        compiler_params=pltpu.CompilerParams(vmem_limit_bytes=60 * 1024 * 1024),
    )(*results)
    shape = weight_one.shape
    return (output, gw1.reshape(shape), gb1.reshape(C), gw2.reshape(shape), gb2.reshape(C))


def whole_columns(mesh, tiles):
    columns, samples = mesh.shape["tile"], mesh.shape["tm"]
    return columns == 4 * S and tiles == 3 * S * columns and samples in (1, 2)


def solution(mesh):
    def call(*arrays):
        if whole_columns(mesh, arrays[0].shape[0]):
            chosen = strip_body
        else:
            chosen = body
        return jax.shard_map(
            chosen,
            mesh=mesh,
            in_specs=(
                P("tile", "tm", None, None, None),
                P(),
                P(),
                P(),
                P(),
                P("tile", "tm", None, None, None),
            ),
            out_specs=(P("tile", "tm", None, None, None), P(), P(), P(), P()),
            check_vma=False,
        )(*arrays)

    return call
```

```python
import functools
import math

import jax
import jax.numpy as jnp
import numpy as np
from jax import lax
from jax.experimental import pallas as pl
from jax.experimental.pallas import tpu as pltpu
from jax.sharding import PartitionSpec as P

S = 4


inv_sqrt_two = 0.7071067811865476
inv_sqrt_tau = 0.3989422804014327
LOG2_E = 1.4426950408889634
MESH = pl.DeviceIdType.MESH


def passed_along(value, axis, steps):
    count = lax.axis_size(axis)
    pairs = [(source, (source + steps) % count) for source in range(count)]
    return lax.ppermute(value, axis, pairs)


def edge_partner(face_id, edge_id):
    group_id = face_id // 4
    within = face_id % 4
    after_id = (within + 1) % 4
    before = (within + 3) % 4
    if group_id == 0:
        options = [(after_id, 2), (4 + within, 0), (before, 0), (4 + after_id, 2)]
    elif group_id == 1:
        options = [(within, 1), (8 + before, 0), (before, 3), (8 + within, 2)]
    else:
        options = [(4 + after_id, 1), (8 + before, 3), (4 + within, 3), (8 + after_id, 1)]
    return options[edge_id]


def entry_pixel(edge_id, along_edge, length):
    if edge_id == 0:
        return (0, along_edge)
    if edge_id == 1:
        return (length - 1, along_edge)
    if edge_id == 2:
        return (along_edge, 0)
    return (along_edge, length - 1)


def step_pixel(face_id, row_at, col_at, row_step, col_step, length):
    row_new = row_at + row_step
    col_new = col_at + col_step
    if 0 <= row_new < length and 0 <= col_new < length:
        return (face_id, row_new, col_new, -1)
    if row_new < 0:
        edge_id = 0
    elif row_new >= length:
        edge_id = 1
    elif col_new < 0:
        edge_id = 2
    else:
        edge_id = 3
    along_edge = col_at if edge_id < 2 else row_at
    partner, entered = edge_partner(face_id, edge_id)
    row_in, col_in = entry_pixel(entered, along_edge, length)
    return (partner, row_in, col_in, entered)


def neighbour_pixel(face_id, row_at, col_at, row_step, col_step, length):
    if row_step == 0 or col_step == 0:
        found = step_pixel(face_id, row_at, col_at, row_step, col_step, length)
        return (found[0], found[1], found[2])
    face_one, row_one, col_one, entered = step_pixel(face_id, row_at, col_at, row_step, 0, length)
    if entered >= 2:
        found = step_pixel(face_one, row_one, col_one, col_step, 0, length)
    else:
        found = step_pixel(face_one, row_one, col_one, 0, col_step, length)
    return (found[0], found[1], found[2])


def tile_slot(face_id, tile_row, tile_col, side_tiles):
    group_id = face_id // 4
    within = face_id % 4
    extra = 1 if group_id == 2 else 0
    column = (side_tiles * (within + extra) + tile_col) % (4 * side_tiles)
    return 3 * side_tiles * column + side_tiles * group_id + tile_row


def cycle_position(row_at, col_at, pixels):
    if row_at == 0:
        return col_at
    if row_at == pixels - 1:
        return pixels + col_at
    if col_at == 0:
        return 2 * pixels + row_at
    return 3 * pixels + row_at


def halo_positions(pixels):
    places = [(-1, column) for column in range(-1, pixels + 1)]
    places = places + [(pixels, column) for column in range(-1, pixels + 1)]
    places = places + [(row_at, -1) for row_at in range(pixels)]
    places = places + [(row_at, pixels) for row_at in range(pixels)]
    return places


def halo_sources(side_tiles, pixels):
    slot_count = 12 * side_tiles * side_tiles
    places = halo_positions(pixels)
    length = side_tiles * pixels
    source_slot = np.zeros((slot_count, len(places)), np.int64)
    source_cycle = np.zeros((slot_count, len(places)), np.int64)
    for face_id in range(12):
        for tile_row in range(side_tiles):
            for tile_col in range(side_tiles):
                slot_id = tile_slot(face_id, tile_row, tile_col, side_tiles)
                for cell_index in range(len(places)):
                    row_at, col_at = places[cell_index]
                    inner_row = min(max(row_at, 0), pixels - 1)
                    inner_col = min(max(col_at, 0), pixels - 1)
                    partner, row_new, col_new = neighbour_pixel(
                        face_id,
                        tile_row * pixels + inner_row,
                        tile_col * pixels + inner_col,
                        row_at - inner_row,
                        col_at - inner_col,
                        length,
                    )
                    source_slot[slot_id, cell_index] = tile_slot(
                        partner, row_new // pixels, col_new // pixels, side_tiles
                    )
                    source_cycle[slot_id, cell_index] = cycle_position(
                        row_new % pixels, col_new % pixels, pixels
                    )
    return (source_slot, source_cycle)


def halo_rows(row_at, col_at, pixels):
    if row_at == -1 or row_at == pixels:
        base = 0 if row_at == -1 else 3 * pixels
        return [
            base + pixels * shift + col_at + 1 - shift
            for shift in range(3)
            if 0 <= col_at + 1 - shift < pixels
        ]
    return [6 * pixels + row_at if col_at == -1 else 7 * pixels + row_at]


def outer_row(row_at, col_at, pixels):
    if col_at == -1:
        return 2 * pixels + row_at + 1
    if col_at == pixels:
        return 4 * pixels + row_at + 1
    return col_at if row_at == -1 else pixels + col_at


def device_tables(device_count, per_device, side_tiles, pixels):
    source_slot, source_cycle = halo_sources(side_tiles, pixels)
    places = halo_positions(pixels)
    rim_len, halo_len, outer_len = 4 * pixels, 8 * pixels, 6 * pixels
    sends = {}
    local = []
    for device in range(device_count):
        local.append([])
        for local_id in range(per_device):
            slot_id = device * per_device + local_id
            for cell in range(len(places)):
                row_at, col_at = places[cell]
                source = int(source_slot[slot_id, cell])
                moved_by = (device - source // per_device) % device_count
                if moved_by > device_count // 2:
                    moved_by -= device_count
                rim = source % per_device * rim_len + int(source_cycle[slot_id, cell])
                halo = [local_id * halo_len + h for h in halo_rows(row_at, col_at, pixels)]
                outer = local_id * outer_len + outer_row(row_at, col_at, pixels)
                record = (rim, halo, outer)
                if moved_by == 0:
                    local[device].append(record)
                else:
                    lists = sends.setdefault(moved_by, [[] for _ in range(device_count)])
                    lists[device].append(record)
    offsets = sorted(sends)
    widths = [-(-max(len(one) for one in sends[offset]) // 16) * 16 for offset in offsets]
    total = sum(widths)
    send = np.full((device_count, total), -1, np.int32)
    receive = np.full((device_count, per_device * halo_len), -1, np.int32)
    back = np.full((device_count, total), -1, np.int32)
    target = np.full((device_count, per_device * outer_len + total), -1, np.int32)
    for device in range(device_count):
        for rim, halo, outer in local[device]:
            receive[device, halo] = rim
            target[device, outer] = rim
        base = 0
        for offset, width in zip(offsets, widths):
            sender = (device - offset) % device_count
            for at, (rim, halo, outer) in enumerate(sends[offset][device]):
                send[sender, base + at] = rim
                receive[device, halo] = per_device * rim_len + base + at
                back[device, base + at] = outer
                target[sender, per_device * outer_len + base + at] = rim
            base += width
    return (offsets, widths, send, receive, back, target)


def one_hot(table_np, tile_index, width):
    row = jnp.asarray(table_np, dtype=jnp.int32)[tile_index]
    return (row[:, None] == lax.broadcasted_iota(jnp.int32, (row.shape[0], width), 1)).astype(
        jnp.bfloat16
    )


def exchanged(rows, offsets, widths, sign):
    pieces, base = [], 0
    for offset, width in zip(offsets, widths):
        pieces.append(passed_along(rows[base : base + width], "tile", sign * offset))
        base += width
    return pieces


def halo_of(rim, layout, tile_index):
    offsets, widths, send, receive = layout[:4]
    outgoing = jnp.dot(one_hot(send, tile_index, rim.shape[0]), rim)
    pool = jnp.concatenate([rim] + exchanged(outgoing, offsets, widths, 1), axis=0)
    return jnp.dot(one_hot(receive, tile_index, pool.shape[0]), pool)


def folded(outer, layout, tile_index, rim_rows):
    offsets, widths, _, _, back, target = layout
    outgoing = jnp.dot(one_hot(back, tile_index, outer.shape[0]), outer)
    pool = jnp.concatenate([outer] + exchanged(outgoing, offsets, widths, -1), axis=0)
    spread = one_hot(target, tile_index, rim_rows)
    return lax.dot_general(
        spread, pool, (((0,), (0,)), ((), ())), preferred_element_type=jnp.float32
    )


def gelu_parts(value):
    half = 0.5 * (1.0 + lax.erf(value * inv_sqrt_two))
    return value * half, half + value * jnp.exp(-0.5 * value * value) * inv_sqrt_tau


def columns_at(tile, halo, work, pixels):
    count = pixels * pixels
    wide = tile.astype(jnp.float32)
    halo_wide = halo[6 * pixels :].astype(jnp.float32)
    work[0, pl.ds(1, count - 1), :] = wide[: count - 1]
    work[0, pl.ds(0, pixels, stride=pixels), :] = halo_wide[:pixels]
    work[1, pl.ds(0, count - 1), :] = wide[1:]
    work[1, pl.ds(pixels - 1, pixels, stride=pixels), :] = halo_wide[pixels:]
    middles = [work[0].astype(jnp.bfloat16), tile, work[1].astype(jnp.bfloat16)]
    joined = jnp.concatenate(
        [
            jnp.concatenate(
                [
                    halo[pixels * b : pixels * (b + 1)],
                    middles[b],
                    halo[pixels * (3 + b) : pixels * (4 + b)],
                ],
                axis=0,
            )
            for b in range(3)
        ],
        axis=1,
    )
    return jnp.concatenate([joined[pixels * a : pixels * a + count] for a in range(3)], axis=1)


def first_kernel(x_ref, halo_ref, w_ref, bias_ref, hidden_ref, slope_ref, rim_ref, work):
    batch, pixels, channels = x_ref.shape[1], x_ref.shape[2], x_ref.shape[4]
    count = pixels * pixels
    for s in range(batch):
        lanes = slice(s * channels, (s + 1) * channels)
        tile = x_ref[0, s].reshape(count, channels)
        cols = columns_at(tile, halo_ref[0, :, lanes], work.at[pl.ds(2 * s, 2)], pixels)
        pre = jnp.dot(cols, w_ref[...], preferred_element_type=jnp.float32) + bias_ref[...]
        hidden, slope = gelu_parts(pre)
        slope_ref[0, s] = slope
        work[2 * batch + s] = hidden
        rounded = hidden.astype(jnp.bfloat16)
        hidden_ref[0, s] = rounded.reshape(pixels, pixels, channels)
        rim_ref[0, 0:pixels, lanes] = rounded[:pixels]
        rim_ref[0, pixels : 2 * pixels, lanes] = rounded[count - pixels :]
        for side in range(2):
            edge = work[2 * batch + s, pl.ds(side * (pixels - 1), pixels, stride=pixels), :]
            rim_ref[0, (2 + side) * pixels : (3 + side) * pixels, lanes] = edge.astype(jnp.bfloat16)


def second_kernel(
    x_ref, halo_ref, cot_ref, w_ref, flip_ref, side_ref, bias_ref,
    out_ref, inner_ref, outer_ref, grad_ref, sum_ref, work, cols_ref, delta_ref, edge_ref,
):
    batch, pixels, channels = x_ref.shape[1], x_ref.shape[2], x_ref.shape[4]
    count = pixels * pixels

    @pl.when(pl.program_id(0) == 0)
    def _():
        grad_ref[...] = jnp.zeros_like(grad_ref)
        sum_ref[...] = jnp.zeros_like(sum_ref)

    zero_row = jnp.zeros((1, channels), jnp.float32)
    zero_col = jnp.zeros((pixels, channels), jnp.float32)
    zeros = jnp.zeros((2 * pixels, 3 * channels), jnp.bfloat16)
    for s in range(batch):
        lanes = slice(s * channels, (s + 1) * channels)
        tile = x_ref[0, s].reshape(count, channels)
        here = work.at[pl.ds(2 * s, 2)]
        cols = columns_at(tile, halo_ref[0, :, lanes], here, pixels)
        cols_ref[s * count : (s + 1) * count, :] = cols
        pre = jnp.dot(cols, w_ref[...], preferred_element_type=jnp.float32) + bias_ref[...]
        value, slope = gelu_parts(pre)
        out_ref[0, s] = value.astype(jnp.bfloat16).reshape(pixels, pixels, channels)
        cot = cot_ref[0, s].reshape(count, channels).astype(jnp.float32)
        delta = (cot * slope).astype(jnp.bfloat16)
        delta_ref[s * count : (s + 1) * count, :] = delta
        wide = delta.astype(jnp.float32)
        sum_ref[...] += jnp.sum(wide, axis=0, keepdims=True)
        edge_ref[s] = jnp.zeros(edge_ref.shape[1:], jnp.float32)
        work[2 * batch + s] = wide
        for side in range(2):
            edge_ref[s, side, pl.ds(2, pixels), :] = work[
                2 * batch + s, pl.ds(side * (pixels - 1), pixels, stride=pixels), :
            ]
        here[0, pl.ds(0, count - 1), :] = wide[1:]
        here[0, pl.ds(pixels - 1, pixels, stride=pixels), :] = zero_col
        here[1, pl.ds(1, count - 1), :] = wide[: count - 1]
        here[1, pl.ds(0, pixels, stride=pixels), :] = zero_col
        joined = jnp.concatenate(
            [here[0].astype(jnp.bfloat16), delta, here[1].astype(jnp.bfloat16)], axis=1
        )
        joined = jnp.concatenate([zeros, joined, zeros], axis=0)
        tall = count + 2 * pixels
        spread = jnp.concatenate(
            [joined[pixels * (2 - a) : pixels * (2 - a) + tall] for a in range(3)], axis=1
        )
        grad = jnp.dot(spread, flip_ref[...], preferred_element_type=jnp.float32)
        inner_ref[0, s] = grad[pixels : pixels + count]
        outer_ref[0, 0:pixels, lanes] = grad[:pixels].astype(jnp.bfloat16)
        outer_ref[0, pixels : 2 * pixels, lanes] = grad[pixels + count :].astype(jnp.bfloat16)
        for side in range(2):
            lhs = jnp.concatenate(
                [edge_ref[s, side, pl.ds(2 - a, 2 * pixels), :] for a in range(3)], axis=1
            ).astype(jnp.bfloat16)
            part = jnp.dot(lhs, side_ref[side], preferred_element_type=jnp.float32)
            outer_ref[0, 2 * pixels * (1 + side) : 2 * pixels * (2 + side), lanes] = part.astype(
                jnp.bfloat16
            )
    grad_ref[...] += lax.dot_general(
        delta_ref[...], cols_ref[...], (((0,), (0,)), ((), ())), preferred_element_type=jnp.float32
    )


def third_kernel(
    x_ref, halo_ref, inner_ref, rim_ref, slope_ref, grad_ref, sum_ref, work, cols_ref, delta_ref
):
    batch, pixels, channels = x_ref.shape[1], x_ref.shape[2], x_ref.shape[4]
    count = pixels * pixels

    @pl.when(pl.program_id(0) == 0)
    def _():
        grad_ref[...] = jnp.zeros_like(grad_ref)
        sum_ref[...] = jnp.zeros_like(sum_ref)

    for s in range(batch):
        lanes = slice(s * channels, (s + 1) * channels)
        tile = x_ref[0, s].reshape(count, channels)
        cols_ref[s * count : (s + 1) * count, :] = columns_at(
            tile, halo_ref[0, :, lanes], work.at[pl.ds(2 * s, 2)], pixels
        )
        at = 2 * batch + s
        work[at] = inner_ref[0, s]
        work[at, pl.ds(0, pixels), :] += rim_ref[0, 0:pixels, lanes]
        work[at, pl.ds(count - pixels, pixels), :] += rim_ref[0, pixels : 2 * pixels, lanes]
        for side in range(2):
            place = pl.ds(side * (pixels - 1), pixels, stride=pixels)
            edge = rim_ref[0, (2 + side) * pixels : (3 + side) * pixels, lanes]
            work[at, place, :] = work[at, place, :] + edge
        delta = (work[at] * slope_ref[0, s]).astype(jnp.bfloat16)
        delta_ref[s * count : (s + 1) * count, :] = delta
        sum_ref[...] += jnp.sum(delta.astype(jnp.float32), axis=0, keepdims=True)
    grad_ref[...] += lax.dot_general(
        delta_ref[...], cols_ref[...], (((0,), (0,)), ((), ())), preferred_element_type=jnp.float32
    )


def per_tile(shape):
    return pl.BlockSpec((1,) + tuple(shape), lambda t: (t,) + (0,) * len(shape))


def whole(shape):
    return pl.BlockSpec(tuple(shape), lambda t: (0,) * len(shape))


params = dict(vmem_limit_bytes=48 * 1024 * 1024)


def body(features, weight_one, bias_one, weight_two, bias_two, cotangent):
    device_count = lax.axis_size("tile")
    samples_count = lax.axis_size("tm")
    tile_index = lax.axis_index("tile")
    per_device, batch, pixels, _, channels = features.shape
    count = pixels * pixels
    lane_count = batch * channels
    layout = device_tables(device_count, per_device, S, pixels)
    bf16, f32 = jnp.bfloat16, jnp.float32
    tile_shape = (batch, pixels, pixels, channels)
    flat_shape = (batch, count, channels)
    halo_shape = (8 * pixels, lane_count)
    rim_shape = (4 * pixels, lane_count)
    outer_shape = (6 * pixels, lane_count)
    mat_one = weight_one.reshape(9 * channels, channels)
    mat_two = weight_two.reshape(9 * channels, channels)
    turned = weight_two.transpose(0, 1, 3, 2)
    flip = turned.reshape(9 * channels, channels)
    sides = jnp.stack([turned[:, 0], turned[:, 2]]).reshape(2, 3 * channels, channels)

    def out(shape, dtype):
        return jax.ShapeDtypeStruct((per_device,) + tuple(shape), dtype)

    work = pltpu.VMEM((3 * batch, count, channels), f32)
    cols = pltpu.VMEM((batch * count, 9 * channels), bf16)
    deltas = pltpu.VMEM((batch * count, channels), bf16)
    grad_shape = (channels, 9 * channels)

    rim_one = jnp.concatenate(
        [features[:, :, 0], features[:, :, -1], features[:, :, :, 0], features[:, :, :, -1]], axis=2
    )
    rim_one = rim_one.transpose(0, 2, 1, 3).reshape(per_device * 4 * pixels, lane_count)
    halo_one = halo_of(rim_one, layout, tile_index).reshape((per_device,) + halo_shape)
    hidden, slope, rim_two = pl.pallas_call(
        first_kernel,
        grid=(per_device,),
        in_specs=[per_tile(tile_shape), per_tile(halo_shape), whole(mat_one.shape), whole((1, channels))],
        out_specs=[per_tile(tile_shape), per_tile(flat_shape), per_tile(rim_shape)],
        out_shape=[out(tile_shape, bf16), out(flat_shape, f32), out(rim_shape, bf16)],
        scratch_shapes=[work],
        compiler_params=pltpu.CompilerParams(**params),
    )(features, halo_one, mat_one, bias_one.reshape(1, channels))
    halo_two = halo_of(rim_two.reshape(-1, lane_count), layout, tile_index)
    output, inner, outer, grad_two, sum_two = pl.pallas_call(
        second_kernel,
        grid=(per_device,),
        in_specs=[
            per_tile(tile_shape), per_tile(halo_shape), per_tile(tile_shape), whole(mat_two.shape),
            whole(flip.shape), whole(sides.shape), whole((1, channels)),
        ],
        out_specs=[
            per_tile(tile_shape), per_tile(flat_shape), per_tile(outer_shape),
            whole(grad_shape), whole((1, channels)),
        ],
        out_shape=[
            out(tile_shape, bf16), out(flat_shape, f32), out(outer_shape, bf16),
            jax.ShapeDtypeStruct(grad_shape, f32), jax.ShapeDtypeStruct((1, channels), f32),
        ],
        scratch_shapes=[work, cols, deltas, pltpu.VMEM((batch, 2, 2 * pixels + 8, channels), f32)],
        compiler_params=pltpu.CompilerParams(**params),
    )(
        hidden, halo_two.reshape((per_device,) + halo_shape), cotangent, mat_two, flip, sides,
        bias_two.reshape(1, channels),
    )
    rim_grad = folded(outer.reshape(-1, lane_count), layout, tile_index, per_device * 4 * pixels)
    grad_one, sum_one = pl.pallas_call(
        third_kernel,
        grid=(per_device,),
        in_specs=[
            per_tile(tile_shape), per_tile(halo_shape), per_tile(flat_shape), per_tile(rim_shape),
            per_tile(flat_shape),
        ],
        out_specs=[whole(grad_shape), whole((1, channels))],
        out_shape=[jax.ShapeDtypeStruct(grad_shape, f32), jax.ShapeDtypeStruct((1, channels), f32)],
        scratch_shapes=[work, cols, deltas],
        compiler_params=pltpu.CompilerParams(**params),
    )(features, halo_one, inner, rim_grad.reshape((per_device,) + rim_shape), slope)

    total_pixels = 12 * S * S * count * batch * samples_count
    grad_scale = 1.0 / math.sqrt(total_pixels)
    devices = device_count * samples_count
    axes = ("tile", "tm")

    def summed(grad, bias):
        rows = jnp.concatenate([grad.reshape(-1, channels), bias], axis=0)
        used = rows.shape[0]
        chunk = -(-used // (8 * devices)) * 8
        rows = jnp.pad(rows, ((0, chunk * devices - used), (0, 0)))
        parts = lax.all_to_all(rows.reshape(devices, chunk, channels), axes, 0, 0)
        mine = (jnp.sum(parts, axis=0) * grad_scale).astype(bf16)
        copies = jnp.broadcast_to(mine[None], (devices, chunk, channels))
        total = lax.all_to_all(copies, axes, 0, 0).reshape(devices * chunk, channels).astype(f32)
        weight = total[: used - 1].reshape(channels, 3, 3, channels).transpose(1, 2, 3, 0)
        return weight, total[used - 1]

    grad_weight_two, grad_bias_two = summed(grad_two, sum_two)
    grad_weight_one, grad_bias_one = summed(grad_one, sum_one)
    return (output, grad_weight_one, grad_bias_one, grad_weight_two, grad_bias_two)


def cdf_parts(value):
    bell = jnp.exp2(value * value * (-0.5 * LOG2_E))
    t = 1.0 / (1.0 + (0.3275911 * inv_sqrt_two) * jnp.abs(value))
    poly = 0.5 * 1.061405429
    for coefficient in (-1.453152027, 1.421413741, -0.284496736, 0.254829592):
        poly = poly * t + 0.5 * coefficient
    tail = poly * t * bell
    return jnp.where(value < 0.0, tail, 1.0 - tail), bell


def put_shifted(ref, sample, at, row, first, last, from_left, from_right):
    low, high = row[:8], row[8:]
    low_down, high_down = turned_by(low, 1), turned_by(high, 1)
    shifted = jnp.concatenate(
        [jnp.where(first, from_left, low_down), jnp.where(first, low_down, high_down)], axis=0
    )
    ref[sample, at, 0] = shifted.astype(jnp.bfloat16)
    low_up, high_up = turned_by(low, 7), turned_by(high, 7)
    shifted = jnp.concatenate(
        [jnp.where(last, high_up, low_up), jnp.where(last, from_right, high_up)], axis=0
    )
    ref[sample, at, 2] = shifted.astype(jnp.bfloat16)


def turned_by(value, steps):
    steps = steps % 8
    return value if steps == 0 else pltpu.roll(value, steps, 0)


class Edges:
    def __init__(self, half):
        self.half, self.lefts, self.rights = half, [], []

    def add(self, t, row):
        if t % 8 == 0:
            self.lefts.append(row[:8])
            self.rights.append(turned_by(row[8:], 1))
        else:
            here = self.half == t % 8
            self.lefts[-1] = jnp.where(here, turned_by(row[:8], t), self.lefts[-1])
            self.rights[-1] = jnp.where(here, turned_by(row[8:], t + 1), self.rights[-1])

    def columns(self):
        return jnp.concatenate(self.lefts, axis=0), jnp.concatenate(self.rights, axis=0)


def pair_window(ref, sample, start, pairs):
    lanes = ref.shape[4]
    v = ref[sample, pl.ds(start, 2 * pairs + 2)].reshape(pairs + 1, 2, 3, 16, lanes)
    parts = [v[:pairs, 0], v[:pairs, 1], v[1:, 0], v[1:, 1]]
    return jnp.concatenate(
        [p[:, b].reshape(pairs * 16, lanes) for p in parts for b in range(3)], axis=1
    )


def strip_kernel(
    tm_count,
    x_hbm, cot_hbm, w1_ref, b1_ref, w2_ref, b2_ref,
    out_hbm, gw1_ref, gb1_ref, gw2_ref, gb2_ref,
    field, xs, hs, ds, d1, turned, slope, ghid, pre_f, w1p, w2p, wback, wside, acc, bias_acc,
    edge_f, fold_f, edge_send, halo_recv, outer_send, corner_send, outer_recv,
    grad_send, grad_recv, plane_recv, plane_send, part_send, part_recv,
    in_sem, cot_sem, out_sem, send_sem, recv_sem, osend_sem, orecv_sem, gsend_sem, grecv_sem,
):
    f32, bf16 = jnp.float32, jnp.bfloat16
    tiles, batch, pixels, _, C = x_hbm.shape
    height = tiles * pixels
    columns = 16
    me = lax.axis_index("tile")
    other = lax.axis_index("tm")
    n, j = me // 4, me % 4
    peers = 4 * tm_count
    plane = j * tm_count + other

    def wrap(c):
        return (c + 2 * columns) % columns

    def dma_in(s):
        return pltpu.make_async_copy(x_hbm.at[:, s], field.at[:, s], in_sem.at[s])

    def dma_cot(s):
        return pltpu.make_async_copy(cot_hbm.at[:, s], field.at[:, s], cot_sem.at[s])

    def dma_out(s):
        return pltpu.make_async_copy(field.at[:, s], out_hbm.at[:, s], out_sem.at[s])

    def remote(src, dst, send, recv, device, side=None):
        pltpu.make_async_remote_copy(
            src_ref=src, dst_ref=dst, send_sem=send, recv_sem=recv,
            device_id=(device, other if side is None else side), device_id_type=MESH,
        ).start()

    def finish(ref, count, sem):
        view = ref.at[pl.ds(0, count)]
        pltpu.make_async_copy(view, view, sem).wait()

    for s in range(batch):
        dma_in(s).start()

    barrier = pltpu.get_barrier_semaphore()
    for offset in range(1, columns):
        pl.semaphore_signal(
            barrier, inc=1, device_id=(wrap(me + offset), other), device_id_type=MESH
        )
    for step in range(1, tm_count):
        for jj in range(4):
            pl.semaphore_signal(
                barrier, inc=1, device_id=(4 * n + jj, (other + step) % tm_count),
                device_id_type=MESH,
            )
    pl.semaphore_wait(barrier, columns - 1 + 4 * (tm_count - 1))

    def send_rim(f, s, field_ref, top, bottom):
        es, er = edge_send.at[f, s, 0], edge_send.at[f, s, 1]
        ss, rs = send_sem.at[f, s], recv_sem.at[f, s]
        land = halo_recv.at[f, s]

        def cut(ref, start, count):
            return ref.at[pl.ds(start, count)]

        @pl.when(j >= 1)
        def _():
            remote(cut(es, 16, height), cut(land, height, height), ss, rs, wrap(me - 1))

        @pl.when(j == 0)
        def _():
            remote(cut(es, 80, height - 64), cut(land, height, height - 64), ss, rs, wrap(me - 1))

        @pl.when(j <= 2)
        def _():
            remote(cut(er, 0, height), cut(land, 0, height), ss, rs, wrap(me + 1))

        @pl.when(j == 3)
        def _():
            remote(cut(er, 0, height - 64), cut(land, 64, height - 64), ss, rs, wrap(me + 1))

        remote(top, cut(land, 16 * j, 16), ss, rs, wrap(4 * n + 4))
        remote(bottom, cut(land, height + 128 + 16 * j, 16), ss, rs, wrap(4 * n - 1))
        upper, lower = 2 * height, 2 * height + 48

        @pl.when(j == 0)
        def _():
            remote(cut(es, 16, 32), cut(land, upper + 16, 32), ss, rs, wrap(me - 4))
            for jj in range(1, 4):
                remote(cut(es, 16 * jj, 48), cut(land, upper, 48), ss, rs, wrap(me - 4 + jj))
            remote(cut(es, 0, 16), cut(land, upper, 16), ss, rs, wrap(me + 8))

        @pl.when(j == 3)
        def _():
            for jj in range(3):
                remote(
                    cut(er, 112 + 16 * jj, 48), cut(land, lower, 48), ss, rs, wrap(me + 1 + jj)
                )
            remote(cut(er, height - 32, 32), cut(land, lower, 32), ss, rs, wrap(me + 4))
            remote(cut(er, height, 16), cut(land, lower + 32, 16), ss, rs, wrap(me + 8))

    half_iota = lax.broadcasted_iota(jnp.int32, (8, C), 0)
    first_pixel, last_pixel = half_iota == 0, half_iota == 7

    def put_edges(f, s, k, edges):
        left, right = edges.columns()
        edge_send[f, s, 0, pl.ds(16 + 16 * k, 16), :] = left.astype(bf16)
        edge_send[f, s, 1, pl.ds(16 * k, 16), :] = right.astype(bf16)

    def put_corners(f, s):
        row = edge_send[f, s, 0, 16:32, :].astype(f32)
        edge_send[f, s, 0, 0:16, :] = jnp.broadcast_to(row[0:1], (16, C)).astype(bf16)
        row = edge_send[f, s, 1, height - 16 : height, :].astype(f32)
        edge_send[f, s, 1, height : height + 16, :] = jnp.broadcast_to(row[15:16], (16, C)).astype(
            bf16
        )

    def put_halo_rows(f, s, ref):
        for side in range(2):
            edge_f[0:48, :] = halo_recv[f, s, pl.ds(2 * height + 48 * side, 48), :].astype(f32)
            for b in range(3):
                ref[s, side * (height + 1), b] = edge_f[
                    15 + b : 31 + b, :
                ].astype(bf16)

    def shift_tile(f, s, k, ref, row_of):
        left = halo_recv[f, s, pl.ds(16 * k, 16), :].astype(f32)
        right = halo_recv[f, s, pl.ds(height + 16 * k, 16), :].astype(f32)
        for t in range(16):
            group = 8 * (t // 8)
            put_shifted(
                ref, s, 1 + 16 * k + t, row_of(t), first_pixel, last_pixel,
                turned_by(left[group : group + 8], -t), turned_by(right[group : group + 8], 7 - t),
            )

    def features_out(s, carry):
        dma_in(s).wait()

        def step(k, carry):
            edges = Edges(half_iota)
            for t in range(16):
                edges.add(t, field[k, s, t].astype(f32))
            put_edges(0, s, k, edges)
            return carry

        lax.fori_loop(0, tiles, step, 0)
        put_corners(0, s)
        send_rim(0, s, field, field.at[0, s, 0], field.at[tiles - 1, s, pixels - 1])
        return carry

    lax.fori_loop(0, batch, features_out, 0)

    one, two = w1_ref[...].reshape(9 * C, C), w2_ref[...].reshape(9 * C, C)
    zeros = jnp.zeros((3 * C, C), bf16)
    for packed, flat in ((w1p, one), (w2p, two)):
        packed[0 : 9 * C, 0:C] = flat
        packed[9 * C : 12 * C, 0:C] = zeros
        packed[0 : 3 * C, C : 2 * C] = zeros
        packed[3 * C : 12 * C, C : 2 * C] = flat
    for e in range(2):
        gap = 3 * (1 - e)
        wback[(9 if e == 0 else 0) * C + 0 : (12 if e == 0 else 3) * C, e * C : (e + 1) * C] = zeros
    for a in range(3):
        for b in range(3):
            block = w2_ref[a, b].T
            for e in range(2):
                at = ((2 + e - a) * 3 + 2 - b) * C
                wback[at : at + C, e * C : (e + 1) * C] = block
            if b != 1:
                wside[b // 2, a * C : (a + 1) * C, :] = block

    bias_one = jnp.concatenate([b1_ref[...], b1_ref[...]], axis=1)
    bias_two = jnp.concatenate([b2_ref[...], b2_ref[...]], axis=1)
    bias_acc[...] = jnp.zeros_like(bias_acc)

    def build_one(s, k):
        for t in range(16):
            xs[s, 1 + 16 * k + t, 1] = field[k, s, t]
        shift_tile(0, s, k, xs, lambda t: field[k, s, t].astype(f32))

    def build_two(s, k):
        shift_tile(1, s, k, hs, lambda t: hs[s, 1 + 16 * k + t, 1].astype(f32))

    def first_copies(f, ref, build):
        finish(halo_recv.at[f, 0], 2 * height + 96, recv_sem.at[f, 0])
        put_halo_rows(f, 0, ref)

        def step(k, carry):
            build(0, k)
            return carry

        lax.fori_loop(0, tiles, step, 0)

    def stage_one(s, carry):
        @pl.when(s + 1 < batch)
        def _():
            finish(halo_recv.at[0, s + 1], 2 * height + 96, recv_sem.at[0, s + 1])

        following = s + 1 - (s + 1) // batch

        def dot(c):
            pre_f[rows_of * c : rows_of * (c + 1), :] = jnp.dot(
                pair_window(xs, s, 2 * per_chunk * c, per_chunk), w1p[...],
                preferred_element_type=f32,
            )

        def after(k):
            edges = Edges(half_iota)
            for q in range(8):
                at = 128 * k + 16 * q
                pre = pre_f[at : at + 16, :] + bias_one
                half, bell = cdf_parts(pre)
                hidden = pre * half
                slopes = half + pre * (bell * inv_sqrt_tau)
                for e in range(2):
                    t = 2 * q + e
                    row = hidden[:, e * C : (e + 1) * C]
                    hs[s, 1 + 16 * k + t, 1] = row.astype(bf16)
                    slope[s, 16 * k + t] = slopes[:, e * C : (e + 1) * C]
                    edges.add(t, row)
            put_edges(1, s, k, edges)

        dot(0)
        put_halo_rows(0, following, xs)
        for k in range(tiles // 2):
            build_one(following, k)
        dot(1)
        for k in range(tiles // 2, tiles):
            build_one(following, k)
            if k % 2:
                after((k - tiles // 2) // 2)
        after(3)
        dot(2)
        for k in range(4, tiles):
            after(k)
        put_corners(1, s)
        top = hs.at[s, 1, 1]
        bottom = hs.at[s, height, 1]
        send_rim(1, s, hs, top, bottom)
        @pl.when((j == 0) | (j == 3))
        def _():
            finish(all_rows, 544, send_sem.at[0, s])

        @pl.when((j != 0) & (j != 3))
        def _():
            finish(all_rows, 416, send_sem.at[0, s])

        dma_cot(s).start()
        return carry

    all_rows = outer_recv.at[0]
    chunks = 3
    per_chunk = pairs_of = height // 2 // chunks
    rows_of = 16 * per_chunk

    first_copies(0, xs, build_one)
    lax.fori_loop(0, batch, stage_one, 0)

    for at in (0, 1, height + 2, height + 3):
        ds[0, at] = jnp.zeros((3, pixels, C), bf16)
    for side in range(2):
        edge_f[48 + 240 * side : 48 + 240 * side + 24, :] = jnp.zeros((24, C), f32)
        edge_f[48 + 240 * side + 24 + height : 288 + 240 * side, :] = jnp.zeros(
            (216 - height, C), f32
        )

    def send_outer(s):
        ss, rs = osend_sem.at[s], orecv_sem.at[s]
        ol, orr = outer_send.at[s, 0], outer_send.at[s, 1]
        tb, bb = corner_send.at[s, 0], corner_send.at[s, 1]
        land = outer_recv.at[s]
        g_top, g_bottom, extra = 2 * height, 2 * height + 16, 2 * height + 32

        def cut(ref, start, count):
            return ref.at[pl.ds(start, count)]

        @pl.when(j >= 1)
        def _():
            remote(cut(ol, 16, height), cut(land, height, height), ss, rs, wrap(me - 1))

        @pl.when(j <= 2)
        def _():
            remote(cut(orr, 16, height), cut(land, 0, height), ss, rs, wrap(me + 1))

        @pl.when(j == 0)
        def _():
            remote(cut(ol, 80, height - 64), cut(land, height, height - 64), ss, rs, wrap(me - 1))
            for i in range(4):
                remote(cut(ol, 16 + 16 * i, 16), cut(land, g_top, 16), ss, rs, wrap(me - 4 + i))
            remote(cut(tb, 0, 16), cut(land, extra + 192, 16), ss, rs, wrap(me + 8))

        @pl.when(j == 3)
        def _():
            remote(cut(orr, 16, height - 64), cut(land, 64, height - 64), ss, rs, wrap(me + 1))
            for i in range(4):
                remote(
                    cut(orr, 144 + 16 * i, 16), cut(land, g_bottom, 16), ss, rs, wrap(me + 1 + i)
                )
            remote(cut(bb, 32, 16), cut(land, extra + 192, 16), ss, rs, wrap(me + 8))

        remote(tb, cut(land, extra + 48 * j, 48), ss, rs, wrap(4 * n + 4))
        remote(bb, cut(land, extra + 48 * j, 48), ss, rs, wrap(4 * n - 1))

    def stage_two(s, carry):
        @pl.when(s + 1 < batch)
        def _():
            finish(halo_recv.at[1, s + 1], 2 * height + 96, recv_sem.at[1, s + 1])

        following = s + 1 - (s + 1) // batch
        earlier = s - (s + batch - 1) // batch
        dma_cot(s).wait()

        def dot(c):
            pre_f[rows_of * c : rows_of * (c + 1), :] = jnp.dot(
                pair_window(hs, s, 2 * per_chunk * c, per_chunk), w2p[...],
                preferred_element_type=f32,
            )

        zero = jnp.zeros((8, C), f32)

        def after(k):
            edges = Edges(half_iota)
            total = jnp.zeros((pixels, C), f32)
            for q in range(8):
                at = 128 * k + 16 * q
                pre = pre_f[at : at + 16, :] + bias_two
                half, bell = cdf_parts(pre)
                outs = pre * half
                slopes = half + pre * (bell * inv_sqrt_tau)
                for e in range(2):
                    t = 2 * q + e
                    delta = field[k, s, t].astype(f32) * slopes[:, e * C : (e + 1) * C]
                    field[k, s, t] = outs[:, e * C : (e + 1) * C].astype(bf16)
                    row = 2 + 16 * k + t
                    ds[0, row, 1] = delta.astype(bf16)
                    total = total + delta
                    put_shifted(ds, 0, row, delta, first_pixel, last_pixel, zero, zero)
                    edges.add(t, delta)
            left, right = edges.columns()
            edge_f[72 + 16 * k : 88 + 16 * k, :] = left
            edge_f[312 + 16 * k : 328 + 16 * k, :] = right
            bias_acc[1] += total

        def back(c):
            first, last = (pairs_of * c, pairs_of * (c + 1) + c // (chunks - 1))
            ghid[s, 16 * first : 16 * last] = jnp.dot(
                pair_window(ds, 0, 2 * first, last - first), wback[...],
                preferred_element_type=f32,
            )

        dot(0)
        dot(1)
        for k in range(tiles):
            after(k)
            if k == 3:
                dot(2)
            if k in (1, 5, 9):
                window_sum(hs, earlier, s, ((1, 5, 9).index(k),))
            if k in (6, 10):
                back((k - 6) // 4)
        window_sum(hs, earlier, s, (3,))
        put_halo_rows(1, following, hs)
        for k in range(tiles // 2):
            build_two(following, k)
        back(2)
        for k in range(tiles // 2, tiles):
            build_two(following, k)
        dma_out(s).start()

        fold_f[0:96, :] = jnp.zeros((96, C), f32)
        for side in range(2):
            base = 48 + 240 * side
            lhs = jnp.concatenate(
                [edge_f[base + 9 - a : base + 233 - a, :] for a in range(3)], axis=1
            ).astype(bf16)
            cells = jnp.dot(lhs, wside[side], preferred_element_type=f32)
            outer_send[s, side] = cells.astype(bf16)
            fold_f[15 + 17 * side : 16 + 17 * side, :] = cells[15:16]
            fold_f[63 + 17 * side : 64 + 17 * side, :] = cells[16 + height : 17 + height]

        fold_f[16:32, :] = ghid[s, 0:16, 0:C]
        fold_f[64:80, :] = ghid[s, 8 * height : 8 * height + 16, C : 2 * C]
        corner_send[s, 0] = fold_f[0:48, :].astype(bf16)
        corner_send[s, 1] = fold_f[48:96, :].astype(bf16)
        send_outer(s)

        turn_pairs(s, ds[0, 2 : 2 + height, 1])
        return carry

    def turn_pairs(s, value):
        v = value.reshape(height // 2, 2, pixels, C)
        turned[s + 1] = jnp.concatenate(
            [v[:, e].reshape(8 * height, C) for e in range(2)], axis=1
        ).T

    def window_sum(ref, s, slot, window):
        pairs = height // 2
        lanes = slice(window[0] * 3 * C, (window[-1] + 1) * 3 * C)
        v = ref[s].reshape(pairs + 1, 2, 3, pixels, C)
        parts = []
        for w in window:
            x = v[:pairs, w] if w < 2 else v[1:, w - 2]
            parts += [x[:, b].reshape(pairs * pixels, C) for b in range(3)]
        acc[:, lanes] += jnp.dot(
            turned[slot], jnp.concatenate(parts, axis=1), preferred_element_type=f32
        )

    def weight_sum(ref, window, samples):
        lanes = slice(window[0] * 3 * C, (window[-1] + 1) * 3 * C)
        if samples[0] == 0:
            acc[:, lanes] = jnp.zeros((2 * C, 3 * C * len(window)), f32)

        def step(s, carry):
            window_sum(ref, s, s + 1, window)
            return carry

        lax.fori_loop(samples[0], samples[1], step, 0)

    acc[...] = jnp.zeros_like(acc)
    turned[0] = jnp.zeros(turned.shape[1:], bf16)
    first_copies(1, hs, build_two)
    lax.fori_loop(0, batch, stage_two, 0)

    share = 3 * C // peers
    blocks = (share + 16, share, share)

    def sum_start(g, p):
        block = blocks[p]
        for b in range(3):
            at = (3 * p + b) * C
            value = acc[0:C, at : at + C] + acc[C : 2 * C, at + 3 * C : at + 4 * C]
            value = value.astype(bf16).T
            for u in range(C // 16):
                row = b * C + 16 * u
                grad_send[g, p, row // share, row % share : row % share + 16, :] = value[
                    16 * u : 16 * u + 16
                ]
        if p == 0:
            bias = jnp.broadcast_to(
                jnp.sum(bias_acc[g], axis=0, keepdims=True), (16, C)
            ).astype(bf16)
            for d in range(peers):
                grad_send[g, p, d, share:block, :] = bias
        for step in range(1, peers):
            to = (plane + step) % peers
            remote(
                grad_send.at[g, p, to, pl.ds(0, block)],
                grad_recv.at[g, p, pl.ds(plane * block, block)],
                gsend_sem.at[g, p, 0], grecv_sem.at[g, p, 0],
                4 * n + to // tm_count, to % tm_count,
            )
        grad_recv[g, p, pl.ds(plane * block, block), :] = grad_send[g, p, plane, 0:block, :]

    def sum_plane(g, p):
        block = blocks[p]
        finish(grad_recv.at[g, p], (peers - 1) * block, grecv_sem.at[g, p, 0])
        total = grad_recv[g, p, 0:block, :].astype(f32)
        for d in range(1, peers):
            total = total + grad_recv[g, p, d * block : (d + 1) * block, :].astype(f32)
        plane_send[g, p, 0:block, :] = total.astype(bf16)
        for step in range(1, 4):
            remote(
                plane_send.at[g, p, pl.ds(0, block)],
                plane_recv.at[g, p, pl.ds(n * block, block)],
                gsend_sem.at[g, p, 1], grecv_sem.at[g, p, 1], wrap(me + 4 * step),
            )
        plane_recv[g, p, pl.ds(n * block, block), :] = total.astype(bf16)

    def sum_copies(g, p):
        block = blocks[p]
        finish(plane_recv.at[g, p], 3 * block, grecv_sem.at[g, p, 1])
        total = plane_recv[g, p, 0:block, :].astype(f32)
        for d in range(1, 4):
            total = total + plane_recv[g, p, d * block : (d + 1) * block, :].astype(f32)
        pixel_count = 16 * height * pixels * batch * tm_count
        total = total * (1.0 / math.sqrt(pixel_count))
        if p == 0:
            (gb1_ref, gb2_ref)[g][...] = total[share : share + 1]
        mine = total[0:share].astype(bf16)
        part_send[g, p] = mine
        for step in range(1, peers):
            to = (plane + step) % peers
            remote(
                part_send.at[g, p], part_recv.at[g, p, pl.ds(plane * share, share)],
                gsend_sem.at[g, p, 2], grecv_sem.at[g, p, 2],
                4 * n + to // tm_count, to % tm_count,
            )
        part_recv[g, p, pl.ds(plane * share, share), :] = mine

    def sum_end(g, p):
        finish(part_recv.at[g, p], (peers - 1) * share, grecv_sem.at[g, p, 2])
        (gw1_ref, gw2_ref)[g][3 * C * p : 3 * C * (p + 1), :] = part_recv[g, p].astype(f32)

    weight_sum(hs, (0, 1), (batch - 1, batch))
    sum_start(1, 0)
    weight_sum(hs, (2,), (batch - 1, batch))
    sum_start(1, 1)
    weight_sum(hs, (3,), (batch - 1, batch))
    sum_start(1, 2)

    def stage_three(s, carry):
        @pl.when((j == 0) | (j == 3))
        def _():
            finish(all_rows, 560, orecv_sem.at[s])

        @pl.when((j != 0) & (j != 3))
        def _():
            finish(all_rows, 416, orecv_sem.at[s])

        extra = 2 * height + 32
        left_at, right_at = 16, 240

        @pl.when(j != 0)
        def _():
            fold_f[left_at : left_at + height, :] = outer_recv[s, 0:height, :].astype(f32)

        @pl.when(j == 0)
        def _():
            fold_f[left_at - 16 : left_at + 64, :] = jnp.zeros((80, C), f32)
            fold_f[left_at + 64 : left_at + height, :] = outer_recv[s, 64:height, :].astype(f32)
            for jj in range(4):
                at = left_at - 16 + 16 * jj
                fold_f[at : at + 48, :] += outer_recv[
                    s, extra + 48 * jj : extra + 48 * jj + 48, :
                ].astype(f32)
            corner = outer_recv[s, extra + 192 : extra + 208, :].astype(f32)
            fold_f[left_at : left_at + 1, :] += corner[15:16]

        @pl.when(j != 3)
        def _():
            fold_f[right_at : right_at + height, :] = outer_recv[s, height : 2 * height, :].astype(
                f32
            )

        @pl.when(j == 3)
        def _():
            fold_f[right_at : right_at + height - 64, :] = outer_recv[
                s, height : 2 * height - 64, :
            ].astype(f32)
            fold_f[right_at + height - 64 : right_at + height + 16, :] = jnp.zeros((80, C), f32)
            for jj in range(4):
                at = right_at + 112 + 16 * jj
                fold_f[at : at + 48, :] += outer_recv[
                    s, extra + 48 * jj : extra + 48 * jj + 48, :
                ].astype(f32)
            corner = outer_recv[s, extra + 192 : extra + 208, :].astype(f32)
            last = right_at + height - 1
            fold_f[last : last + 1, :] += corner[0:1]

        ghid[s, 0:16, C : 2 * C] += outer_recv[s, 2 * height : 2 * height + 16, :].astype(f32)
        ghid[s, 8 * height : 8 * height + 16, 0:C] += outer_recv[s, 2 * height + 16 : 2 * height + 32, :].astype(f32)

        def scale(k):
            total = jnp.zeros((pixels, C), f32)
            half = lax.broadcasted_iota(jnp.int32, (8, C), 0)
            for t in range(16):
                if t % 8 == 0:
                    left = fold_f[pl.ds(left_at + 16 * k + t, 8), :]
                    right = fold_f[pl.ds(right_at + 16 * k + t, 8), :]
                at = t % 8
                pair, e = (1 + t) // 2, (1 + t) % 2
                value = ghid[s, pl.ds(128 * k + 16 * pair, 16), e * C : (e + 1) * C]
                low = value[:8] + jnp.where(half == 0, turned_by(left, -at), 0.0)
                high = value[8:] + jnp.where(half == 7, turned_by(right, 7 - at), 0.0)
                delta = jnp.concatenate([low, high], axis=0) * slope[s, 16 * k + t]
                d1[16 * k + t] = delta.astype(bf16)
                total = total + delta
            bias_acc[0] += total

        earlier = s - (s + batch - 1) // batch
        for k in range(tiles):
            scale(k)
            if k in (3, 7):
                window_sum(xs, earlier, s, (k // 4,))
        turn_pairs(s, d1[...])
        return carry

    middle = batch // 2
    most = batch - 1
    acc[:, 0 : 6 * C] = jnp.zeros((2 * C, 6 * C), f32)
    lax.fori_loop(0, batch, stage_three, 0)
    window_sum(xs, most, batch, (0, 1))
    sum_start(0, 0)
    for p in range(3):
        sum_plane(1, p)
    weight_sum(xs, (2,), (0, batch))
    sum_start(0, 1)
    weight_sum(xs, (3,), (0, middle))
    sum_plane(0, 0)
    for p in range(3):
        sum_copies(1, p)
    weight_sum(xs, (3,), (middle, batch))
    sum_start(0, 2)
    sum_plane(0, 1)
    sum_copies(0, 0)

    for p in range(3):
        sum_end(1, p)
    sum_plane(0, 2)
    sum_copies(0, 1)
    sum_end(0, 0)
    sum_copies(0, 2)
    sum_end(0, 1)
    sum_end(0, 2)
    for g in range(2):
        for p in range(3):
            finish(grad_recv.at[g, p], (peers - 1) * blocks[p], gsend_sem.at[g, p, 0])
            finish(plane_recv.at[g, p], 3 * blocks[p], gsend_sem.at[g, p, 1])
            finish(part_recv.at[g, p], (peers - 1) * share, gsend_sem.at[g, p, 2])
    for s in range(batch):
        dma_out(s).wait()

        @pl.when((j == 0) | (j == 3))
        def _():
            finish(all_rows, 544, send_sem.at[1, s])
            finish(all_rows, 496, osend_sem.at[s])

        @pl.when((j != 0) & (j != 3))
        def _():
            finish(all_rows, 416, send_sem.at[1, s])
            finish(all_rows, 480, osend_sem.at[s])


def hand_over(*refs):
    sources, targets, held, sems = refs[:5], refs[5:10], refs[10:15], refs[15]
    parts = 4
    views = []
    tiles = sources[0].shape[0] // parts
    for i in range(parts):
        views.append(tuple(r[0].at[pl.ds(i * tiles, tiles)] for r in (sources, held, targets)))
    for i in range(1, 5):
        views.append((sources[i], held[i], targets[i]))
    arriving = [
        pltpu.make_async_copy(source, middle, sems.at[0, i])
        for i, (source, middle, _) in enumerate(views)
    ]
    leaving = [
        pltpu.make_async_copy(middle, target, sems.at[1, i])
        for i, (_, middle, target) in enumerate(views)
    ]
    for copy in arriving:
        copy.start()
    for first, second in zip(arriving, leaving):
        first.wait()
        second.start()
    for copy in leaving:
        copy.wait()


def strip_body(features, weight_one, bias_one, weight_two, bias_two, cotangent):
    tm_count = lax.axis_size("tm")
    tiles, batch, pixels, _, C = features.shape
    height = tiles * pixels
    bf16, f32 = jnp.bfloat16, jnp.float32
    peers = 4 * tm_count
    share = 3 * C // peers
    block = share + 16
    vmem = pl.BlockSpec(memory_space=pltpu.VMEM)
    hbm = pl.BlockSpec(memory_space=pl.ANY)
    dma = pltpu.SemaphoreType.DMA
    flops = 10 * tiles * batch * pixels * pixels * 9 * C * C
    output, gw1, gb1, gw2, gb2 = pl.pallas_call(
        functools.partial(strip_kernel, tm_count),
        in_specs=[hbm, hbm, vmem, vmem, vmem, vmem],
        out_specs=[hbm, vmem, vmem, vmem, vmem],
        out_shape=[
            jax.ShapeDtypeStruct(features.shape, bf16),
            jax.ShapeDtypeStruct((9 * C, C), f32), jax.ShapeDtypeStruct((1, C), f32),
            jax.ShapeDtypeStruct((9 * C, C), f32), jax.ShapeDtypeStruct((1, C), f32),
        ],
        scratch_shapes=[
            pltpu.VMEM(features.shape, bf16),
            pltpu.VMEM((batch, height + 2, 3, pixels, C), bf16),
            pltpu.VMEM((batch, height + 2, 3, pixels, C), bf16),
            pltpu.VMEM((1, height + 4, 3, pixels, C), bf16),
            pltpu.VMEM((height, pixels, C), bf16),
            pltpu.VMEM((batch + 1, 2 * C, 8 * height), bf16),
            pltpu.VMEM((batch, height, pixels, C), f32),
            pltpu.VMEM((batch, 8 * height + 16, 2 * C), f32),
            pltpu.VMEM((8 * height, 2 * C), f32),
            pltpu.VMEM((12 * C, 2 * C), bf16),
            pltpu.VMEM((12 * C, 2 * C), bf16),
            pltpu.VMEM((12 * C, 2 * C), bf16),
            pltpu.VMEM((2, 3 * C, C), bf16),
            pltpu.VMEM((2 * C, 12 * C), f32),
            pltpu.VMEM((2, pixels, C), f32),
            pltpu.VMEM((528, C), f32),
            pltpu.VMEM((464, C), f32),
            pltpu.VMEM((2, batch, 2, height + 16, C), bf16),
            pltpu.VMEM((2, batch, 2 * height + 96, C), bf16),
            pltpu.VMEM((batch, 2, height + 32, C), bf16),
            pltpu.VMEM((batch, 2, 48, C), bf16),
            pltpu.VMEM((batch, 2 * height + 240, C), bf16),
            pltpu.VMEM((2, 3, peers, block, C), bf16),
            pltpu.VMEM((2, 3, peers * block, C), bf16),
            pltpu.VMEM((2, 3, 4 * block, C), bf16),
            pltpu.VMEM((2, 3, block, C), bf16),
            pltpu.VMEM((2, 3, share, C), bf16),
            pltpu.VMEM((2, 3, 3 * C, C), bf16),
            dma((batch,)), dma((batch,)), dma((batch,)),
            dma((2, batch)), dma((2, batch)), dma((batch,)), dma((batch,)), dma((2, 3, 3)), dma((2, 3, 3)),
        ],
        compiler_params=pltpu.CompilerParams(
            collective_id=0, has_side_effects=True, vmem_limit_bytes=60 * 1024 * 1024
        ),
        cost_estimate=pl.CostEstimate(
            flops=flops, bytes_accessed=6 * features.size, transcendentals=4 * features.size
        ),
    )(
        features, cotangent, weight_one, bias_one.reshape(1, C), weight_two,
        bias_two.reshape(1, C),
    )
    results = [output, gw1, gb1, gw2, gb2]
    output, gw1, gb1, gw2, gb2 = pl.pallas_call(
        hand_over,
        in_specs=[hbm] * 5,
        out_specs=[hbm] * 5,
        out_shape=[jax.ShapeDtypeStruct(r.shape, r.dtype) for r in results],
        scratch_shapes=[pltpu.VMEM(r.shape, r.dtype) for r in results] + [dma((2, 8))],
        compiler_params=pltpu.CompilerParams(vmem_limit_bytes=60 * 1024 * 1024),
    )(*results)
    shape = weight_one.shape
    return (output, gw1.reshape(shape), gb1.reshape(C), gw2.reshape(shape), gb2.reshape(C))


def whole_columns(mesh, tiles):
    columns, samples = mesh.shape["tile"], mesh.shape["tm"]
    return columns == 4 * S and tiles == 3 * S * columns and samples in (1, 2)


def solution(mesh):
    def call(*arrays):
        if whole_columns(mesh, arrays[0].shape[0]):
            chosen = strip_body
        else:
            chosen = body
        return jax.shard_map(
            chosen,
            mesh=mesh,
            in_specs=(
                P("tile", "tm", None, None, None),
                P(),
                P(),
                P(),
                P(),
                P("tile", "tm", None, None, None),
            ),
            out_specs=(P("tile", "tm", None, None, None), P(), P(), P(), P()),
            check_vma=False,
        )(*arrays)

    return call
```
